32 devices in a mesh: groups: 2 (over x), seq: 16 (over z, y, core).
Axes of the slice: x: 2, y: 2, z: 4, core: 2. Of those that a mesh axis runs over, the one named last changes fastest.
Arguments:
- activations: bfloat16 [4096, 8192], P(('groups', 'seq')), parts along dimension 0, may hold values from -6 to 6
- out_grads: bfloat16 [4096, 28672], P('groups', 'seq'), parts along dimension 0, may hold values from -6 to 6
- proj_in: bfloat16 [8192, 64], replicated, may hold values from -0.0625 to 0.0625
- proj_out: bfloat16 [28672, 64], P('seq'), may hold values from -0.03125 to 0.03125
- queries: bfloat16 [128, 4096], P('seq'), may hold values from -0.09375 to 0.09375
- doc_length: int32 [32], P('groups'), parts along dimension 0, may hold values from 1 to 1024, 2048 in all
- valid_count: int32 [32], P('groups'), parts along dimension 0, may hold values from 1 to 1024
Outputs:
- token_scores: float32 [4096, 128], P(('groups', 'seq')), parts along dimension 0
- doc_scores: float32 [32, 128], P('groups', 'seq'), parts along dimension 0
The draws below stay inside these ranges and needn't reach their ends.
There are 2 independent parts, one for each index of `groups`. The reference program is written for one: setup_inputs(seed, part) draws one part's arguments, and reference() takes and returns one part's arrays. A program takes and returns all parts, laid end to end along the dimension named above; an argument that names none is the same for every part. Nothing has to cross between parts.
Inputs may be any that keep to these rules, and one draw needn't show every extreme that they name: `doc_length`: the lengths sum to 2048; the longest is exactly 1024.
All inputs are finite; a program needn't handle non-finite values.
Results may differ from the reference program's by a relative error of at most 0.0029.
Values may be sent and summed in bfloat16 or wider, within the bound.
No kernel may reach another device: no remote copies, remote signals or barrier semaphores. Data moves between devices by JAX's collectives and lax.ppermute only.
A program may use at most 64 MiB of HBM per device.

```python
import math
import jax
import jax.numpy as jnp
import numpy as np
from jax import lax

D = 8192
FF = 28672
PROJ = 64
DOCS = 16
TOKENS = 2048
QUERIES = 128
FEAT = 4096
MOST = 1024


def set_ends(result, stream_key, low, top_value):
    dims = result.shape
    spot = [jax.random.randint(jax.random.fold_in(stream_key, axis), (), 0, dims[axis]) for axis in range(len(dims))]
    result = result.at[tuple(spot)].set(low)
    longest = dims.index(max(dims))
    spot[longest] = (spot[longest] + 1) % dims[longest]
    return result.at[tuple(spot)].set(top_value)


def with_spikes(drawn, rng, source, target, blocks, factor):
    owner, partner = [(jnp.arange(drawn.shape[position]) // (drawn.shape[position] // blocks)).reshape([-1 if axis == position else 1 for axis in range(drawn.ndim)]) for position in (source, target)]
    chosen = jax.random.permutation(rng, blocks)[partner]
    strong = (owner == chosen) | (owner == (partner + blocks // 2) % blocks)
    return jnp.where(strong, factor * drawn, drawn)


def shard_levels(rng, extent, pieces, low, high):
    gain, own = 1.0, jax.random.fold_in(rng, 6)
    for position, parts in pieces:
        heights = jnp.exp(jax.random.uniform(jax.random.fold_in(own, position), (parts,), jnp.float32, low / len(pieces), high / len(pieces)))
        gain = gain * jnp.repeat(heights, extent[position] // parts).reshape([-1 if axis == position else 1 for axis in range(len(extent))])
    return gain


def profile(amount, total, reach, slope):
    loads = [(1 << 20) // math.isqrt(grade ** slope) + 1 for grade in range(2, amount + 1)]
    surplus, holding = total - reach - (amount - 1), [1] * (amount - 1)
    while surplus > 0:
        movable = [i for i in range(amount - 1) if holding[i] < reach]
        pool, remaining = sum([loads[i] for i in movable]), surplus
        for i in movable:
            addition = min(reach - holding[i], max(1, remaining * loads[i] // pool), surplus)
            holding[i] = holding[i] + addition
            surplus = surplus - addition
    return np.array([reach] + holding)


def uneven_parts(rng, count, total, most, slope):
    if count == 2:
        one = jax.random.randint(rng, (), max(1, total - most), min(most, total - 1) + 1)
        return jnp.stack([one, total - one])
    sizes = jnp.asarray(profile(count, total, most, slope), jnp.int32)
    twos = (count - 1) // 2
    source_of, taker = sizes[1:1 + 2 * twos:2], sizes[2:2 + 2 * twos:2]
    slack = jnp.minimum(source_of - 1, most - taker)
    shifted = jax.random.randint(jax.random.fold_in(rng, 1), (twos,), 0, 1 << 20) % (slack + 1)
    sizes = sizes.at[1:1 + 2 * twos:2].set(source_of - shifted).at[2:2 + 2 * twos:2].set(taker + shifted)
    return sizes[jax.random.permutation(jax.random.fold_in(rng, 2), count)]


def noise(own_key, shape, spread, most, shards=(), held_as=jnp.bfloat16):
    gain = shard_levels(own_key, shape, shards, -0.22, 0.18) if shards else 1.0
    array = jax.random.normal(own_key, shape, jnp.float32) * spread * gain
    return jnp.minimum(jnp.maximum(array, -most), most).astype(held_as)


def gaussian_with(stream_key, shape, spread, limit, shards, heavy, held_as=jnp.bfloat16):
    result = spread * jax.random.normal(stream_key, shape, jnp.float32)
    if shards:
        result = result * shard_levels(stream_key, shape, shards, -0.22, 0.18)
    return jnp.clip(with_spikes(result, jax.random.fold_in(stream_key, 3), *heavy), -limit, limit).astype(held_as)


def setup_inputs(seed: int = 0, part: int = 0) -> dict:
    arg_keys = jax.random.split(jax.random.key(seed), 8)
    own_keys = jax.random.split(jax.random.fold_in(arg_keys[7], part), 8)
    activations = noise(own_keys[0], (TOKENS, D), 1.0, 6.0, ((0, 16),))
    out_grads = gaussian_with(own_keys[1], (TOKENS, FF), 1.0, 6.0, ((1, 16),), (1, 0, 16, 2.0))
    proj_in = noise(arg_keys[2], (D, PROJ), D ** -0.5, 0.0625)
    proj_out = noise(arg_keys[3], (FF, PROJ), FF ** -0.5, 0.03125, ((0, 16),))
    queries = noise(arg_keys[4], (QUERIES, FEAT), FEAT ** -0.5, 0.09375, ((0, 16),))
    doc_length = uneven_parts(own_keys[5], DOCS, TOKENS, MOST, 2).astype(jnp.int32)
    valid_count = set_ends(jax.random.randint(own_keys[6], (DOCS,), 1, MOST + 1), jax.random.fold_in(own_keys[6], 1), 1, MOST).astype(jnp.int32)
    return {"activations": activations, "out_grads": out_grads, "proj_in": proj_in, "proj_out": proj_out, "queries": queries, "doc_length": doc_length, "valid_count": valid_count}


def document_mask(glob_rows, doc_length, valid_count):
    ends = jnp.cumsum(doc_length).astype(jnp.int32)
    starts = ends - doc_length
    used = jnp.minimum(valid_count, doc_length)
    upper = starts + used
    inside = (glob_rows[None, :] >= starts[:, None]) & (glob_rows[None, :] < upper[:, None])
    return (inside.astype(jnp.float32), used)

def reference(activations, out_grads, proj_in, proj_out, queries, doc_length, valid_count):
    act_proj = jnp.dot(activations, proj_in, preferred_element_type=jnp.float32)
    grad_proj = jnp.dot(out_grads, proj_out, preferred_element_type=jnp.float32)
    count = act_proj.shape[0]
    width = act_proj.shape[1]
    outer = (grad_proj[:, :, None] * act_proj[:, None, :]).reshape(count, width * width).astype(jnp.bfloat16)
    token_scores = lax.dot_general(outer, queries, (((1,), (1,)), ((), ())), preferred_element_type=jnp.float32)
    glob_rows = jnp.arange(count, dtype=jnp.int32)
    member, used = document_mask(glob_rows, doc_length, valid_count)
    doc_outer = jnp.dot(member.astype(jnp.bfloat16), outer, preferred_element_type=jnp.float32)
    raw = lax.dot_general(doc_outer, queries.astype(jnp.float32), (((1,), (1,)), ((), ())), precision=lax.Precision.HIGHEST)
    doc_scores = raw / jnp.sqrt(used.astype(jnp.float32))[:, None]
    return (token_scores, doc_scores)
```

```python
import jax
import jax.numpy as jnp
from jax import lax
from jax.sharding import PartitionSpec as P


def document_mask(glob_rows, doc_length, valid_count):
    ends = jnp.cumsum(doc_length)
    starts = ends - doc_length
    used = jnp.minimum(valid_count, doc_length)
    upper = starts + used
    inside = (glob_rows[None, :] >= starts[:, None]) & (glob_rows[None, :] < upper[:, None])
    return (inside.astype(jnp.float32), used)


def gather_xor(block, size, order):
    place = [0]
    for bit in order:
        got = lax.ppermute(block, "seq", [(i, i ^ bit) for i in range(size)])
        block = jnp.concatenate([block, got], axis=0)
        place = place + [p ^ bit for p in place]
    return block, place


def link_order(size):
    bits = []
    bit = 2
    while bit < size:
        bits.append(bit)
        bit *= 2
    return bits[1:] + bits[:1] + [1]


def body(size, activations, out_grads, proj_in, proj_out, queries, doc_length, valid_count):
    rows = activations.shape[0]
    width = proj_in.shape[1]
    own_q = queries.shape[0]
    me = lax.axis_index("seq")
    panel, place = gather_xor(queries, size, link_order(size))

    grad_part = lax.dot_general(
        proj_out, out_grads, (((0,), (1,)), ((), ())), preferred_element_type=jnp.float32
    )
    pieces = grad_part.reshape(width, size, rows).transpose(1, 0, 2)
    got = lax.all_to_all(pieces, "seq", 0, 0, tiled=True)
    act_proj = lax.dot_general(
        proj_in, activations, (((0,), (1,)), ((), ())), preferred_element_type=jnp.float32
    )
    grad_proj = got.sum(axis=0)
    outer = (
        (grad_proj[:, None, :] * act_proj[None, :, :])
        .reshape(width * width, rows)
        .astype(jnp.bfloat16)
    )
    scores = jnp.dot(panel, outer, preferred_element_type=jnp.float32)
    blocks = scores.reshape(size, own_q, rows)
    inverse = [0] * size
    for k, p in enumerate(place):
        inverse[p] = k
    turn = jnp.asarray(inverse, jnp.int32)[jnp.arange(size, dtype=jnp.int32) ^ me]
    blocks = blocks[turn]
    token_scores = blocks.reshape(size * own_q, rows).T
    own_rows = me * rows + jnp.arange(rows, dtype=jnp.int32)
    member, used = document_mask(own_rows, doc_length, valid_count)
    scale = 1.0 / jnp.sqrt(used.astype(jnp.float32))
    partial = lax.dot_general(
        blocks, member, (((2,), (1,)), ((), ())), precision=lax.Precision.HIGHEST
    )
    doc_raw = lax.all_to_all(partial, "seq", 0, 0, tiled=True).sum(axis=0)
    doc_scores = (doc_raw * scale[None, :]).T
    return (token_scores, doc_scores)


def solution(mesh):
    size = mesh.shape["seq"]
    placed = (
        P(("groups", "seq"), None),
        P("groups", "seq"),
        P(),
        P("seq", None),
        P("seq", None),
        P("groups"),
        P("groups"),
    )

    def run(*args):
        return body(size, *args)

    return jax.shard_map(
        run,
        mesh=mesh,
        in_specs=placed,
        out_specs=(P(("groups", "seq"), None), P("groups", "seq")),
        check_vma=False,
    )
```

```python
import functools

import jax
import jax.numpy as jnp
from jax import lax
from jax.experimental import pallas as pl
from jax.experimental.pallas import tpu as pltpu
from jax.sharding import PartitionSpec as P

MIB = 1 << 20


def bit_groups(size):
    bits = [1 << k for k in range(size.bit_length() - 1)]
    groups = [bits[:1]]
    rest = bits[1:]
    if len(rest) % 2:
        groups.append(rest[:1])
        rest = rest[1:]
    while rest:
        groups.append(rest[:2])
        rest = rest[2:]
    return [g for g in groups if g]


def offset_of(part, bits):
    last = len(bits) - 1
    return sum(bit for k, bit in enumerate(bits) if (part >> (last - k)) & 1)


def reverse_bits(position, size):
    count = size.bit_length() - 1
    total = 0
    for k in range(count):
        total = total + (((position >> k) & 1) << (count - 1 - k))
    return total


def swap(value, offset, size):
    return lax.ppermute(value, "seq", [(i, i ^ offset) for i in range(size)])


def stage_parts(current, bits, size):
    count = 1 << len(bits)
    depth = current.shape[0] // count
    parts = [current[:depth]]
    for k in range(1, count):
        parts.append(swap(current[k * depth : (k + 1) * depth], offset_of(k, bits), size))
    return parts


def grad_kernel(per_step, me_ref, proj_ref, *refs):
    del me_ref
    out_ref = refs[per_step]
    for k in range(per_step):
        rows = lax.dot_general(
            refs[k][...],
            proj_ref[...],
            (((1,), (1,)), ((), ())),
            preferred_element_type=jnp.float32,
        )
        out_ref[k] = rows.T


def grad_blocks(me, proj, out_grads, rows, size, first, count):
    width, depth = proj.shape
    per_step = min(2, count)

    def place(k, step, me_ref):
        return (reverse_bits(first + step * per_step + k, size) ^ me_ref[0], 0)

    return pl.pallas_call(
        functools.partial(grad_kernel, per_step),
        grid_spec=pltpu.PrefetchScalarGridSpec(
            num_scalar_prefetch=1,
            grid=(count // per_step,),
            in_specs=[pl.BlockSpec((width, depth), lambda step, me_ref: (0, 0))]
            + [pl.BlockSpec((rows, depth), functools.partial(place, k)) for k in range(per_step)],
            out_specs=pl.BlockSpec((per_step, width, rows), lambda step, me_ref: (step, 0, 0)),
        ),
        out_shape=jax.ShapeDtypeStruct((count, width, rows), jnp.float32),
        compiler_params=pltpu.CompilerParams(vmem_limit_bytes=52 * MIB),
        cost_estimate=pl.CostEstimate(
            flops=2 * count * rows * depth * width,
            bytes_accessed=2 * count * rows * depth,
            transcendentals=0,
        ),
    )(me, proj, *([out_grads] * per_step))


def score_kernel(
    size,
    halves,
    sums,
    panels,
    place,
    me_ref,
    group_ref,
    length_ref,
    valid_ref,
    act_ref,
    *refs,
):
    grad_refs = refs[:sums]
    panel_refs = refs[sums : sums + panels]
    token_ref, doc_ref, outer_ref, turned_ref = refs[sums + panels :]
    me = me_ref[0]
    act = act_ref[...]
    width, rows = act.shape
    grad = grad_refs[0][0]
    for ref in grad_refs[1:]:
        grad = grad + ref[0]
    for i in range(width):
        outer_ref[i * width : (i + 1) * width] = (act * grad[i : i + 1]).astype(jnp.bfloat16)
    depth = width * width // halves
    scores = None
    for h in range(halves):
        start = (group_ref[0] ^ h) * depth if halves > 1 else 0
        part = jnp.concatenate([panel_refs[h][...], panel_refs[halves + h][...]], axis=0)
        term = jnp.dot(
            part,
            outer_ref[pl.ds(pl.multiple_of(start, depth), depth)],
            preferred_element_type=jnp.float32,
        )
        scores = term if scores is None else scores + term
    own_q = scores.shape[0] // size
    for k, p in enumerate(place):
        spot = pl.multiple_of((me ^ p) * own_q, own_q)
        turned_ref[pl.ds(spot, own_q)] = scores[k * own_q : (k + 1) * own_q]
    turned = turned_ref[...]
    token_ref[...] = turned.T

    docs = length_ref.shape[0]
    doc_of = lax.broadcasted_iota(jnp.int32, (docs, rows), 0)
    lower = jnp.zeros((docs, rows), jnp.int32)
    used = jnp.zeros((docs, rows), jnp.int32)
    start = jnp.int32(0)
    for d in range(docs):
        lower = jnp.where(doc_of == d, start, lower)
        used = jnp.where(doc_of == d, jnp.minimum(valid_ref[d], length_ref[d]), used)
        start = start + length_ref[d]
    token = me * rows + lax.broadcasted_iota(jnp.int32, (docs, rows), 1)
    inside = (token >= lower) & (token < lower + used)
    member = jnp.where(inside, 1.0 / jnp.sqrt(used.astype(jnp.float32)), 0.0)
    partial = lax.dot_general(
        turned,
        member,
        (((1,), (1,)), ((), ())),
        precision=lax.Precision.HIGHEST,
        preferred_element_type=jnp.float32,
    )
    turned_ref[:, :docs] = partial
    for p in range(size):
        spot = pl.multiple_of((me ^ reverse_bits(p, size)) * own_q, own_q)
        doc_ref[p] = turned_ref[pl.ds(spot, own_q), :docs]


def score(me, group, lengths, valid, act, grads, panels, place, size, own_q):
    width, rows = act.shape
    docs = lengths.shape[0]
    halves = len(panels) // 2
    smem = pl.BlockSpec(memory_space=pltpu.SMEM)
    vmem = pl.BlockSpec(memory_space=pltpu.VMEM)
    count = size * own_q
    return pl.pallas_call(
        functools.partial(score_kernel, size, halves, len(grads), len(panels), place),
        in_specs=[smem] * 4 + [vmem] * (1 + len(grads) + len(panels)),
        out_specs=(vmem, vmem),
        out_shape=(
            jax.ShapeDtypeStruct((rows, count), jnp.float32),
            jax.ShapeDtypeStruct((size, own_q, docs), jnp.float32),
        ),
        scratch_shapes=[
            pltpu.VMEM((width * width, rows), jnp.bfloat16),
            pltpu.VMEM((count, rows), jnp.float32),
        ],
        compiler_params=pltpu.CompilerParams(vmem_limit_bytes=32 * MIB),
        cost_estimate=pl.CostEstimate(
            flops=2 * rows * width * width * count,
            bytes_accessed=2 * count * width * width,
            transcendentals=0,
        ),
    )(me, group, lengths, valid, act, *grads, *panels)


def gather_queries(queries, size, groups, group):
    if groups == 2:
        half = queries.shape[1] // 2
        panel = lax.dynamic_slice(queries, (0, group * half), (queries.shape[0], half))
    else:
        panel = queries
    place = [0]
    stages = bit_groups(size)
    for bits in stages[:0:-1]:
        offsets = [offset_of(k, bits) for k in range(1, 1 << len(bits))]
        panel = jnp.concatenate([panel] + [swap(panel, o, size) for o in offsets], axis=0)
        place = [p ^ o for o in [0] + offsets for p in place]
    panels = [panel]
    if groups == 2:
        panels.append(lax.ppermute(panel, "groups", [(0, 1), (1, 0)]))
    panels = panels + [swap(part, 1, size) for part in panels]
    return panels, tuple(place + [p ^ 1 for p in place])


def body(size, groups, activations, out_grads, proj_in, proj_out, queries, doc_length, valid_count):
    rows = activations.shape[0]
    me = lax.axis_index("seq").astype(jnp.int32)
    group = lax.axis_index("groups").astype(jnp.int32)
    panels, place = gather_queries(queries, size, groups, group)

    proj = proj_out.T
    half = size // 2
    stages = bit_groups(size)
    theirs = grad_blocks(me[None], proj, out_grads, rows, size, half, half)
    from_core = swap(theirs, 1, size)
    current = grad_blocks(me[None], proj, out_grads, rows, size, 0, half) + from_core
    for bits in stages[1:-1]:
        parts = stage_parts(current, bits, size)
        current = functools.reduce(jnp.add, parts)
    grads = stage_parts(current, stages[-1], size)

    act = lax.dot_general(
        proj_in, activations, (((0,), (1,)), ((), ())), preferred_element_type=jnp.float32
    )
    token_scores, doc = score(
        me[None],
        group[None],
        doc_length,
        valid_count,
        act,
        grads,
        panels,
        place,
        size,
        queries.shape[0],
    )
    bits = [b for g in stages for b in g]
    for k in range(0, len(bits), 2):
        doc = functools.reduce(jnp.add, stage_parts(doc, bits[k : k + 2], size))
    return (token_scores, doc[0].T)


def solution(mesh):
    size = mesh.shape["seq"]
    groups = mesh.shape["groups"]
    placed = (
        P(("groups", "seq"), None),
        P("groups", "seq"),
        P(),
        P("seq", None),
        P("seq", None),
        P("groups"),
        P("groups"),
    )
    return jax.shard_map(
        functools.partial(body, size, groups),
        mesh=mesh,
        in_specs=placed,
        out_specs=(P(("groups", "seq"), None), P("groups", "seq")),
        check_vma=False,
    )
```

```python
import functools

import jax
import jax.numpy as jnp
from jax import lax
from jax.experimental import pallas as pl
from jax.experimental.pallas import tpu as pltpu
from jax.sharding import PartitionSpec as P

MIB = 1 << 20


def swap(value, offset, size):
    return lax.ppermute(value, "seq", [(i, i ^ offset) for i in range(size)])


def grad_kernel(core_ref, proj_ref, grads_ref, out_ref):
    del core_ref
    count, rows, depth = grads_ref.shape
    made = lax.dot_general(
        grads_ref[...].reshape(count * rows, depth),
        proj_ref[...],
        (((1,), (1,)), ((), ())),
        preferred_element_type=jnp.float32,
    )
    for k in range(count):
        out_ref[k] = made[k * rows : (k + 1) * rows].T


def grad_blocks(core, proj, out_grads, per_step):
    width, depth = proj.shape
    chips, _, rows, _ = out_grads.shape
    return pl.pallas_call(
        grad_kernel,
        grid_spec=pltpu.PrefetchScalarGridSpec(
            num_scalar_prefetch=1,
            grid=(chips // per_step,),
            in_specs=[
                pl.BlockSpec((width, depth), lambda step, core_ref: (0, 0)),
                pl.BlockSpec(
                    (per_step, None, rows, depth),
                    lambda step, core_ref: (step, core_ref[0], 0, 0),
                ),
            ],
            out_specs=pl.BlockSpec((per_step, width, rows), lambda step, core_ref: (step, 0, 0)),
        ),
        out_shape=jax.ShapeDtypeStruct((chips, width, rows), jnp.float32),
        compiler_params=pltpu.CompilerParams(vmem_limit_bytes=52 * MIB),
        cost_estimate=pl.CostEstimate(
            flops=2 * chips * rows * depth * width,
            bytes_accessed=2 * chips * rows * depth,
            transcendentals=0,
        ),
    )(core, proj, out_grads)


def score_kernel(size, low, place, me_ref, length_ref, valid_ref, act_ref, grad_ref, *refs):
    panel_refs = refs[:-4]
    token_ref, doc_ref, outer_ref, turned_ref = refs[-4:]
    me = me_ref[0]
    act = act_ref[...]
    width, rows = act.shape
    grad = grad_ref[0]
    for k in range(1, grad_ref.shape[0]):
        grad = grad + grad_ref[k]
    for i in range(width):
        outer_ref[i * width : (i + 1) * width] = (act * grad[i : i + 1]).astype(jnp.bfloat16)
    panel = jnp.concatenate([ref[...] for ref in panel_refs], axis=0)
    scores = jnp.dot(panel, outer_ref[...], preferred_element_type=jnp.float32)
    own_q = scores.shape[0] // size
    for k, (high, offset) in enumerate(place):
        spot = pl.multiple_of((((me & (low - 1)) ^ offset) + high) * own_q, own_q)
        turned_ref[pl.ds(spot, own_q)] = scores[k * own_q : (k + 1) * own_q]
    turned = turned_ref[...]
    token_ref[...] = turned.T

    docs = length_ref.shape[0]
    doc_of = lax.broadcasted_iota(jnp.int32, (docs, rows), 0)
    lower = jnp.zeros((docs, rows), jnp.int32)
    used = jnp.zeros((docs, rows), jnp.int32)
    start = jnp.int32(0)
    for d in range(docs):
        lower = jnp.where(doc_of == d, start, lower)
        used = jnp.where(doc_of == d, jnp.minimum(valid_ref[d], length_ref[d]), used)
        start = start + length_ref[d]
    token = me * rows + lax.broadcasted_iota(jnp.int32, (docs, rows), 1)
    inside = (token >= lower) & (token < lower + used)
    member = jnp.where(inside, 1.0 / jnp.sqrt(used.astype(jnp.float32)), 0.0)
    partial = lax.dot_general(
        turned,
        member,
        (((1,), (1,)), ((), ())),
        precision=lax.Precision.HIGHEST,
        preferred_element_type=jnp.float32,
    )
    for k in range(size):
        doc_ref[k] = partial[k * own_q : (k + 1) * own_q]


def score(me, lengths, valid, act, grads, panels, low, place, size, own_q):
    width, rows = act.shape
    docs = lengths.shape[0]
    smem = pl.BlockSpec(memory_space=pltpu.SMEM)
    vmem = pl.BlockSpec(memory_space=pltpu.VMEM)
    count = size * own_q
    return pl.pallas_call(
        functools.partial(score_kernel, size, low, place),
        in_specs=[smem] * 3 + [vmem] * (2 + len(panels)),
        out_specs=(vmem, vmem),
        out_shape=(
            jax.ShapeDtypeStruct((rows, count), jnp.float32),
            jax.ShapeDtypeStruct((size, own_q, docs), jnp.float32),
        ),
        scratch_shapes=[
            pltpu.VMEM((width * width, rows), jnp.bfloat16),
            pltpu.VMEM((count, rows), jnp.float32),
        ],
        compiler_params=pltpu.CompilerParams(vmem_limit_bytes=32 * MIB),
        cost_estimate=pl.CostEstimate(
            flops=2 * rows * width * width * count,
            bytes_accessed=2 * count * width * width,
            transcendentals=0,
        ),
    )(me, lengths, valid, act, grads, *panels)


def gather_lines(queries, size):
    count = size.bit_length() - 1
    low = 1 << (count - count // 2)
    lines = [[low * k + i for k in range(size // low)] for i in range(low)]
    return lax.all_gather(queries, "seq", axis=0, tiled=True, axis_index_groups=lines), low


def gather_queries(panel, low, size):
    place = [(low * k, 0) for k in range(size // low)]
    offset = low // 2
    while offset > 1:
        panel = jnp.concatenate([panel, swap(panel, offset, size)], axis=0)
        place = place + [(high, o ^ offset) for high, o in place]
        offset //= 2
    place = place + [(high, o ^ 1) for high, o in place]
    return [panel, swap(panel, 1, size)], tuple(place)


def body(size, activations, out_grads, proj_in, proj_out, queries, doc_length, valid_count):
    rows = activations.shape[0]
    me = lax.axis_index("seq").astype(jnp.int32)
    panel, low = gather_lines(queries, size)

    proj = proj_out.T
    chips = size // 2
    split = out_grads.reshape(chips, 2, rows, out_grads.shape[1])
    core = (me & 1)[None]
    from_core = swap(grad_blocks(1 - core, proj, split, 2), 1, size)
    chip_sum = grad_blocks(core, proj, split, 2) + from_core
    alike = [[2 * k + c for k in range(chips)] for c in range(2)]
    grads = lax.all_to_all(chip_sum, "seq", 0, 0, tiled=True, axis_index_groups=alike)

    panel, _ = lax.optimization_barrier((panel, chip_sum))
    panels, place = gather_queries(panel, low, size)
    act = lax.dot_general(
        proj_in, activations, (((0,), (1,)), ((), ())), preferred_element_type=jnp.float32
    )
    token_scores, doc = score(
        me[None],
        doc_length,
        valid_count,
        act,
        grads,
        panels,
        low,
        place,
        size,
        queries.shape[0],
    )
    doc = lax.all_to_all(doc, "seq", 0, 0, tiled=True).sum(axis=0)
    return (token_scores, doc.T)


def solution(mesh):
    size = mesh.shape["seq"]
    placed = (
        P(("groups", "seq"), None),
        P("groups", "seq"),
        P(),
        P("seq", None),
        P("seq", None),
        P("groups"),
        P("groups"),
    )
    return jax.shard_map(
        functools.partial(body, size),
        mesh=mesh,
        in_specs=placed,
        out_specs=(P(("groups", "seq"), None), P("groups", "seq")),
        check_vma=False,
    )
```

```python
import functools

import jax
import jax.numpy as jnp
from jax import lax
from jax.experimental import pallas as pl
from jax.experimental.pallas import tpu as pltpu
from jax.sharding import PartitionSpec as P

MIB = 1 << 20
SMEM = pl.BlockSpec(memory_space=pltpu.SMEM)
VMEM = pl.BlockSpec(memory_space=pltpu.VMEM)
HBM = pl.BlockSpec(memory_space=pltpu.HBM)


def swap(value, offset, size):
    return lax.ppermute(value, "seq", [(i, i ^ offset) for i in range(size)])


def grad_kernel(offsets, me_ref, proj_ref, grads_ref, out_ref, proj_buf, grads_buf, proj_sem, sems):
    count, rows, depth = grads_buf.shape
    load = pltpu.make_async_copy(proj_ref, proj_buf, proj_sem)
    load.start()
    copies = []
    for k, offset in enumerate(offsets):
        first = pl.multiple_of((me_ref[0] ^ offset) * rows, rows)
        copy = pltpu.make_async_copy(grads_ref.at[pl.ds(first, rows)], grads_buf.at[k], sems.at[k])
        copy.start()
        copies.append(copy)
    load.wait()
    for k in range(0, count, 2):
        copies[k].wait()
        copies[k + 1].wait()
        made = lax.dot_general(
            proj_buf[...],
            grads_buf[k : k + 2].reshape(2 * rows, depth),
            (((1,), (1,)), ((), ())),
            preferred_element_type=jnp.float32,
        )
        out_ref[k] = made[:, :rows]
        out_ref[k + 1] = made[:, rows:]


def grad_blocks(me, proj, out_grads, rows, offsets):
    width, depth = proj.shape
    count = len(offsets)
    return pl.pallas_call(
        functools.partial(grad_kernel, offsets),
        in_specs=[SMEM, HBM, HBM],
        out_specs=VMEM,
        out_shape=jax.ShapeDtypeStruct((count, width, rows), jnp.float32),
        scratch_shapes=[
            pltpu.VMEM((width, depth), jnp.bfloat16),
            pltpu.VMEM((count, rows, depth), jnp.bfloat16),
            pltpu.SemaphoreType.DMA,
            pltpu.SemaphoreType.DMA((count,)),
        ],
        compiler_params=pltpu.CompilerParams(vmem_limit_bytes=52 * MIB),
        cost_estimate=pl.CostEstimate(
            flops=2 * count * rows * depth * width,
            bytes_accessed=2 * count * rows * depth,
            transcendentals=0,
        ),
    )(me, proj, out_grads)


def inner_kernel(pieces, act_ref, *refs):
    out_ref = refs[pieces]
    columns = []
    for r in range(act_ref.shape[0]):
        act = act_ref[r]
        high = act.astype(jnp.bfloat16)
        low = (act - high.astype(jnp.float32)).astype(jnp.bfloat16)
        none = jnp.zeros_like(high)
        columns.append(jnp.concatenate([high, none, low, none], axis=0))
        columns.append(jnp.concatenate([none, high, none, low], axis=0))
    table = jnp.concatenate(columns, axis=1)
    pair = 2 * act_ref.shape[1]
    rows = []
    for k in range(refs[0].shape[1] // pair):
        for ref in refs[:pieces]:
            rows.append(ref[:, k * pair : (k + 1) * pair])
    left = jnp.concatenate(rows, axis=0)
    left = jnp.concatenate([left, left], axis=1)
    out_ref[...] = jnp.dot(left, table, preferred_element_type=jnp.float32)


def inner(act, panels, steps):
    halves, width, rows = act.shape
    count = sum(p.shape[0] for p in panels)
    pairs = panels[0].shape[1] // (2 * width)
    total = pairs * count
    if steps == 1:
        grid = {"in_specs": [VMEM] * (1 + len(panels)), "out_specs": VMEM}
    else:
        grid = {
            "grid": (steps,),
            "in_specs": [VMEM]
            + [pl.BlockSpec((p.shape[0], p.shape[1] // steps), lambda s: (0, s)) for p in panels],
            "out_specs": pl.BlockSpec((total // steps, 2 * halves * rows), lambda s: (s, 0)),
        }
    return pl.pallas_call(
        functools.partial(inner_kernel, len(panels)),
        out_shape=jax.ShapeDtypeStruct((total, 2 * halves * rows), jnp.float32),
        compiler_params=pltpu.CompilerParams(vmem_limit_bytes=32 * MIB),
        cost_estimate=pl.CostEstimate(
            flops=16 * total * width * halves * rows,
            bytes_accessed=8 * total * halves * rows,
            transcendentals=0,
        ),
        **grid,
    )(act, *panels)


def score_kernel(steps, top, me_ref, length_ref, valid_ref, own_ref, other_ref, inner_ref, token_ref, doc_ref, grad_ref):
    halves, width, rows = own_ref.shape
    count = token_ref.shape[1]
    pairs = inner_ref.shape[0] // count
    step = pl.program_id(0) if steps > 1 else 0

    def begin():
        for r in range(halves):
            grad_ref[r] = own_ref[r] + other_ref[halves - 1 - r]

    if steps == 1:
        begin()
    else:
        pl.when(step == 0)(begin)

    for r in range(halves):
        total = None
        for k in range(pairs):
            for parity in range(2):
                if steps == 1:
                    line = grad_ref[r, 2 * k + parity : 2 * k + parity + 1]
                else:
                    line = grad_ref[r, pl.ds(2 * (step * pairs + k) + parity, 1)]
                column = (2 * r + parity) * rows
                term = line * inner_ref[k * count : (k + 1) * count, column : column + rows]
                total = term if total is None else total + term
        if steps == 1:
            token_ref[r] = total
        else:
            token_ref[r] = jnp.where(step == 0, total, token_ref[r] + total)

    def finish():
        me = me_ref[0]
        docs = length_ref.shape[0]
        doc_of = lax.broadcasted_iota(jnp.int32, (docs, rows), 0)
        lower = jnp.zeros((docs, rows), jnp.int32)
        used = jnp.zeros((docs, rows), jnp.int32)
        start = jnp.int32(0)
        for d in range(docs):
            lower = jnp.where(doc_of == d, start, lower)
            used = jnp.where(doc_of == d, jnp.minimum(valid_ref[d], length_ref[d]), used)
            start = start + length_ref[d]
        scale = 1.0 / jnp.sqrt(used.astype(jnp.float32))
        partial = None
        for r in range(halves):
            token = (me ^ (top * r)) * rows + lax.broadcasted_iota(jnp.int32, (docs, rows), 1)
            inside = (token >= lower) & (token < lower + used)
            term = lax.dot_general(
                token_ref[r],
                jnp.where(inside, scale, 0.0),
                (((1,), (1,)), ((), ())),
                precision=lax.Precision.HIGHEST,
                preferred_element_type=jnp.float32,
            )
            partial = term if partial is None else partial + term
        own_q = doc_ref.shape[1]
        for k in range(doc_ref.shape[0]):
            doc_ref[k] = partial[k * own_q : (k + 1) * own_q]

    if steps == 1:
        finish()
    else:
        pl.when(step == steps - 1)(finish)


def score(me, lengths, valid, own, other, products, top, own_q, steps):
    halves, width, rows = own.shape
    docs = lengths.shape[0]
    count = 2 * products.shape[0] // width
    if steps == 1:
        grid = {"in_specs": [SMEM] * 3 + [VMEM] * 3, "out_specs": (VMEM, VMEM)}
    else:
        block = (products.shape[0] // steps, products.shape[1])
        grid = {
            "grid": (steps,),
            "in_specs": [SMEM] * 3 + [VMEM] * 2 + [pl.BlockSpec(block, lambda s: (s, 0))],
            "out_specs": (VMEM, VMEM),
        }
    return pl.pallas_call(
        functools.partial(score_kernel, steps, top),
        out_shape=(
            jax.ShapeDtypeStruct((halves, count, rows), jnp.float32),
            jax.ShapeDtypeStruct((count // own_q, own_q, docs), jnp.float32),
        ),
        scratch_shapes=[pltpu.VMEM((halves, width, rows), jnp.float32)],
        compiler_params=pltpu.CompilerParams(vmem_limit_bytes=32 * MIB),
        cost_estimate=pl.CostEstimate(
            flops=2 * products.shape[0] * products.shape[1],
            bytes_accessed=4 * products.shape[0] * products.shape[1],
            transcendentals=0,
        ),
        **grid,
    )(me, lengths, valid, own, other, products)


def place_kernel(place, top, own_q, me_ref, own_ref, other_ref, out_ref, turned_ref):
    for r, ref in enumerate((own_ref, other_ref)):
        for k, offset in enumerate(place):
            spot = pl.multiple_of((me_ref[0] ^ (offset + top * r)) * own_q, own_q)
            turned_ref[pl.ds(spot, own_q)] = ref[k * own_q : (k + 1) * own_q]
    out_ref[...] = turned_ref[...].T


def place_tokens(me, own, other, place, top, own_q):
    count, rows = own.shape
    return pl.pallas_call(
        functools.partial(place_kernel, place, top, own_q),
        in_specs=[SMEM, VMEM, VMEM],
        out_specs=VMEM,
        out_shape=jax.ShapeDtypeStruct((rows, 2 * count), jnp.float32),
        scratch_shapes=[pltpu.VMEM((2 * count, rows), jnp.float32)],
    )(me, own, other)


def body(size, activations, out_grads, proj_in, proj_out, queries, doc_length, valid_count):
    rows = activations.shape[0]
    width = proj_in.shape[1]
    own_q = queries.shape[0]
    me = lax.axis_index("seq").astype(jnp.int32)[None]
    top = size // 2
    middle = [1 << k for k in range(1, top.bit_length() - 1)]

    panel, place = queries, [0]
    panels = []
    for bit in middle[::-1]:
        got = swap(panel, bit, size)
        place = place + [p ^ bit for p in place]
        panel = jnp.concatenate([panel, got], axis=0)
    panels = [panel, swap(panel, 1, size)]
    place = tuple(place + [p ^ 1 for p in place])

    proj = pltpu.with_memory_space_constraint(proj_out.T, pltpu.HBM)
    spots = [2 * m + top * r for m in range(top // 2) for r in range(2)]
    from_core = swap(grad_blocks(me, proj, out_grads, rows, [s + 1 for s in spots]), 1, size)
    chip_sums = grad_blocks(me, proj, out_grads, rows, spots) + from_core
    sums = chip_sums
    for bit in middle[::-1]:
        half = sums.shape[0] // 2
        sums = sums[:half] + swap(sums[half:], bit, size)
    across = swap(sums, top, size)

    late, _ = lax.optimization_barrier((proj_in, chip_sums))
    act = lax.dot_general(
        late, activations, (((0,), (1,)), ((), ())), preferred_element_type=jnp.float32
    )
    act = jnp.stack([act, swap(act, top, size)])
    steps = max(1, 8 * width * top * own_q * rows // (4 * MIB))
    products = inner(act, panels, steps)
    tokens, doc = score(me, doc_length, valid_count, sums, across, products, top, own_q, steps)
    others = swap(tokens[1], top, size)
    token_scores = place_tokens(me, tokens[0], others, place, top, own_q)
    for bit in [1] + middle:
        half = doc.shape[0] // 2
        if half == 1:
            doc, _ = lax.optimization_barrier((doc, others))
        doc = doc[:half] + swap(doc[half:], bit, size)
    return (token_scores, doc[0].T)


def solution(mesh):
    size = mesh.shape["seq"]
    placed = (
        P(("groups", "seq"), None),
        P("groups", "seq"),
        P(),
        P("seq", None),
        P("seq", None),
        P("groups"),
        P("groups"),
    )
    return jax.shard_map(
        functools.partial(body, size),
        mesh=mesh,
        in_specs=placed,
        out_specs=(P(("groups", "seq"), None), P("groups", "seq")),
        check_vma=False,
    )
```

```python
import functools

import jax
import jax.numpy as jnp
from jax import lax
from jax.experimental import pallas as pl
from jax.experimental.pallas import tpu as pltpu
from jax.sharding import PartitionSpec as P

MIB = 1 << 20
SMEM = pl.BlockSpec(memory_space=pltpu.SMEM)
VMEM = pl.BlockSpec(memory_space=pltpu.VMEM)
HBM = pl.BlockSpec(memory_space=pltpu.HBM)


def swap(value, offset, size):
    return lax.ppermute(value, "seq", [(i, i ^ offset) for i in range(size)])


def grad_kernel(offsets, me_ref, proj_ref, grads_ref, out_ref, proj_buf, table, grads_buf, proj_sem, sems):
    halves, total, depth = grads_buf.shape
    count = len(offsets) // halves
    rows = total // count
    width = proj_buf.shape[0]
    load = pltpu.make_async_copy(proj_ref, proj_buf, proj_sem)
    load.start()
    copies = []
    for k, offset in enumerate(offsets):
        first = pl.multiple_of((me_ref[0] ^ offset) * rows, rows)
        copy = pltpu.make_async_copy(
            grads_ref.at[pl.ds(first, rows)],
            grads_buf.at[k % halves, pl.ds((k // halves) * rows, rows)],
            sems.at[k],
        )
        copy.start()
        copies.append(copy)
    load.wait()
    turned = proj_buf[...].T
    none = jnp.zeros_like(turned)
    for r in range(halves):
        table[r] = jnp.concatenate([turned if c == r else none for c in range(halves)], axis=1)
    for k in range(0, count, 2):
        for copy in copies[k * halves : (k + 2) * halves]:
            copy.wait()
        made = None
        for r in range(halves):
            part = jnp.dot(
                grads_buf[r, k * rows : (k + 2) * rows],
                table[r],
                preferred_element_type=jnp.float32,
            )
            made = part if made is None else made + part
        out_ref[k] = made[:rows]
        out_ref[k + 1] = made[rows:]


def grad_blocks(me, proj, out_grads, rows, offsets):
    width, depth = proj.shape
    count = len(offsets) // 2
    return pl.pallas_call(
        functools.partial(grad_kernel, offsets),
        in_specs=[SMEM, HBM, HBM],
        out_specs=VMEM,
        out_shape=jax.ShapeDtypeStruct((count, rows, 2 * width), jnp.float32),
        scratch_shapes=[
            pltpu.VMEM((width, depth), jnp.bfloat16),
            pltpu.VMEM((2, depth, 2 * width), jnp.bfloat16),
            pltpu.VMEM((2, count * rows, depth), jnp.bfloat16),
            pltpu.SemaphoreType.DMA,
            pltpu.SemaphoreType.DMA((2 * count,)),
        ],
        compiler_params=pltpu.CompilerParams(vmem_limit_bytes=52 * MIB),
        cost_estimate=pl.CostEstimate(
            flops=4 * count * rows * depth * width,
            bytes_accessed=4 * count * rows * depth,
            transcendentals=0,
        ),
    )(me, proj, out_grads)


def inner_kernel(pieces, act_ref, *refs):
    out_ref = refs[pieces]
    columns = []
    for r in range(act_ref.shape[0]):
        act = act_ref[r]
        high = act.astype(jnp.bfloat16)
        low = (act - high.astype(jnp.float32)).astype(jnp.bfloat16)
        none = jnp.zeros_like(high)
        columns.append(jnp.concatenate([high, none, low, none], axis=0))
        columns.append(jnp.concatenate([none, high, none, low], axis=0))
    table = jnp.concatenate(columns, axis=1)
    pair = 2 * act_ref.shape[1]
    rows = []
    for k in range(refs[0].shape[1] // pair):
        for ref in refs[:pieces]:
            rows.append(ref[:, k * pair : (k + 1) * pair])
    left = jnp.concatenate(rows, axis=0)
    left = jnp.concatenate([left, left], axis=1)
    out_ref[...] = jnp.dot(left, table, preferred_element_type=jnp.float32)


def inner(act, panels, steps):
    halves, width, rows = act.shape
    count = sum(p.shape[0] for p in panels)
    pairs = panels[0].shape[1] // (2 * width)
    total = pairs * count
    if steps == 1:
        grid = {"in_specs": [VMEM] * (1 + len(panels)), "out_specs": VMEM}
    else:
        grid = {
            "grid": (steps,),
            "in_specs": [VMEM]
            + [pl.BlockSpec((p.shape[0], p.shape[1] // steps), lambda s: (0, s)) for p in panels],
            "out_specs": pl.BlockSpec((total // steps, 2 * halves * rows), lambda s: (s, 0)),
        }
    return pl.pallas_call(
        functools.partial(inner_kernel, len(panels)),
        out_shape=jax.ShapeDtypeStruct((total, 2 * halves * rows), jnp.float32),
        compiler_params=pltpu.CompilerParams(vmem_limit_bytes=32 * MIB),
        cost_estimate=pl.CostEstimate(
            flops=16 * total * width * halves * rows,
            bytes_accessed=8 * total * halves * rows,
            transcendentals=0,
        ),
        **grid,
    )(act, *panels)


def score_kernel(
    steps, split, me_ref, length_ref, valid_ref, own_ref, other_ref, inner_ref, own_tok, other_tok, doc_ref, grad_ref
):
    rows, wide = own_ref.shape
    halves, width = 2, wide // 2
    count = own_tok.shape[0]
    pairs = inner_ref.shape[0] // count
    step = pl.program_id(0) if steps > 1 else 0
    tokens = (own_tok, other_tok)

    def begin():
        other = other_ref[...].T
        grad_ref[...] = own_ref[...].T + jnp.concatenate([other[width:], other[:width]], axis=0)

    if steps == 1:
        begin()
    else:
        pl.when(step == 0)(begin)

    for r in range(halves):
        total = None
        for k in range(pairs):
            for parity in range(2):
                feature = 2 * k + parity
                if steps == 1:
                    line = grad_ref[r * width + feature : r * width + feature + 1]
                else:
                    line = grad_ref[pl.ds(r * width + 2 * pairs * step + feature, 1)]
                column = (2 * r + parity) * rows
                term = line * inner_ref[k * count : (k + 1) * count, column : column + rows]
                total = term if total is None else total + term
        if steps == 1:
            tokens[r][...] = total
        else:
            tokens[r][...] = jnp.where(step == 0, total, tokens[r][...] + total)

    def finish():
        me = me_ref[0]
        docs = length_ref.shape[0]
        doc_of = lax.broadcasted_iota(jnp.int32, (docs, rows), 0)
        lower = jnp.zeros((docs, rows), jnp.int32)
        upper = jnp.zeros((docs, rows), jnp.int32)
        start = jnp.int32(0)
        for d in range(docs):
            lower = jnp.where(doc_of == d, start, lower)
            used = jnp.minimum(valid_ref[d], length_ref[d])
            upper = jnp.where(doc_of == d, start + used, upper)
            start = start + length_ref[d]
        members, parts = [], []
        for r in range(halves):
            token = (me ^ (split * r)) * rows + lax.broadcasted_iota(jnp.int32, (docs, rows), 1)
            inside = (token >= lower) & (token < upper)
            members.append(jnp.where(inside, 1.0, 0.0).astype(jnp.bfloat16))
            left = tokens[r][...]
            for _ in range(3):
                part = left.astype(jnp.bfloat16)
                left = left - part.astype(jnp.float32)
                parts.append(part)
        partial = lax.dot_general(
            jnp.concatenate(parts, axis=1),
            jnp.concatenate([m for m in members for _ in range(3)], axis=1),
            (((1,), (1,)), ((), ())),
            preferred_element_type=jnp.float32,
        )
        own_q = doc_ref.shape[1]
        for k in range(doc_ref.shape[0]):
            doc_ref[k] = partial[k * own_q : (k + 1) * own_q]

    if steps == 1:
        finish()
    else:
        pl.when(step == steps - 1)(finish)


def score(me, lengths, valid, own, other, products, split, own_q, steps):
    rows, wide = own.shape
    docs = lengths.shape[0]
    count = 4 * products.shape[0] // wide
    if steps == 1:
        grid = {"in_specs": [SMEM] * 3 + [VMEM] * 3, "out_specs": (VMEM,) * 3}
    else:
        block = (products.shape[0] // steps, products.shape[1])
        grid = {
            "grid": (steps,),
            "in_specs": [SMEM] * 3 + [VMEM] * 2 + [pl.BlockSpec(block, lambda s: (s, 0))],
            "out_specs": (VMEM,) * 3,
        }
    return pl.pallas_call(
        functools.partial(score_kernel, steps, split),
        out_shape=(
            jax.ShapeDtypeStruct((count, rows), jnp.float32),
            jax.ShapeDtypeStruct((count, rows), jnp.float32),
            jax.ShapeDtypeStruct((count // own_q, own_q, docs), jnp.float32),
        ),
        scratch_shapes=[pltpu.VMEM((wide, rows), jnp.float32)],
        compiler_params=pltpu.CompilerParams(vmem_limit_bytes=32 * MIB),
        cost_estimate=pl.CostEstimate(
            flops=2 * products.shape[0] * products.shape[1],
            bytes_accessed=4 * products.shape[0] * products.shape[1],
            transcendentals=0,
        ),
        **grid,
    )(me, lengths, valid, own, other, products)


def last_kernel(
    place, split, me_ref, length_ref, valid_ref, own_ref, other_ref, doc_ref, more_ref, token_out, doc_out, turned_ref
):
    own_q, docs = doc_out.shape
    for r, ref in enumerate((own_ref, other_ref)):
        for k, offset in enumerate(place):
            spot = pl.multiple_of((me_ref[0] ^ (offset + split * r)) * own_q, own_q)
            turned_ref[pl.ds(spot, own_q)] = ref[k * own_q : (k + 1) * own_q]
    token_out[...] = turned_ref[...].T
    doc_of = lax.broadcasted_iota(jnp.int32, (own_q, docs), 1)
    used = jnp.zeros((own_q, docs), jnp.int32)
    for d in range(docs):
        used = jnp.where(doc_of == d, jnp.minimum(valid_ref[d], length_ref[d]), used)
    doc_out[...] = (doc_ref[0] + more_ref[0]) * (1.0 / jnp.sqrt(used.astype(jnp.float32)))


def last(me, lengths, valid, own, other, doc, more, place, split):
    count, rows = own.shape
    _, own_q, docs = doc.shape
    return pl.pallas_call(
        functools.partial(last_kernel, place, split),
        in_specs=[SMEM] * 3 + [VMEM] * 4,
        out_specs=(VMEM, VMEM),
        out_shape=(
            jax.ShapeDtypeStruct((rows, 2 * count), jnp.float32),
            jax.ShapeDtypeStruct((own_q, docs), jnp.float32),
        ),
        scratch_shapes=[pltpu.VMEM((2 * count, rows), jnp.float32)],
    )(me, lengths, valid, own, other, doc, more)


def offset_of(number, bits):
    last_bit = len(bits) - 1
    return sum(bit for k, bit in enumerate(bits) if (number >> (last_bit - k)) & 1)


def body(size, activations, out_grads, proj_in, proj_out, queries, doc_length, valid_count):
    rows = activations.shape[0]
    width = proj_in.shape[1]
    own_q = queries.shape[0]
    me = lax.axis_index("seq").astype(jnp.int32)[None]
    split = size // 4
    middle = [1 << k for k in range(1, size.bit_length() - 1) if 1 << k != split]

    panel, place = queries, [0]
    got = swap(panel, middle[-1], size)

    proj = pltpu.with_memory_space_constraint(proj_out.T, pltpu.HBM)
    spots = [offset_of(m, middle) + split * r for m in range(size // 4) for r in range(2)]
    from_core = swap(grad_blocks(me, proj, out_grads, rows, [s + 1 for s in spots]), 1, size)
    sums = grad_blocks(me, proj, out_grads, rows, spots) + from_core
    late, _ = lax.optimization_barrier((proj_in, sums))
    for k, bit in enumerate(middle):
        half = sums.shape[0] // 2
        sent = swap(sums[half:].astype(jnp.bfloat16), bit, size)
        sums = sums[:half] + sent.astype(jnp.float32)
        if k == 0:
            got, _ = lax.optimization_barrier((got, sums))
    own = sums[0]
    across = swap(own, split, size)

    panel = jnp.concatenate([panel, got], axis=0)
    place = [0, middle[-1]]
    for bit in middle[-2::-1]:
        panel = jnp.concatenate([panel, swap(panel, bit, size)], axis=0)
        place = place + [p ^ bit for p in place]
    panels = [panel, swap(panel, 1, size)]
    place = tuple(place + [p ^ 1 for p in place])

    act = lax.dot_general(
        late, activations, (((0,), (1,)), ((), ())), preferred_element_type=jnp.float32
    )
    act = jnp.stack([act, swap(act, split, size)])
    steps = max(1, 4 * width * size * own_q * rows // (4 * MIB))
    products = inner(act, panels, steps)
    mine, theirs, doc = score(
        me, doc_length, valid_count, own, across, products, split, own_q, steps
    )
    others = swap(theirs, split, size)
    bits = [1] + middle
    for bit in bits[:-1]:
        half = doc.shape[0] // 2
        doc = doc[:half] + swap(doc[half:], bit, size)
    more = swap(doc[1:], bits[-1], size)
    token_scores, doc = last(
        me, doc_length, valid_count, mine, others, doc[:1], more, place, split
    )
    return (token_scores, doc.T)


def solution(mesh):
    size = mesh.shape["seq"]
    placed = (
        P(("groups", "seq"), None),
        P("groups", "seq"),
        P(),
        P("seq", None),
        P("seq", None),
        P("groups"),
        P("groups"),
    )
    return jax.shard_map(
        functools.partial(body, size),
        mesh=mesh,
        in_specs=placed,
        out_specs=(P(("groups", "seq"), None), P("groups", "seq")),
        check_vma=False,
    )
```

```python
import functools

import jax
import jax.numpy as jnp
from jax import lax
from jax.experimental import pallas as pl
from jax.experimental.pallas import tpu as pltpu
from jax.sharding import PartitionSpec as P

MIB = 1 << 20
SMEM = pl.BlockSpec(memory_space=pltpu.SMEM)
VMEM = pl.BlockSpec(memory_space=pltpu.VMEM)
HBM = pl.BlockSpec(memory_space=pltpu.HBM)


def swap(value, offset, size):
    return lax.ppermute(value, "seq", [(i, i ^ offset) for i in range(size)])


def grad_kernel(offsets, me_ref, proj_ref, grads_ref, out_ref, proj_buf, table, grads_buf, proj_sem, sems):
    halves, total, depth = grads_buf.shape
    count = len(offsets) // halves
    rows = total // count
    width = proj_buf.shape[0]
    load = pltpu.make_async_copy(proj_ref, proj_buf, proj_sem)
    load.start()
    copies = []
    for k, offset in enumerate(offsets):
        first = pl.multiple_of((me_ref[0] ^ offset) * rows, rows)
        copy = pltpu.make_async_copy(
            grads_ref.at[pl.ds(first, rows)],
            grads_buf.at[k % halves, pl.ds((k // halves) * rows, rows)],
            sems.at[k],
        )
        copy.start(priority=k % 2)
        copies.append(copy)
    load.wait()
    turned = proj_buf[...].T
    none = jnp.zeros_like(turned)
    for r in range(halves):
        table[r] = jnp.concatenate([turned if c == r else none for c in range(halves)], axis=1)
    for k in range(0, count, 2):
        for copy in copies[k * halves : (k + 2) * halves]:
            copy.wait()
        made = None
        for r in range(halves):
            part = jnp.dot(
                grads_buf[r, k * rows : (k + 2) * rows],
                table[r],
                preferred_element_type=jnp.float32,
            )
            made = part if made is None else made + part
        out_ref[k] = made[:rows]
        out_ref[k + 1] = made[rows:]


def grad_blocks(me, proj, out_grads, rows, offsets):
    width, depth = proj.shape
    count = len(offsets) // 2
    return pl.pallas_call(
        functools.partial(grad_kernel, offsets),
        in_specs=[SMEM, HBM, HBM],
        out_specs=VMEM,
        out_shape=jax.ShapeDtypeStruct((count, rows, 2 * width), jnp.float32),
        scratch_shapes=[
            pltpu.VMEM((width, depth), jnp.bfloat16),
            pltpu.VMEM((2, depth, 2 * width), jnp.bfloat16),
            pltpu.VMEM((2, count * rows, depth), jnp.bfloat16),
            pltpu.SemaphoreType.DMA,
            pltpu.SemaphoreType.DMA((2 * count,)),
        ],
        compiler_params=pltpu.CompilerParams(vmem_limit_bytes=52 * MIB),
        cost_estimate=pl.CostEstimate(
            flops=4 * count * rows * depth * width,
            bytes_accessed=4 * count * rows * depth,
            transcendentals=0,
        ),
    )(me, proj, out_grads)


def inner_kernel(pieces, act_ref, *refs):
    out_ref = refs[pieces]
    columns = []
    for r in range(act_ref.shape[0]):
        act = act_ref[r]
        high = act.astype(jnp.bfloat16)
        low = (act - high.astype(jnp.float32)).astype(jnp.bfloat16)
        none = jnp.zeros_like(high)
        columns.append(jnp.concatenate([high, none, low, none], axis=0))
        columns.append(jnp.concatenate([none, high, none, low], axis=0))
    table = jnp.concatenate(columns, axis=1)
    pair = 2 * act_ref.shape[1]
    rows = []
    for k in range(refs[0].shape[1] // pair):
        for ref in refs[:pieces]:
            rows.append(ref[:, k * pair : (k + 1) * pair])
    left = jnp.concatenate(rows, axis=0)
    left = jnp.concatenate([left, left], axis=1)
    out_ref[...] = jnp.dot(left, table, preferred_element_type=jnp.float32)


def inner(act, panels, steps):
    halves, width, rows = act.shape
    count = sum(p.shape[0] for p in panels)
    pairs = panels[0].shape[1] // (2 * width)
    total = pairs * count
    if steps == 1:
        grid = {"in_specs": [VMEM] * (1 + len(panels)), "out_specs": VMEM}
    else:
        grid = {
            "grid": (steps,),
            "in_specs": [VMEM]
            + [pl.BlockSpec((p.shape[0], p.shape[1] // steps), lambda s: (0, s)) for p in panels],
            "out_specs": pl.BlockSpec((total // steps, 2 * halves * rows), lambda s: (s, 0)),
        }
    return pl.pallas_call(
        functools.partial(inner_kernel, len(panels)),
        out_shape=jax.ShapeDtypeStruct((total, 2 * halves * rows), jnp.float32),
        compiler_params=pltpu.CompilerParams(vmem_limit_bytes=32 * MIB),
        cost_estimate=pl.CostEstimate(
            flops=16 * total * width * halves * rows,
            bytes_accessed=8 * total * halves * rows,
            transcendentals=0,
        ),
        **grid,
    )(act, *panels)


def score_kernel(
    steps, split, me_ref, length_ref, valid_ref, own_ref, other_ref, inner_ref, own_tok, other_tok, doc_ref, grad_ref
):
    rows, wide = own_ref.shape
    halves, width = 2, wide // 2
    count = own_tok.shape[0]
    pairs = inner_ref.shape[0] // count
    step = pl.program_id(0) if steps > 1 else 0
    tokens = (own_tok, other_tok)

    def begin():
        other = other_ref[...].T
        grad_ref[...] = own_ref[...].T + jnp.concatenate([other[width:], other[:width]], axis=0)

    if steps == 1:
        begin()
    else:
        pl.when(step == 0)(begin)

    for r in range(halves):
        total = None
        for k in range(pairs):
            for parity in range(2):
                feature = 2 * k + parity
                if steps == 1:
                    line = grad_ref[r * width + feature : r * width + feature + 1]
                else:
                    line = grad_ref[pl.ds(r * width + 2 * pairs * step + feature, 1)]
                column = (2 * r + parity) * rows
                term = line * inner_ref[k * count : (k + 1) * count, column : column + rows]
                total = term if total is None else total + term
        if steps == 1:
            tokens[r][...] = total
        else:
            tokens[r][...] = jnp.where(step == 0, total, tokens[r][...] + total)

    def finish():
        me = me_ref[0]
        docs = length_ref.shape[0]
        doc_of = lax.broadcasted_iota(jnp.int32, (docs, rows), 0)
        lower = jnp.zeros((docs, rows), jnp.int32)
        upper = jnp.zeros((docs, rows), jnp.int32)
        start = jnp.int32(0)
        for d in range(docs):
            lower = jnp.where(doc_of == d, start, lower)
            used = jnp.minimum(valid_ref[d], length_ref[d])
            upper = jnp.where(doc_of == d, start + used, upper)
            start = start + length_ref[d]
        members, parts = [], []
        for r in range(halves):
            token = (me ^ (split * r)) * rows + lax.broadcasted_iota(jnp.int32, (docs, rows), 1)
            inside = (token >= lower) & (token < upper)
            members.append(jnp.where(inside, 1.0, 0.0).astype(jnp.bfloat16))
            left = tokens[r][...]
            for _ in range(3):
                part = left.astype(jnp.bfloat16)
                left = left - part.astype(jnp.float32)
                parts.append(part)
        partial = lax.dot_general(
            jnp.concatenate(parts, axis=1),
            jnp.concatenate([m for m in members for _ in range(3)], axis=1),
            (((1,), (1,)), ((), ())),
            preferred_element_type=jnp.float32,
        )
        own_q = doc_ref.shape[1]
        for k in range(doc_ref.shape[0]):
            doc_ref[k] = partial[k * own_q : (k + 1) * own_q]

    if steps == 1:
        finish()
    else:
        pl.when(step == steps - 1)(finish)


def score(me, lengths, valid, own, other, products, split, own_q, steps):
    rows, wide = own.shape
    docs = lengths.shape[0]
    count = 4 * products.shape[0] // wide
    if steps == 1:
        grid = {"in_specs": [SMEM] * 3 + [VMEM] * 3, "out_specs": (VMEM,) * 3}
    else:
        block = (products.shape[0] // steps, products.shape[1])
        grid = {
            "grid": (steps,),
            "in_specs": [SMEM] * 3 + [VMEM] * 2 + [pl.BlockSpec(block, lambda s: (s, 0))],
            "out_specs": (VMEM,) * 3,
        }
    return pl.pallas_call(
        functools.partial(score_kernel, steps, split),
        out_shape=(
            jax.ShapeDtypeStruct((count, rows), jnp.float32),
            jax.ShapeDtypeStruct((count, rows), jnp.float32),
            jax.ShapeDtypeStruct((count // own_q, own_q, docs), jnp.float32),
        ),
        scratch_shapes=[pltpu.VMEM((wide, rows), jnp.float32)],
        compiler_params=pltpu.CompilerParams(vmem_limit_bytes=32 * MIB),
        cost_estimate=pl.CostEstimate(
            flops=2 * products.shape[0] * products.shape[1],
            bytes_accessed=4 * products.shape[0] * products.shape[1],
            transcendentals=0,
        ),
        **grid,
    )(me, lengths, valid, own, other, products)


def last_kernel(
    place, split, me_ref, length_ref, valid_ref, own_ref, other_ref, doc_ref, more_ref, token_out, doc_out, turned_ref
):
    own_q, docs = doc_out.shape
    for r, ref in enumerate((own_ref, other_ref)):
        for k, offset in enumerate(place):
            spot = pl.multiple_of((me_ref[0] ^ (offset + split * r)) * own_q, own_q)
            turned_ref[pl.ds(spot, own_q)] = ref[k * own_q : (k + 1) * own_q]
    token_out[...] = turned_ref[...].T
    doc_of = lax.broadcasted_iota(jnp.int32, (own_q, docs), 1)
    used = jnp.zeros((own_q, docs), jnp.int32)
    for d in range(docs):
        used = jnp.where(doc_of == d, jnp.minimum(valid_ref[d], length_ref[d]), used)
    doc_out[...] = (doc_ref[0] + more_ref[0]) * (1.0 / jnp.sqrt(used.astype(jnp.float32)))


def last(me, lengths, valid, own, other, doc, more, place, split):
    count, rows = own.shape
    _, own_q, docs = doc.shape
    return pl.pallas_call(
        functools.partial(last_kernel, place, split),
        in_specs=[SMEM] * 3 + [VMEM] * 4,
        out_specs=(VMEM, VMEM),
        out_shape=(
            jax.ShapeDtypeStruct((rows, 2 * count), jnp.float32),
            jax.ShapeDtypeStruct((own_q, docs), jnp.float32),
        ),
        scratch_shapes=[pltpu.VMEM((2 * count, rows), jnp.float32)],
        compiler_params=pltpu.CompilerParams(vmem_limit_bytes=16 * MIB),
    )(me, lengths, valid, own, other, doc, more)


def offset_of(number, bits):
    last_bit = len(bits) - 1
    return sum(bit for k, bit in enumerate(bits) if (number >> (last_bit - k)) & 1)


def body(size, activations, out_grads, proj_in, proj_out, queries, doc_length, valid_count):
    rows = activations.shape[0]
    width = proj_in.shape[1]
    own_q = queries.shape[0]
    me = lax.axis_index("seq").astype(jnp.int32)[None]
    split = size // 4
    middle = [1 << k for k in range(1, size.bit_length() - 1) if 1 << k != split]

    panel, place = queries, [0]
    got = swap(panel, middle[-1], size)

    proj = pltpu.with_memory_space_constraint(proj_out.T, pltpu.HBM)
    spots = [offset_of(m, middle) + split * r for m in range(size // 4) for r in range(2)]
    from_core = swap(grad_blocks(me, proj, out_grads, rows, [s + 1 for s in spots]), 1, size)
    sums = grad_blocks(me, proj, out_grads, rows, spots) + from_core
    late, _ = lax.optimization_barrier((proj_in, sums))
    for k, bit in enumerate(middle):
        half = sums.shape[0] // 2
        sent = swap(sums[half:].astype(jnp.bfloat16), bit, size)
        sums = sums[:half] + sent.astype(jnp.float32)
        if k == 0:
            got, _ = lax.optimization_barrier((got, sums))
    own = sums[0]
    across = swap(own, split, size)

    panel = jnp.concatenate([panel, got], axis=0)
    place = [0, middle[-1]]
    for bit in middle[-2::-1]:
        panel = jnp.concatenate([panel, swap(panel, bit, size)], axis=0)
        place = place + [p ^ bit for p in place]
    panels = [panel, swap(panel, 1, size)]
    place = tuple(place + [p ^ 1 for p in place])

    act = lax.dot_general(
        late, activations, (((0,), (1,)), ((), ())), preferred_element_type=jnp.float32
    )
    act = jnp.stack([act, swap(act, split, size)])
    steps = max(1, 4 * width * size * own_q * rows // (4 * MIB))
    products = inner(act, panels, steps)
    mine, theirs, doc = score(
        me, doc_length, valid_count, own, across, products, split, own_q, steps
    )
    others = swap(theirs, split, size)
    bits = [1] + middle
    for bit in bits[:-1]:
        half = doc.shape[0] // 2
        doc = doc[:half] + swap(doc[half:], bit, size)
    more = swap(doc[1:], bits[-1], size)
    token_scores, doc = last(
        me, doc_length, valid_count, mine, others, doc[:1], more, place, split
    )
    return (token_scores, doc.T)


def solution(mesh):
    size = mesh.shape["seq"]
    placed = (
        P(("groups", "seq"), None),
        P("groups", "seq"),
        P(),
        P("seq", None),
        P("seq", None),
        P("groups"),
        P("groups"),
    )
    return jax.shard_map(
        functools.partial(body, size),
        mesh=mesh,
        in_specs=placed,
        out_specs=(P(("groups", "seq"), None), P("groups", "seq")),
        check_vma=False,
    )
```

```python
import functools

import jax
import jax.numpy as jnp
from jax import lax
from jax.experimental import pallas as pl
from jax.experimental.pallas import tpu as pltpu
from jax.sharding import PartitionSpec as P

MIB = 1 << 20
SMEM = pl.BlockSpec(memory_space=pltpu.SMEM)
VMEM = pl.BlockSpec(memory_space=pltpu.VMEM)
HBM = pl.BlockSpec(memory_space=pltpu.HBM)


def swap(value, offset, size, cores=(0, 1)):
    pairs = [(i, i ^ offset) for i in range(size) if i % 2 in cores]
    return lax.ppermute(value, "seq", pairs)


def grad_kernel(offsets, fresh, me_ref, proj_ref, grads_ref, out_ref, *refs):
    if fresh:
        table, proj_buf, grads_buf, sems, proj_sem = refs
        load = pltpu.make_async_copy(proj_ref, proj_buf, proj_sem)
        load.start()
    else:
        table, (grads_buf, sems) = proj_ref, refs
    halves, total, depth = grads_buf.shape
    count = len(offsets) // halves
    rows = total // count
    copies = []
    for k, offset in enumerate(offsets):
        first = pl.multiple_of((me_ref[0] ^ offset) * rows, rows)
        copy = pltpu.make_async_copy(
            grads_ref.at[pl.ds(first, rows)],
            grads_buf.at[k % halves, pl.ds((k // halves) * rows, rows)],
            sems.at[k],
        )
        copy.start(priority=k % 2)
        copies.append(copy)
    if fresh:
        load.wait()
        turned = proj_buf[...].T
        none = jnp.zeros_like(turned)
        for r in range(halves):
            table[r] = jnp.concatenate([turned if c == r else none for c in range(halves)], axis=1)
    for k in range(0, count, 2):
        for copy in copies[k * halves : (k + 2) * halves]:
            copy.wait()
        made = None
        for r in range(halves):
            part = jnp.dot(
                grads_buf[r, k * rows : (k + 2) * rows],
                table[r],
                preferred_element_type=jnp.float32,
            )
            made = part if made is None else made + part
        out_ref[k] = made[:rows]
        out_ref[k + 1] = made[rows:]


def grad_blocks(me, proj, out_grads, rows, offsets, fresh):
    depth = out_grads.shape[1]
    width = proj.shape[0] if fresh else proj.shape[2] // 2
    count = len(offsets) // 2
    made = jax.ShapeDtypeStruct((count, rows, 2 * width), jnp.float32)
    table = jax.ShapeDtypeStruct((2, depth, 2 * width), jnp.bfloat16)
    scratch = [
        pltpu.VMEM((2, count * rows, depth), jnp.bfloat16),
        pltpu.SemaphoreType.DMA((2 * count,)),
    ]
    if fresh:
        scratch = [pltpu.VMEM((width, depth), jnp.bfloat16)] + scratch + [pltpu.SemaphoreType.DMA]
    return pl.pallas_call(
        functools.partial(grad_kernel, offsets, fresh),
        in_specs=[SMEM, HBM if fresh else VMEM, HBM],
        out_specs=(VMEM, VMEM) if fresh else VMEM,
        out_shape=(made, table) if fresh else made,
        scratch_shapes=scratch,
        compiler_params=pltpu.CompilerParams(vmem_limit_bytes=48 * MIB),
        cost_estimate=pl.CostEstimate(
            flops=4 * count * rows * depth * width,
            bytes_accessed=4 * count * rows * depth,
            transcendentals=0,
        ),
    )(me, proj, out_grads)


def inner_kernel(pieces, act_ref, *refs):
    out_ref = refs[pieces]
    columns = []
    for r in range(act_ref.shape[0]):
        act = act_ref[r]
        high = act.astype(jnp.bfloat16)
        low = (act - high.astype(jnp.float32)).astype(jnp.bfloat16)
        none = jnp.zeros_like(high)
        columns.append(jnp.concatenate([high, none, low, none], axis=0))
        columns.append(jnp.concatenate([none, high, none, low], axis=0))
    table = jnp.concatenate(columns, axis=1)
    pair = 2 * act_ref.shape[1]
    rows = []
    for k in range(refs[0].shape[1] // pair):
        for ref in refs[:pieces]:
            rows.append(ref[:, k * pair : (k + 1) * pair])
    left = jnp.concatenate(rows, axis=0)
    left = jnp.concatenate([left, left], axis=1)
    out_ref[...] = jnp.dot(left, table, preferred_element_type=jnp.float32)


def inner(act, panels, steps):
    halves, width, rows = act.shape
    count = sum(p.shape[0] for p in panels)
    pairs = panels[0].shape[1] // (2 * width)
    total = pairs * count
    if steps == 1:
        grid = {"in_specs": [VMEM] * (1 + len(panels)), "out_specs": VMEM}
    else:
        grid = {
            "grid": (steps,),
            "in_specs": [VMEM]
            + [pl.BlockSpec((p.shape[0], p.shape[1] // steps), lambda s: (0, s)) for p in panels],
            "out_specs": pl.BlockSpec((total // steps, 2 * halves * rows), lambda s: (s, 0)),
        }
    return pl.pallas_call(
        functools.partial(inner_kernel, len(panels)),
        out_shape=jax.ShapeDtypeStruct((total, 2 * halves * rows), jnp.float32),
        compiler_params=pltpu.CompilerParams(vmem_limit_bytes=32 * MIB),
        cost_estimate=pl.CostEstimate(
            flops=16 * total * width * halves * rows,
            bytes_accessed=8 * total * halves * rows,
            transcendentals=0,
        ),
        **grid,
    )(act, *panels)


def score_kernel(
    steps, split, me_ref, length_ref, valid_ref, own_ref, other_ref, inner_ref, own_tok, other_tok, doc_ref, grad_ref
):
    rows, wide = own_ref.shape
    halves, width = 2, wide // 2
    count = own_tok.shape[0]
    pairs = inner_ref.shape[0] // count
    step = pl.program_id(0) if steps > 1 else 0
    tokens = (own_tok, other_tok)

    def begin():
        other = other_ref[...].T
        grad_ref[...] = own_ref[...].T + jnp.concatenate([other[width:], other[:width]], axis=0)

    if steps == 1:
        begin()
    else:
        pl.when(step == 0)(begin)

    for r in range(halves):
        total = None
        for k in range(pairs):
            for parity in range(2):
                feature = 2 * k + parity
                if steps == 1:
                    line = grad_ref[r * width + feature : r * width + feature + 1]
                else:
                    line = grad_ref[pl.ds(r * width + 2 * pairs * step + feature, 1)]
                column = (2 * r + parity) * rows
                term = line * inner_ref[k * count : (k + 1) * count, column : column + rows]
                total = term if total is None else total + term
        if steps == 1:
            tokens[r][...] = total
        else:
            tokens[r][...] = jnp.where(step == 0, total, tokens[r][...] + total)

    def finish():
        me = me_ref[0]
        docs = length_ref.shape[0]
        doc_of = lax.broadcasted_iota(jnp.int32, (docs, rows), 0)
        lower = jnp.zeros((docs, rows), jnp.int32)
        upper = jnp.zeros((docs, rows), jnp.int32)
        start = jnp.int32(0)
        for d in range(docs):
            lower = jnp.where(doc_of == d, start, lower)
            used = jnp.minimum(valid_ref[d], length_ref[d])
            upper = jnp.where(doc_of == d, start + used, upper)
            start = start + length_ref[d]
        members, parts = [], []
        for r in range(halves):
            token = (me ^ (split * r)) * rows + lax.broadcasted_iota(jnp.int32, (docs, rows), 1)
            inside = (token >= lower) & (token < upper)
            members.append(jnp.where(inside, 1.0, 0.0).astype(jnp.bfloat16))
            left = tokens[r][...]
            for _ in range(3):
                part = left.astype(jnp.bfloat16)
                left = left - part.astype(jnp.float32)
                parts.append(part)
        partial = lax.dot_general(
            jnp.concatenate(parts, axis=1),
            jnp.concatenate([m for m in members for _ in range(3)], axis=1),
            (((1,), (1,)), ((), ())),
            preferred_element_type=jnp.float32,
        )
        own_q = doc_ref.shape[1]
        for k in range(doc_ref.shape[0]):
            doc_ref[k] = partial[k * own_q : (k + 1) * own_q]

    if steps == 1:
        finish()
    else:
        pl.when(step == steps - 1)(finish)


def score(me, lengths, valid, own, other, products, split, own_q, steps):
    rows, wide = own.shape
    docs = lengths.shape[0]
    count = 4 * products.shape[0] // wide
    if steps == 1:
        grid = {"in_specs": [SMEM] * 3 + [VMEM] * 3, "out_specs": (VMEM,) * 3}
    else:
        block = (products.shape[0] // steps, products.shape[1])
        grid = {
            "grid": (steps,),
            "in_specs": [SMEM] * 3 + [VMEM] * 2 + [pl.BlockSpec(block, lambda s: (s, 0))],
            "out_specs": (VMEM,) * 3,
        }
    return pl.pallas_call(
        functools.partial(score_kernel, steps, split),
        out_shape=(
            jax.ShapeDtypeStruct((count, rows), jnp.float32),
            jax.ShapeDtypeStruct((count, rows), jnp.float32),
            jax.ShapeDtypeStruct((count // own_q, own_q, docs), jnp.float32),
        ),
        scratch_shapes=[pltpu.VMEM((wide, rows), jnp.float32)],
        compiler_params=pltpu.CompilerParams(vmem_limit_bytes=32 * MIB),
        cost_estimate=pl.CostEstimate(
            flops=2 * products.shape[0] * products.shape[1],
            bytes_accessed=4 * products.shape[0] * products.shape[1],
            transcendentals=0,
        ),
        **grid,
    )(me, lengths, valid, own, other, products)


def last_kernel(
    place, split, me_ref, length_ref, valid_ref, own_ref, other_ref, doc_ref, more_ref, token_out, doc_out, turned_ref
):
    own_q, docs = doc_out.shape
    for r, ref in enumerate((own_ref, other_ref)):
        for k, offset in enumerate(place):
            spot = pl.multiple_of((me_ref[0] ^ (offset + split * r)) * own_q, own_q)
            turned_ref[pl.ds(spot, own_q)] = ref[k * own_q : (k + 1) * own_q]
    token_out[...] = turned_ref[...].T
    doc_of = lax.broadcasted_iota(jnp.int32, (own_q, docs), 1)
    used = jnp.zeros((own_q, docs), jnp.int32)
    for d in range(docs):
        used = jnp.where(doc_of == d, jnp.minimum(valid_ref[d], length_ref[d]), used)
    doc = jnp.where(me_ref[0] % 2 == 1, doc_ref[0], more_ref[0])
    doc_out[...] = doc * (1.0 / jnp.sqrt(used.astype(jnp.float32)))


def last(me, lengths, valid, own, other, doc, more, place, split):
    count, rows = own.shape
    _, own_q, docs = doc.shape
    return pl.pallas_call(
        functools.partial(last_kernel, place, split),
        in_specs=[SMEM] * 3 + [VMEM] * 4,
        out_specs=(VMEM, VMEM),
        out_shape=(
            jax.ShapeDtypeStruct((rows, 2 * count), jnp.float32),
            jax.ShapeDtypeStruct((own_q, docs), jnp.float32),
        ),
        scratch_shapes=[pltpu.VMEM((2 * count, rows), jnp.float32)],
        compiler_params=pltpu.CompilerParams(vmem_limit_bytes=16 * MIB),
    )(me, lengths, valid, own, other, doc, more)


def offset_of(number, bits):
    last_bit = len(bits) - 1
    return sum(bit for k, bit in enumerate(bits) if (number >> (last_bit - k)) & 1)


def body(size, activations, out_grads, proj_in, proj_out, queries, doc_length, valid_count):
    rows = activations.shape[0]
    width = proj_in.shape[1]
    own_q = queries.shape[0]
    me = lax.axis_index("seq").astype(jnp.int32)[None]
    split = size // 4
    middle = [1 << k for k in range(1, size.bit_length() - 1) if 1 << k != split]

    proj = pltpu.with_memory_space_constraint(proj_out.T, pltpu.HBM)
    spots = [offset_of(m, middle) + split * r for m in range(size // 4) for r in range(2)]
    theirs, table = grad_blocks(me, proj, out_grads, rows, [s + 1 for s in spots], True)
    from_core = swap(theirs, 1, size)
    panel, _ = lax.optimization_barrier((queries, theirs))
    got = swap(panel, middle[-1], size)
    sums = grad_blocks(me, table, out_grads, rows, spots, False) + from_core
    late, _ = lax.optimization_barrier((proj_in, sums))
    for k, bit in enumerate(middle):
        half = sums.shape[0] // 2
        sent = swap(sums[half:].astype(jnp.bfloat16), bit, size)
        sums = sums[:half] + sent.astype(jnp.float32)
        if k == 0:
            got, _ = lax.optimization_barrier((got, sums))
    own = sums[0]
    across = swap(own, split, size)

    panel = jnp.concatenate([panel, got], axis=0)
    place = [0, middle[-1]]
    for bit in middle[-2::-1]:
        panel = jnp.concatenate([panel, swap(panel, bit, size)], axis=0)
        place = place + [p ^ bit for p in place]
    panels = [panel, swap(panel, 1, size)]
    place = tuple(place + [p ^ 1 for p in place])

    act = lax.dot_general(
        late, activations, (((0,), (1,)), ((), ())), preferred_element_type=jnp.float32
    )
    act = jnp.stack([act, swap(act, split, size)])
    steps = max(1, 4 * width * size * own_q * rows // (4 * MIB))
    products = inner(act, panels, steps)
    mine, theirs, doc = score(
        me, doc_length, valid_count, own, across, products, split, own_q, steps
    )
    others = swap(theirs, split, size)
    half = doc.shape[0] // 2
    from_even = swap(doc, 1, size, (0,))
    doc = doc + jnp.concatenate([from_even[half:], from_even[:half]], axis=0)
    doc = doc.reshape((2, half) + doc.shape[1:])
    for bit in middle:
        half //= 2
        doc = doc[:, :half] + swap(doc[:, half:], bit, size, (1,))
    own_doc, even_doc = doc[0], doc[1]
    from_odd = swap(even_doc, 1, size, (1,))
    token_scores, doc = last(
        me, doc_length, valid_count, mine, others, own_doc, from_odd, place, split
    )
    return (token_scores, doc.T)


def solution(mesh):
    size = mesh.shape["seq"]
    placed = (
        P(("groups", "seq"), None),
        P("groups", "seq"),
        P(),
        P("seq", None),
        P("seq", None),
        P("groups"),
        P("groups"),
    )
    return jax.shard_map(
        functools.partial(body, size),
        mesh=mesh,
        in_specs=placed,
        out_specs=(P(("groups", "seq"), None), P("groups", "seq")),
        check_vma=False,
    )
```

```python
import functools

import jax
import jax.numpy as jnp
from jax import lax
from jax.experimental import pallas as pl
from jax.experimental.pallas import tpu as pltpu
from jax.sharding import PartitionSpec as P

MIB = 1 << 20
SMEM = pl.BlockSpec(memory_space=pltpu.SMEM)
VMEM = pl.BlockSpec(memory_space=pltpu.VMEM)


def swap(value, offset, size):
    return lax.ppermute(value, "seq", [(i, i ^ offset) for i in range(size)])


def grad_kernel(offsets, fresh, me_ref, proj_ref, grads_ref, out_ref, *refs):
    table = refs[0] if fresh else proj_ref
    halves = table.shape[0]
    count, rows, _ = out_ref.shape
    if fresh:
        turned = proj_ref[...].T
        none = jnp.zeros_like(turned)
        for r in range(halves):
            table[r] = jnp.concatenate([turned if c == r else none for c in range(halves)], axis=1)
    for k in range(0, count, 2):
        made = None
        for r in range(halves):
            left = []
            for offset in (offsets[k * halves + r], offsets[(k + 1) * halves + r]):
                first = pl.multiple_of((me_ref[0] ^ offset) * rows, rows)
                left.append(grads_ref[pl.ds(first, rows)])
            part = jnp.dot(
                jnp.concatenate(left, axis=0), table[r], preferred_element_type=jnp.float32
            )
            made = part if made is None else made + part
        out_ref[k] = made[:rows]
        out_ref[k + 1] = made[rows:]


def grad_blocks(me, proj, out_grads, rows, offsets, fresh):
    depth = out_grads.shape[1]
    width = proj.shape[0] if fresh else proj.shape[2] // 2
    count = len(offsets) // 2
    made = jax.ShapeDtypeStruct((count, rows, 2 * width), jnp.float32)
    table = jax.ShapeDtypeStruct((2, depth, 2 * width), jnp.bfloat16)
    held = jax.ShapeDtypeStruct(out_grads.shape, out_grads.dtype)
    return pl.pallas_call(
        functools.partial(grad_kernel, offsets, fresh),
        in_specs=[SMEM, VMEM, VMEM],
        out_specs=(VMEM,) * 3 if fresh else VMEM,
        out_shape=(made, table, held) if fresh else made,
        input_output_aliases={2: 2} if fresh else {},
        compiler_params=pltpu.CompilerParams(vmem_limit_bytes=24 * MIB),
        cost_estimate=pl.CostEstimate(
            flops=4 * count * rows * depth * width,
            bytes_accessed=4 * count * rows * depth,
            transcendentals=0,
        ),
    )(me, proj, out_grads)


def inner_kernel(pieces, act_ref, *refs):
    out_ref = refs[pieces]
    columns = []
    for r in range(act_ref.shape[0]):
        act = act_ref[r]
        high = act.astype(jnp.bfloat16)
        low = (act - high.astype(jnp.float32)).astype(jnp.bfloat16)
        none = jnp.zeros_like(high)
        columns.append(jnp.concatenate([high, none, low, none], axis=0))
        columns.append(jnp.concatenate([none, high, none, low], axis=0))
    table = jnp.concatenate(columns, axis=1)
    pair = 2 * act_ref.shape[1]
    rows = []
    for k in range(refs[0].shape[1] // pair):
        for ref in refs[:pieces]:
            rows.append(ref[:, k * pair : (k + 1) * pair])
    left = jnp.concatenate(rows, axis=0)
    left = jnp.concatenate([left, left], axis=1)
    out_ref[...] = jnp.dot(left, table, preferred_element_type=jnp.float32)


def inner(act, panels, steps):
    halves, width, rows = act.shape
    count = sum(p.shape[0] for p in panels)
    pairs = panels[0].shape[1] // (2 * width)
    total = pairs * count
    if steps == 1:
        grid = {"in_specs": [VMEM] * (1 + len(panels)), "out_specs": VMEM}
    else:
        grid = {
            "grid": (steps,),
            "in_specs": [VMEM]
            + [pl.BlockSpec((p.shape[0], p.shape[1] // steps), lambda s: (0, s)) for p in panels],
            "out_specs": pl.BlockSpec((total // steps, 2 * halves * rows), lambda s: (s, 0)),
        }
    return pl.pallas_call(
        functools.partial(inner_kernel, len(panels)),
        out_shape=jax.ShapeDtypeStruct((total, 2 * halves * rows), jnp.float32),
        compiler_params=pltpu.CompilerParams(vmem_limit_bytes=32 * MIB),
        cost_estimate=pl.CostEstimate(
            flops=16 * total * width * halves * rows,
            bytes_accessed=8 * total * halves * rows,
            transcendentals=0,
        ),
        **grid,
    )(act, *panels)


def score_kernel(
    steps, split, me_ref, length_ref, valid_ref, own_ref, other_ref, inner_ref, own_tok, other_tok, doc_ref, grad_ref
):
    rows, wide = own_ref.shape
    halves, width = 2, wide // 2
    count = own_tok.shape[0]
    pairs = inner_ref.shape[0] // count
    step = pl.program_id(0) if steps > 1 else 0
    tokens = (own_tok, other_tok)

    def begin():
        other = other_ref[...].T
        grad_ref[...] = own_ref[...].T + jnp.concatenate([other[width:], other[:width]], axis=0)

    if steps == 1:
        begin()
    else:
        pl.when(step == 0)(begin)

    for r in range(halves):
        total = None
        for k in range(pairs):
            for parity in range(2):
                feature = 2 * k + parity
                if steps == 1:
                    line = grad_ref[r * width + feature : r * width + feature + 1]
                else:
                    line = grad_ref[pl.ds(r * width + 2 * pairs * step + feature, 1)]
                column = (2 * r + parity) * rows
                term = line * inner_ref[k * count : (k + 1) * count, column : column + rows]
                total = term if total is None else total + term
        if steps == 1:
            tokens[r][...] = total
        else:
            tokens[r][...] = jnp.where(step == 0, total, tokens[r][...] + total)

    def finish():
        me = me_ref[0]
        docs = length_ref.shape[0]
        doc_of = lax.broadcasted_iota(jnp.int32, (docs, rows), 0)
        lower = jnp.zeros((docs, rows), jnp.int32)
        upper = jnp.zeros((docs, rows), jnp.int32)
        start = jnp.int32(0)
        for d in range(docs):
            lower = jnp.where(doc_of == d, start, lower)
            used = jnp.minimum(valid_ref[d], length_ref[d])
            upper = jnp.where(doc_of == d, start + used, upper)
            start = start + length_ref[d]
        members, parts = [], []
        for r in range(halves):
            token = (me ^ (split * r)) * rows + lax.broadcasted_iota(jnp.int32, (docs, rows), 1)
            inside = (token >= lower) & (token < upper)
            members.append(jnp.where(inside, 1.0, 0.0).astype(jnp.bfloat16))
            left = tokens[r][...]
            for _ in range(3):
                part = left.astype(jnp.bfloat16)
                left = left - part.astype(jnp.float32)
                parts.append(part)
        partial = lax.dot_general(
            jnp.concatenate(parts, axis=1),
            jnp.concatenate([m for m in members for _ in range(3)], axis=1),
            (((1,), (1,)), ((), ())),
            preferred_element_type=jnp.float32,
        )
        own_q = doc_ref.shape[1]
        for k in range(doc_ref.shape[0]):
            doc_ref[k] = partial[k * own_q : (k + 1) * own_q]

    if steps == 1:
        finish()
    else:
        pl.when(step == steps - 1)(finish)


def score(me, lengths, valid, own, other, products, split, own_q, steps):
    rows, wide = own.shape
    docs = lengths.shape[0]
    count = 4 * products.shape[0] // wide
    if steps == 1:
        grid = {"in_specs": [SMEM] * 3 + [VMEM] * 3, "out_specs": (VMEM,) * 3}
    else:
        block = (products.shape[0] // steps, products.shape[1])
        grid = {
            "grid": (steps,),
            "in_specs": [SMEM] * 3 + [VMEM] * 2 + [pl.BlockSpec(block, lambda s: (s, 0))],
            "out_specs": (VMEM,) * 3,
        }
    return pl.pallas_call(
        functools.partial(score_kernel, steps, split),
        out_shape=(
            jax.ShapeDtypeStruct((count, rows), jnp.float32),
            jax.ShapeDtypeStruct((count, rows), jnp.float32),
            jax.ShapeDtypeStruct((count // own_q, own_q, docs), jnp.float32),
        ),
        scratch_shapes=[pltpu.VMEM((wide, rows), jnp.float32)],
        compiler_params=pltpu.CompilerParams(vmem_limit_bytes=32 * MIB),
        cost_estimate=pl.CostEstimate(
            flops=2 * products.shape[0] * products.shape[1],
            bytes_accessed=4 * products.shape[0] * products.shape[1],
            transcendentals=0,
        ),
        **grid,
    )(me, lengths, valid, own, other, products)


def last_kernel(
    place, split, me_ref, length_ref, valid_ref, own_ref, other_ref, doc_ref, more_ref, token_out, doc_out, turned_ref
):
    own_q, docs = doc_out.shape
    for r, ref in enumerate((own_ref, other_ref)):
        for k, offset in enumerate(place):
            spot = pl.multiple_of((me_ref[0] ^ (offset + split * r)) * own_q, own_q)
            turned_ref[pl.ds(spot, own_q)] = ref[k * own_q : (k + 1) * own_q]
    token_out[...] = turned_ref[...].T
    doc_of = lax.broadcasted_iota(jnp.int32, (own_q, docs), 1)
    used = jnp.zeros((own_q, docs), jnp.int32)
    for d in range(docs):
        used = jnp.where(doc_of == d, jnp.minimum(valid_ref[d], length_ref[d]), used)
    doc_out[...] = (doc_ref[0] + more_ref[0]) * (1.0 / jnp.sqrt(used.astype(jnp.float32)))


def last(me, lengths, valid, own, other, doc, more, place, split):
    count, rows = own.shape
    _, own_q, docs = doc.shape
    return pl.pallas_call(
        functools.partial(last_kernel, place, split),
        in_specs=[SMEM] * 3 + [VMEM] * 4,
        out_specs=(VMEM, VMEM),
        out_shape=(
            jax.ShapeDtypeStruct((rows, 2 * count), jnp.float32),
            jax.ShapeDtypeStruct((own_q, docs), jnp.float32),
        ),
        scratch_shapes=[pltpu.VMEM((2 * count, rows), jnp.float32)],
        compiler_params=pltpu.CompilerParams(vmem_limit_bytes=16 * MIB),
    )(me, lengths, valid, own, other, doc, more)


def offset_of(number, bits):
    last_bit = len(bits) - 1
    return sum(bit for k, bit in enumerate(bits) if (number >> (last_bit - k)) & 1)


def body(size, activations, out_grads, proj_in, proj_out, queries, doc_length, valid_count):
    rows = activations.shape[0]
    width = proj_in.shape[1]
    own_q = queries.shape[0]
    me = lax.axis_index("seq").astype(jnp.int32)[None]
    split = size // 4
    middle = [1 << k for k in range(1, size.bit_length() - 1) if 1 << k != split]

    proj = proj_out.T
    spots = [offset_of(m, middle) + split * r for m in range(size // 4) for r in range(2)]
    theirs, table, held = grad_blocks(me, proj, out_grads, rows, [s + 1 for s in spots], True)
    from_core = swap(theirs, 1, size)
    panel = queries
    got = swap(panel, middle[-1], size)
    sums = grad_blocks(me, table, held, rows, spots, False) + from_core
    late, _ = lax.optimization_barrier((proj_in, sums))
    for k, bit in enumerate(middle):
        half = sums.shape[0] // 2
        sent = swap(sums[half:].astype(jnp.bfloat16), bit, size)
        sums = sums[:half] + sent.astype(jnp.float32)
        if k == 0:
            got, _ = lax.optimization_barrier((got, sums))
    own = sums[0]
    across = swap(own, split, size)

    panel = jnp.concatenate([panel, got], axis=0)
    place = [0, middle[-1]]
    for bit in middle[-2::-1]:
        panel = jnp.concatenate([panel, swap(panel, bit, size)], axis=0)
        place = place + [p ^ bit for p in place]
    panels = [panel, swap(panel, 1, size)]
    place = tuple(place + [p ^ 1 for p in place])

    act = lax.dot_general(
        late, activations, (((0,), (1,)), ((), ())), preferred_element_type=jnp.float32
    )
    act = jnp.stack([act, swap(act, split, size)])
    steps = max(1, 4 * width * size * own_q * rows // (4 * MIB))
    products = inner(act, panels, steps)
    mine, theirs, doc = score(
        me, doc_length, valid_count, own, across, products, split, own_q, steps
    )
    others = swap(theirs, split, size)
    bits = [1] + middle
    for bit in bits[:-1]:
        half = doc.shape[0] // 2
        doc = doc[:half] + swap(doc[half:], bit, size)
    more = swap(doc[1:], bits[-1], size)
    token_scores, doc = last(
        me, doc_length, valid_count, mine, others, doc[:1], more, place, split
    )
    return (token_scores, doc.T)


def solution(mesh):
    size = mesh.shape["seq"]
    placed = (
        P(("groups", "seq"), None),
        P("groups", "seq"),
        P(),
        P("seq", None),
        P("seq", None),
        P("groups"),
        P("groups"),
    )
    return jax.shard_map(
        functools.partial(body, size),
        mesh=mesh,
        in_specs=placed,
        out_specs=(P(("groups", "seq"), None), P("groups", "seq")),
        check_vma=False,
    )
```

```python
import functools

import jax
import jax.numpy as jnp
from jax import lax
from jax.experimental import pallas as pl
from jax.experimental.pallas import tpu as pltpu
from jax.sharding import PartitionSpec as P

MIB = 1 << 20
SMEM = pl.BlockSpec(memory_space=pltpu.SMEM)
VMEM = pl.BlockSpec(memory_space=pltpu.VMEM)
HBM = pl.BlockSpec(memory_space=pltpu.HBM)


def swap(value, offset, size):
    return lax.ppermute(value, "seq", [(i, i ^ offset) for i in range(size)])


def grad_kernel(offsets, fresh, me_ref, proj_ref, grads_ref, out_ref, *refs):
    if fresh:
        table, proj_buf, grads_buf, sems, proj_sem = refs
        load = pltpu.make_async_copy(proj_ref, proj_buf, proj_sem)
        load.start()
    else:
        table, (grads_buf, sems) = proj_ref, refs
    halves, total, depth = grads_buf.shape
    count = len(offsets) // halves
    rows = total // count
    copies = []
    for k, offset in enumerate(offsets):
        first = pl.multiple_of((me_ref[0] ^ offset) * rows, rows)
        copy = pltpu.make_async_copy(
            grads_ref.at[pl.ds(first, rows)],
            grads_buf.at[k % halves, pl.ds((k // halves) * rows, rows)],
            sems.at[k],
        )
        copy.start(priority=k % 2)
        copies.append(copy)
    if fresh:
        load.wait()
        turned = proj_buf[...].T
        none = jnp.zeros_like(turned)
        for r in range(halves):
            table[r] = jnp.concatenate([turned if c == r else none for c in range(halves)], axis=1)
    for k in range(0, count, 2):
        for copy in copies[k * halves : (k + 2) * halves]:
            copy.wait()
        made = None
        for r in range(halves):
            part = jnp.dot(
                grads_buf[r, k * rows : (k + 2) * rows],
                table[r],
                preferred_element_type=jnp.float32,
            )
            made = part if made is None else made + part
        out_ref[k] = made[:rows]
        out_ref[k + 1] = made[rows:]


def paired_kernel(offsets, fresh, me_ref, proj_ref, grads_ref, out_ref, *refs):
    if fresh:
        table, proj_buf, grads_buf, sems, proj_sem = refs
        load = pltpu.make_async_copy(proj_ref, proj_buf, proj_sem)
        load.start()
    else:
        table, (grads_buf, sems) = proj_ref, refs
    halves, total, pairs, _, lanes = grads_buf.shape
    count, rows, wide = out_ref.shape
    groups = rows // 8
    copies = []
    for k, offset in enumerate(offsets):
        first = pl.multiple_of((me_ref[0] ^ offset) * groups, groups)
        copy = pltpu.make_async_copy(
            grads_ref.at[pl.ds(first, groups)],
            grads_buf.at[k % halves, pl.ds((k // halves) * groups, groups)],
            sems.at[k],
        )
        copy.start(priority=k % 2)
        copies.append(copy)
    if fresh:
        load.wait()
        turned = proj_buf[...].T
        for p in range(pairs):
            one = turned[2 * p * lanes : (2 * p + 1) * lanes]
            two = turned[(2 * p + 1) * lanes : (2 * p + 2) * lanes]
            table[0, p * lanes : (p + 1) * lanes] = jnp.concatenate([one, two], axis=1)
            table[1, p * lanes : (p + 1) * lanes] = jnp.concatenate([two, one], axis=1)
    lane = lax.broadcasted_iota(jnp.int32, (2 * rows, wide), 1)
    for k in range(0, count, 2):
        for copy in copies[k * halves : (k + 2) * halves]:
            copy.wait()
        sums = []
        for r in range(halves):
            left = [
                grads_buf[r, k * groups : (k + 2) * groups, p].reshape(4 * rows, lanes)
                for p in range(pairs)
            ]
            made = jnp.dot(
                jnp.concatenate(left, axis=1), table[r], preferred_element_type=jnp.float32
            ).reshape(2 * groups, 2, 8, wide)
            one = made[:, 0].reshape(2 * rows, wide)
            two = made[:, 1].reshape(2 * rows, wide)
            sums.append(one + pltpu.roll(two, wide // 2, 1))
        both = jnp.where(lane < wide // 2, sums[0], sums[1])
        out_ref[k] = both[:rows]
        out_ref[k + 1] = both[rows:]


def grad_blocks(me, proj, out_grads, rows, offsets, fresh):
    tokens, depth = out_grads.shape
    width = proj.shape[0] if fresh else proj.shape[2] // 2
    count = len(offsets) // 2
    made = jax.ShapeDtypeStruct((count, rows, 2 * width), jnp.float32)
    if depth % 256 == 0 and rows % 8 == 0 and width == 64:
        kernel, deep = paired_kernel, depth // 2
        held = (2, count * rows // 8, depth // 256, 16, 128)
        tiles = out_grads.reshape(tokens // 8, 8, depth // 128, 128).transpose(0, 2, 1, 3)
        out_grads = tiles.reshape(tokens // 8, depth // 256, 16, 128)
    else:
        kernel, deep = grad_kernel, depth
        held = (2, count * rows, depth)
    table = jax.ShapeDtypeStruct((2, deep, 2 * width), jnp.bfloat16)
    scratch = [pltpu.VMEM(held, jnp.bfloat16), pltpu.SemaphoreType.DMA((2 * count,))]
    if fresh:
        scratch = [pltpu.VMEM((width, depth), jnp.bfloat16)] + scratch + [pltpu.SemaphoreType.DMA]
    return pl.pallas_call(
        functools.partial(kernel, offsets, fresh),
        in_specs=[SMEM, HBM if fresh else VMEM, HBM],
        out_specs=(VMEM, VMEM) if fresh else VMEM,
        out_shape=(made, table) if fresh else made,
        scratch_shapes=scratch,
        compiler_params=pltpu.CompilerParams(vmem_limit_bytes=48 * MIB),
        cost_estimate=pl.CostEstimate(
            flops=4 * count * rows * depth * width,
            bytes_accessed=4 * count * rows * depth,
            transcendentals=0,
        ),
    )(me, proj, pltpu.with_memory_space_constraint(out_grads, pltpu.HBM))


def inner_kernel(pieces, act_ref, *refs):
    out_ref = refs[pieces]
    columns = []
    for r in range(act_ref.shape[0]):
        act = act_ref[r]
        high = act.astype(jnp.bfloat16)
        low = (act - high.astype(jnp.float32)).astype(jnp.bfloat16)
        none = jnp.zeros_like(high)
        columns.append(jnp.concatenate([high, none, low, none], axis=0))
        columns.append(jnp.concatenate([none, high, none, low], axis=0))
    table = jnp.concatenate(columns, axis=1)
    pair = 2 * act_ref.shape[1]
    rows = []
    for k in range(refs[0].shape[1] // pair):
        for ref in refs[:pieces]:
            rows.append(ref[:, k * pair : (k + 1) * pair])
    left = jnp.concatenate(rows, axis=0)
    left = jnp.concatenate([left, left], axis=1)
    out_ref[...] = jnp.dot(left, table, preferred_element_type=jnp.float32)


def inner(act, panels, steps):
    halves, width, rows = act.shape
    count = sum(p.shape[0] for p in panels)
    pairs = panels[0].shape[1] // (2 * width)
    total = pairs * count
    if steps == 1:
        grid = {"in_specs": [VMEM] * (1 + len(panels)), "out_specs": VMEM}
    else:
        grid = {
            "grid": (steps,),
            "in_specs": [VMEM]
            + [pl.BlockSpec((p.shape[0], p.shape[1] // steps), lambda s: (0, s)) for p in panels],
            "out_specs": pl.BlockSpec((total // steps, 2 * halves * rows), lambda s: (s, 0)),
        }
    return pl.pallas_call(
        functools.partial(inner_kernel, len(panels)),
        out_shape=jax.ShapeDtypeStruct((total, 2 * halves * rows), jnp.float32),
        compiler_params=pltpu.CompilerParams(vmem_limit_bytes=32 * MIB),
        cost_estimate=pl.CostEstimate(
            flops=16 * total * width * halves * rows,
            bytes_accessed=8 * total * halves * rows,
            transcendentals=0,
        ),
        **grid,
    )(act, *panels)


def score_kernel(
    steps, split, me_ref, length_ref, valid_ref, own_ref, other_ref, inner_ref, own_tok, other_tok, doc_ref, grad_ref
):
    rows, wide = own_ref.shape
    halves, width = 2, wide // 2
    count = own_tok.shape[0]
    pairs = inner_ref.shape[0] // count
    step = pl.program_id(0) if steps > 1 else 0
    tokens = (own_tok, other_tok)

    def begin():
        other = other_ref[...].T
        grad_ref[...] = own_ref[...].T + jnp.concatenate([other[width:], other[:width]], axis=0)

    if steps == 1:
        begin()
    else:
        pl.when(step == 0)(begin)

    for r in range(halves):
        total = None
        for k in range(pairs):
            for parity in range(2):
                feature = 2 * k + parity
                if steps == 1:
                    line = grad_ref[r * width + feature : r * width + feature + 1]
                else:
                    line = grad_ref[pl.ds(r * width + 2 * pairs * step + feature, 1)]
                column = (2 * r + parity) * rows
                term = line * inner_ref[k * count : (k + 1) * count, column : column + rows]
                total = term if total is None else total + term
        if steps == 1:
            tokens[r][...] = total
        else:
            tokens[r][...] = jnp.where(step == 0, total, tokens[r][...] + total)

    def finish():
        me = me_ref[0]
        docs = length_ref.shape[0]
        doc_of = lax.broadcasted_iota(jnp.int32, (docs, rows), 0)
        lower = jnp.zeros((docs, rows), jnp.int32)
        upper = jnp.zeros((docs, rows), jnp.int32)
        start = jnp.int32(0)
        for d in range(docs):
            lower = jnp.where(doc_of == d, start, lower)
            used = jnp.minimum(valid_ref[d], length_ref[d])
            upper = jnp.where(doc_of == d, start + used, upper)
            start = start + length_ref[d]
        members, parts = [], []
        for r in range(halves):
            token = (me ^ (split * r)) * rows + lax.broadcasted_iota(jnp.int32, (docs, rows), 1)
            inside = (token >= lower) & (token < upper)
            members.append(jnp.where(inside, 1.0, 0.0).astype(jnp.bfloat16))
            left = tokens[r][...]
            for _ in range(3):
                part = left.astype(jnp.bfloat16)
                left = left - part.astype(jnp.float32)
                parts.append(part)
        partial = lax.dot_general(
            jnp.concatenate(parts, axis=1),
            jnp.concatenate([m for m in members for _ in range(3)], axis=1),
            (((1,), (1,)), ((), ())),
            preferred_element_type=jnp.float32,
        )
        own_q = doc_ref.shape[1]
        for k in range(doc_ref.shape[0]):
            doc_ref[k] = partial[k * own_q : (k + 1) * own_q]

    if steps == 1:
        finish()
    else:
        pl.when(step == steps - 1)(finish)


def score(me, lengths, valid, own, other, products, split, own_q, steps):
    rows, wide = own.shape
    docs = lengths.shape[0]
    count = 4 * products.shape[0] // wide
    if steps == 1:
        grid = {"in_specs": [SMEM] * 3 + [VMEM] * 3, "out_specs": (VMEM,) * 3}
    else:
        block = (products.shape[0] // steps, products.shape[1])
        grid = {
            "grid": (steps,),
            "in_specs": [SMEM] * 3 + [VMEM] * 2 + [pl.BlockSpec(block, lambda s: (s, 0))],
            "out_specs": (VMEM,) * 3,
        }
    return pl.pallas_call(
        functools.partial(score_kernel, steps, split),
        out_shape=(
            jax.ShapeDtypeStruct((count, rows), jnp.float32),
            jax.ShapeDtypeStruct((count, rows), jnp.float32),
            jax.ShapeDtypeStruct((count // own_q, own_q, docs), jnp.float32),
        ),
        scratch_shapes=[pltpu.VMEM((wide, rows), jnp.float32)],
        compiler_params=pltpu.CompilerParams(vmem_limit_bytes=32 * MIB),
        cost_estimate=pl.CostEstimate(
            flops=2 * products.shape[0] * products.shape[1],
            bytes_accessed=4 * products.shape[0] * products.shape[1],
            transcendentals=0,
        ),
        **grid,
    )(me, lengths, valid, own, other, products)


def last_kernel(
    place, split, me_ref, length_ref, valid_ref, own_ref, other_ref, doc_ref, more_ref, token_out, doc_out, turned_ref
):
    own_q, docs = doc_out.shape
    for r, ref in enumerate((own_ref, other_ref)):
        for k, offset in enumerate(place):
            spot = pl.multiple_of((me_ref[0] ^ (offset + split * r)) * own_q, own_q)
            turned_ref[pl.ds(spot, own_q)] = ref[k * own_q : (k + 1) * own_q]
    token_out[...] = turned_ref[...].T
    doc_of = lax.broadcasted_iota(jnp.int32, (own_q, docs), 1)
    used = jnp.zeros((own_q, docs), jnp.int32)
    for d in range(docs):
        used = jnp.where(doc_of == d, jnp.minimum(valid_ref[d], length_ref[d]), used)
    doc_out[...] = (doc_ref[0] + more_ref[0]) * (1.0 / jnp.sqrt(used.astype(jnp.float32)))


def last(me, lengths, valid, own, other, doc, more, place, split):
    count, rows = own.shape
    _, own_q, docs = doc.shape
    return pl.pallas_call(
        functools.partial(last_kernel, place, split),
        in_specs=[SMEM] * 3 + [VMEM] * 4,
        out_specs=(VMEM, VMEM),
        out_shape=(
            jax.ShapeDtypeStruct((rows, 2 * count), jnp.float32),
            jax.ShapeDtypeStruct((own_q, docs), jnp.float32),
        ),
        scratch_shapes=[pltpu.VMEM((2 * count, rows), jnp.float32)],
        compiler_params=pltpu.CompilerParams(vmem_limit_bytes=16 * MIB),
    )(me, lengths, valid, own, other, doc, more)


def offset_of(number, bits):
    last_bit = len(bits) - 1
    return sum(bit for k, bit in enumerate(bits) if (number >> (last_bit - k)) & 1)


def body(size, activations, out_grads, proj_in, proj_out, queries, doc_length, valid_count):
    rows = activations.shape[0]
    width = proj_in.shape[1]
    own_q = queries.shape[0]
    me = lax.axis_index("seq").astype(jnp.int32)[None]
    split = size // 4
    middle = [1 << k for k in range(1, size.bit_length() - 1) if 1 << k != split]

    proj = pltpu.with_memory_space_constraint(proj_out.T, pltpu.HBM)
    spots = [offset_of(m, middle) + split * r for m in range(size // 4) for r in range(2)]
    theirs, table = grad_blocks(me, proj, out_grads, rows, [s + 1 for s in spots], True)
    from_core = swap(theirs, 1, size)
    panel = queries
    got = swap(panel, middle[-1], size)
    sums = grad_blocks(me, table, out_grads, rows, spots, False) + from_core
    late, _ = lax.optimization_barrier((proj_in, sums))
    for k, bit in enumerate(middle):
        half = sums.shape[0] // 2
        sent = swap(sums[half:].astype(jnp.bfloat16), bit, size)
        sums = sums[:half] + sent.astype(jnp.float32)
        if k == 0:
            got, _ = lax.optimization_barrier((got, sums))
    own = sums[0]
    across = swap(own, split, size)

    panel = jnp.concatenate([panel, got], axis=0)
    place = [0, middle[-1]]
    for bit in middle[-2::-1]:
        panel = jnp.concatenate([panel, swap(panel, bit, size)], axis=0)
        place = place + [p ^ bit for p in place]
    panels = [panel, swap(panel, 1, size)]
    place = tuple(place + [p ^ 1 for p in place])

    act = lax.dot_general(
        late, activations, (((0,), (1,)), ((), ())), preferred_element_type=jnp.float32
    )
    act = jnp.stack([act, swap(act, split, size)])
    steps = max(1, 4 * width * size * own_q * rows // (4 * MIB))
    products = inner(act, panels, steps)
    mine, theirs, doc = score(
        me, doc_length, valid_count, own, across, products, split, own_q, steps
    )
    others = swap(theirs, split, size)
    bits = [1] + middle
    for bit in bits[:-1]:
        half = doc.shape[0] // 2
        doc = doc[:half] + swap(doc[half:], bit, size)
    more = swap(doc[1:], bits[-1], size)
    token_scores, doc = last(
        me, doc_length, valid_count, mine, others, doc[:1], more, place, split
    )
    return (token_scores, doc.T)


def solution(mesh):
    size = mesh.shape["seq"]
    placed = (
        P(("groups", "seq"), None),
        P("groups", "seq"),
        P(),
        P("seq", None),
        P("seq", None),
        P("groups"),
        P("groups"),
    )
    return jax.shard_map(
        functools.partial(body, size),
        mesh=mesh,
        in_specs=placed,
        out_specs=(P(("groups", "seq"), None), P("groups", "seq")),
        check_vma=False,
    )
```

```python
import functools

import jax
import jax.numpy as jnp
from jax import lax
from jax.experimental import pallas as pl
from jax.experimental.pallas import tpu as pltpu
from jax.sharding import PartitionSpec as P

MIB = 1 << 20
SMEM = pl.BlockSpec(memory_space=pltpu.SMEM)
VMEM = pl.BlockSpec(memory_space=pltpu.VMEM)
HBM = pl.BlockSpec(memory_space=pltpu.HBM)


def swap(value, offset, size):
    return lax.ppermute(value, "seq", [(i, i ^ offset) for i in range(size)])


def grad_kernel(offsets, me_ref, proj_ref, grads_ref, out_ref, table, proj_buf, grads_buf, proj_sem, sems):
    load = pltpu.make_async_copy(proj_ref, proj_buf, proj_sem)
    load.start()
    halves, total, depth = grads_buf.shape
    count = len(offsets) // halves
    rows = total // count
    copies = []
    for k, offset in enumerate(offsets):
        first = pl.multiple_of((me_ref[0] ^ offset) * rows, rows)
        copy = pltpu.make_async_copy(
            grads_ref.at[pl.ds(first, rows)],
            grads_buf.at[k % halves, pl.ds((k // halves) * rows, rows)],
            sems.at[k],
        )
        copy.start(priority=k % 2)
        copies.append(copy)
    load.wait()
    turned = proj_buf[...].T
    none = jnp.zeros_like(turned)
    for r in range(halves):
        table[r] = jnp.concatenate([turned if c == r else none for c in range(halves)], axis=1)
    for k in range(count):
        made = None
        for r in range(halves):
            copies[k * halves + r].wait()
            part = jnp.dot(
                grads_buf[r, k * rows : (k + 1) * rows],
                table[r],
                preferred_element_type=jnp.float32,
            )
            made = part if made is None else made + part
        out_ref[k] = made


def held_kernel(offsets, me_ref, table, grads_ref, out_ref):
    halves = table.shape[0]
    count, rows, _ = out_ref.shape
    for k in range(0, count, 2):
        made = None
        for r in range(halves):
            left = []
            for offset in (offsets[k * halves + r], offsets[(k + 1) * halves + r]):
                first = pl.multiple_of((me_ref[0] ^ offset) * rows, rows)
                left.append(grads_ref[pl.ds(first, rows)])
            part = jnp.dot(
                jnp.concatenate(left, axis=0), table[r], preferred_element_type=jnp.float32
            )
            made = part if made is None else made + part
        out_ref[k] = made[:rows]
        out_ref[k + 1] = made[rows:]


def grad_blocks(me, proj, out_grads, rows, offsets, table=None):
    width, depth = proj.shape
    count = len(offsets) // 2
    made = jax.ShapeDtypeStruct((count, rows, 2 * width), jnp.float32)
    shared = dict(
        compiler_params=pltpu.CompilerParams(vmem_limit_bytes=24 * MIB),
        cost_estimate=pl.CostEstimate(
            flops=4 * count * rows * depth * width,
            bytes_accessed=4 * count * rows * depth,
            transcendentals=0,
        ),
    )
    if table is not None:
        return pl.pallas_call(
            functools.partial(held_kernel, offsets),
            in_specs=[SMEM, VMEM, VMEM],
            out_specs=VMEM,
            out_shape=made,
            **shared,
        )(me, table, out_grads)
    return pl.pallas_call(
        functools.partial(grad_kernel, offsets),
        in_specs=[SMEM, HBM, HBM],
        out_specs=(VMEM, VMEM),
        out_shape=(made, jax.ShapeDtypeStruct((2, depth, 2 * width), jnp.bfloat16)),
        scratch_shapes=[
            pltpu.VMEM((width, depth), jnp.bfloat16),
            pltpu.VMEM((2, count * rows, depth), jnp.bfloat16),
            pltpu.SemaphoreType.DMA,
            pltpu.SemaphoreType.DMA((2 * count,)),
        ],
        **shared,
    )(
        me,
        pltpu.with_memory_space_constraint(proj, pltpu.HBM),
        pltpu.with_memory_space_constraint(out_grads, pltpu.HBM),
    )


def inner_kernel(pieces, act_ref, *refs):
    out_ref = refs[pieces]
    columns = []
    for r in range(act_ref.shape[0]):
        act = act_ref[r]
        high = act.astype(jnp.bfloat16)
        low = (act - high.astype(jnp.float32)).astype(jnp.bfloat16)
        none = jnp.zeros_like(high)
        columns.append(jnp.concatenate([high, none, low, none], axis=0))
        columns.append(jnp.concatenate([none, high, none, low], axis=0))
    table = jnp.concatenate(columns, axis=1)
    pair = 2 * act_ref.shape[1]
    rows = []
    for k in range(refs[0].shape[1] // pair):
        for ref in refs[:pieces]:
            rows.append(ref[:, k * pair : (k + 1) * pair])
    left = jnp.concatenate(rows, axis=0)
    left = jnp.concatenate([left, left], axis=1)
    out_ref[...] = jnp.dot(left, table, preferred_element_type=jnp.float32)


def inner(act, panels, steps):
    halves, width, rows = act.shape
    count = sum(p.shape[0] for p in panels)
    pairs = panels[0].shape[1] // (2 * width)
    total = pairs * count
    if steps == 1:
        grid = {"in_specs": [VMEM] * (1 + len(panels)), "out_specs": VMEM}
    else:
        grid = {
            "grid": (steps,),
            "in_specs": [VMEM]
            + [pl.BlockSpec((p.shape[0], p.shape[1] // steps), lambda s: (0, s)) for p in panels],
            "out_specs": pl.BlockSpec((total // steps, 2 * halves * rows), lambda s: (s, 0)),
        }
    return pl.pallas_call(
        functools.partial(inner_kernel, len(panels)),
        out_shape=jax.ShapeDtypeStruct((total, 2 * halves * rows), jnp.float32),
        compiler_params=pltpu.CompilerParams(vmem_limit_bytes=32 * MIB),
        cost_estimate=pl.CostEstimate(
            flops=16 * total * width * halves * rows,
            bytes_accessed=8 * total * halves * rows,
            transcendentals=0,
        ),
        **grid,
    )(act, *panels)


def score_kernel(
    steps, split, me_ref, length_ref, valid_ref, own_ref, other_ref, inner_ref, own_tok, other_tok, doc_ref, grad_ref
):
    rows, wide = own_ref.shape
    halves, width = 2, wide // 2
    count = own_tok.shape[0]
    pairs = inner_ref.shape[0] // count
    step = pl.program_id(0) if steps > 1 else 0
    tokens = (own_tok, other_tok)

    def begin():
        other = other_ref[...].T
        grad_ref[...] = own_ref[...].T + jnp.concatenate([other[width:], other[:width]], axis=0)

    if steps == 1:
        begin()
    else:
        pl.when(step == 0)(begin)

    for r in range(halves):
        total = None
        for k in range(pairs):
            for parity in range(2):
                feature = 2 * k + parity
                if steps == 1:
                    line = grad_ref[r * width + feature : r * width + feature + 1]
                else:
                    line = grad_ref[pl.ds(r * width + 2 * pairs * step + feature, 1)]
                column = (2 * r + parity) * rows
                term = line * inner_ref[k * count : (k + 1) * count, column : column + rows]
                total = term if total is None else total + term
        if steps == 1:
            tokens[r][...] = total
        else:
            tokens[r][...] = jnp.where(step == 0, total, tokens[r][...] + total)

    def finish():
        me = me_ref[0]
        docs = length_ref.shape[0]
        doc_of = lax.broadcasted_iota(jnp.int32, (docs, rows), 0)
        lower = jnp.zeros((docs, rows), jnp.int32)
        upper = jnp.zeros((docs, rows), jnp.int32)
        start = jnp.int32(0)
        for d in range(docs):
            lower = jnp.where(doc_of == d, start, lower)
            used = jnp.minimum(valid_ref[d], length_ref[d])
            upper = jnp.where(doc_of == d, start + used, upper)
            start = start + length_ref[d]
        members, parts = [], []
        for r in range(halves):
            token = (me ^ (split * r)) * rows + lax.broadcasted_iota(jnp.int32, (docs, rows), 1)
            inside = (token >= lower) & (token < upper)
            members.append(jnp.where(inside, 1.0, 0.0).astype(jnp.bfloat16))
            left = tokens[r][...]
            for _ in range(3):
                part = left.astype(jnp.bfloat16)
                left = left - part.astype(jnp.float32)
                parts.append(part)
        partial = lax.dot_general(
            jnp.concatenate(parts, axis=1),
            jnp.concatenate([m for m in members for _ in range(3)], axis=1),
            (((1,), (1,)), ((), ())),
            preferred_element_type=jnp.float32,
        )
        own_q = doc_ref.shape[1]
        for k in range(doc_ref.shape[0]):
            doc_ref[k] = partial[k * own_q : (k + 1) * own_q]

    if steps == 1:
        finish()
    else:
        pl.when(step == steps - 1)(finish)


def score(me, lengths, valid, own, other, products, split, own_q, steps):
    rows, wide = own.shape
    docs = lengths.shape[0]
    count = 4 * products.shape[0] // wide
    if steps == 1:
        grid = {"in_specs": [SMEM] * 3 + [VMEM] * 3, "out_specs": (VMEM,) * 3}
    else:
        block = (products.shape[0] // steps, products.shape[1])
        grid = {
            "grid": (steps,),
            "in_specs": [SMEM] * 3 + [VMEM] * 2 + [pl.BlockSpec(block, lambda s: (s, 0))],
            "out_specs": (VMEM,) * 3,
        }
    return pl.pallas_call(
        functools.partial(score_kernel, steps, split),
        out_shape=(
            jax.ShapeDtypeStruct((count, rows), jnp.float32),
            jax.ShapeDtypeStruct((count, rows), jnp.float32),
            jax.ShapeDtypeStruct((count // own_q, own_q, docs), jnp.float32),
        ),
        scratch_shapes=[pltpu.VMEM((wide, rows), jnp.float32)],
        compiler_params=pltpu.CompilerParams(vmem_limit_bytes=32 * MIB),
        cost_estimate=pl.CostEstimate(
            flops=2 * products.shape[0] * products.shape[1],
            bytes_accessed=4 * products.shape[0] * products.shape[1],
            transcendentals=0,
        ),
        **grid,
    )(me, lengths, valid, own, other, products)


def last_kernel(
    place, split, me_ref, length_ref, valid_ref, own_ref, other_ref, doc_ref, more_ref, token_out, doc_out, turned_ref
):
    own_q, docs = doc_out.shape
    for r, ref in enumerate((own_ref, other_ref)):
        for k, offset in enumerate(place):
            spot = pl.multiple_of((me_ref[0] ^ (offset + split * r)) * own_q, own_q)
            turned_ref[pl.ds(spot, own_q)] = ref[k * own_q : (k + 1) * own_q]
    token_out[...] = turned_ref[...].T
    doc_of = lax.broadcasted_iota(jnp.int32, (own_q, docs), 1)
    used = jnp.zeros((own_q, docs), jnp.int32)
    for d in range(docs):
        used = jnp.where(doc_of == d, jnp.minimum(valid_ref[d], length_ref[d]), used)
    doc_out[...] = (doc_ref[0] + more_ref[0]) * (1.0 / jnp.sqrt(used.astype(jnp.float32)))


def last(me, lengths, valid, own, other, doc, more, place, split):
    count, rows = own.shape
    _, own_q, docs = doc.shape
    return pl.pallas_call(
        functools.partial(last_kernel, place, split),
        in_specs=[SMEM] * 3 + [VMEM] * 4,
        out_specs=(VMEM, VMEM),
        out_shape=(
            jax.ShapeDtypeStruct((rows, 2 * count), jnp.float32),
            jax.ShapeDtypeStruct((own_q, docs), jnp.float32),
        ),
        scratch_shapes=[pltpu.VMEM((2 * count, rows), jnp.float32)],
        compiler_params=pltpu.CompilerParams(vmem_limit_bytes=16 * MIB),
    )(me, lengths, valid, own, other, doc, more)


def offset_of(number, bits):
    last_bit = len(bits) - 1
    return sum(bit for k, bit in enumerate(bits) if (number >> (last_bit - k)) & 1)


def body(size, activations, out_grads, proj_in, proj_out, queries, doc_length, valid_count):
    rows = activations.shape[0]
    width = proj_in.shape[1]
    own_q = queries.shape[0]
    me = lax.axis_index("seq").astype(jnp.int32)[None]
    split = size // 4
    middle = [1 << k for k in range(1, size.bit_length() - 1) if 1 << k != split]

    proj = proj_out.T
    spots = [offset_of(m, middle) + split * r for m in range(size // 4) for r in range(2)]
    theirs, table = grad_blocks(me, proj, out_grads, rows, [s + 1 for s in spots])
    from_core = swap(theirs, 1, size)
    panel = queries
    got = swap(panel, middle[-1], size)
    sums = grad_blocks(me, proj, out_grads, rows, spots, table) + from_core
    late, _ = lax.optimization_barrier((proj_in, sums))
    for k, bit in enumerate(middle):
        half = sums.shape[0] // 2
        sent = swap(sums[half:].astype(jnp.bfloat16), bit, size)
        sums = sums[:half] + sent.astype(jnp.float32)
        if k == 0:
            got, _ = lax.optimization_barrier((got, sums))
    own = sums[0]
    across = swap(own, split, size)

    panel = jnp.concatenate([panel, got], axis=0)
    place = [0, middle[-1]]
    for bit in middle[-2::-1]:
        panel = jnp.concatenate([panel, swap(panel, bit, size)], axis=0)
        place = place + [p ^ bit for p in place]
    panels = [panel, swap(panel, 1, size)]
    place = tuple(place + [p ^ 1 for p in place])

    act = lax.dot_general(
        late, activations, (((0,), (1,)), ((), ())), preferred_element_type=jnp.float32
    )
    act = jnp.stack([act, swap(act, split, size)])
    steps = max(1, 4 * width * size * own_q * rows // (4 * MIB))
    products = inner(act, panels, steps)
    mine, theirs, doc = score(
        me, doc_length, valid_count, own, across, products, split, own_q, steps
    )
    others = swap(theirs, split, size)
    bits = [1] + middle
    for bit in bits[:-1]:
        half = doc.shape[0] // 2
        doc = doc[:half] + swap(doc[half:], bit, size)
    more = swap(doc[1:], bits[-1], size)
    token_scores, doc = last(
        me, doc_length, valid_count, mine, others, doc[:1], more, place, split
    )
    return (token_scores, doc.T)


def solution(mesh):
    size = mesh.shape["seq"]
    placed = (
        P(("groups", "seq"), None),
        P("groups", "seq"),
        P(),
        P("seq", None),
        P("seq", None),
        P("groups"),
        P("groups"),
    )
    return jax.shard_map(
        functools.partial(body, size),
        mesh=mesh,
        in_specs=placed,
        out_specs=(P(("groups", "seq"), None), P("groups", "seq")),
        check_vma=False,
    )
```

```python
import functools
import operator

import jax
import jax.numpy as jnp
from jax import lax
from jax.experimental import pallas as pl
from jax.experimental.pallas import tpu as pltpu
from jax.sharding import PartitionSpec as P

MIB = 1 << 20
SMEM = pl.BlockSpec(memory_space=pltpu.SMEM)
VMEM = pl.BlockSpec(memory_space=pltpu.VMEM)
HBM = pl.BlockSpec(memory_space=pltpu.HBM)


def swap(value, offset, size):
    return lax.ppermute(value, "seq", [(i, i ^ offset) for i in range(size)])


def grad_kernel(offsets, me_ref, proj_ref, grads_ref, out_ref, table, proj_buf, grads_buf, proj_sem, sems):
    load = pltpu.make_async_copy(proj_ref, proj_buf, proj_sem)
    load.start()
    halves, total, depth = grads_buf.shape
    count = len(offsets) // halves
    rows = total // count
    copies = []
    for k, offset in enumerate(offsets):
        first = pl.multiple_of((me_ref[0] ^ offset) * rows, rows)
        copy = pltpu.make_async_copy(
            grads_ref.at[pl.ds(first, rows)],
            grads_buf.at[k % halves, pl.ds((k // halves) * rows, rows)],
            sems.at[k],
        )
        copy.start(priority=k % 2)
        copies.append(copy)
    load.wait()
    turned = proj_buf[...].T
    none = jnp.zeros_like(turned)
    for r in range(halves):
        table[r] = jnp.concatenate([turned if c == r else none for c in range(halves)], axis=1)
    for k in range(count):
        made = None
        for r in range(halves):
            copies[k * halves + r].wait()
            part = jnp.dot(
                grads_buf[r, k * rows : (k + 1) * rows],
                table[r],
                preferred_element_type=jnp.float32,
            )
            made = part if made is None else made + part
        out_ref[k] = made


def held_kernel(offsets, me_ref, table, grads_ref, out_ref):
    halves = table.shape[0]
    count, rows, _ = out_ref.shape
    for k in range(0, count, 2):
        made = None
        for r in range(halves):
            left = []
            for offset in (offsets[k * halves + r], offsets[(k + 1) * halves + r]):
                first = pl.multiple_of((me_ref[0] ^ offset) * rows, rows)
                left.append(grads_ref[pl.ds(first, rows)])
            part = jnp.dot(
                jnp.concatenate(left, axis=0), table[r], preferred_element_type=jnp.float32
            )
            made = part if made is None else made + part
        out_ref[k] = made[:rows]
        out_ref[k + 1] = made[rows:]


def grad_blocks(me, proj, out_grads, rows, offsets, table=None):
    width, depth = proj.shape
    count = len(offsets) // 2
    made = jax.ShapeDtypeStruct((count, rows, 2 * width), jnp.float32)
    shared = dict(
        compiler_params=pltpu.CompilerParams(vmem_limit_bytes=24 * MIB),
        cost_estimate=pl.CostEstimate(
            flops=4 * count * rows * depth * width,
            bytes_accessed=4 * count * rows * depth,
            transcendentals=0,
        ),
    )
    if table is not None:
        return pl.pallas_call(
            functools.partial(held_kernel, offsets),
            in_specs=[SMEM, VMEM, VMEM],
            out_specs=VMEM,
            out_shape=made,
            **shared,
        )(me, table, out_grads)
    return pl.pallas_call(
        functools.partial(grad_kernel, offsets),
        in_specs=[SMEM, HBM, HBM],
        out_specs=(VMEM, VMEM),
        out_shape=(made, jax.ShapeDtypeStruct((2, depth, 2 * width), jnp.bfloat16)),
        scratch_shapes=[
            pltpu.VMEM((width, depth), jnp.bfloat16),
            pltpu.VMEM((2, count * rows, depth), jnp.bfloat16),
            pltpu.SemaphoreType.DMA,
            pltpu.SemaphoreType.DMA((2 * count,)),
        ],
        **shared,
    )(
        me,
        pltpu.with_memory_space_constraint(proj, pltpu.HBM),
        pltpu.with_memory_space_constraint(out_grads, pltpu.HBM),
    )


def inner_kernel(pieces, act_ref, *refs):
    out_ref = refs[pieces]
    columns = []
    for r in range(act_ref.shape[0]):
        act = act_ref[r]
        high = act.astype(jnp.bfloat16)
        low = (act - high.astype(jnp.float32)).astype(jnp.bfloat16)
        none = jnp.zeros_like(high)
        columns.append(jnp.concatenate([high, none, low, none], axis=0))
        columns.append(jnp.concatenate([none, high, none, low], axis=0))
    table = jnp.concatenate(columns, axis=1)
    pair = 2 * act_ref.shape[1]
    rows = []
    for k in range(refs[0].shape[1] // pair):
        for ref in refs[:pieces]:
            rows.append(ref[:, k * pair : (k + 1) * pair])
    left = jnp.concatenate(rows, axis=0)
    left = jnp.concatenate([left, left], axis=1)
    out_ref[...] = jnp.dot(left, table, preferred_element_type=jnp.float32)


def inner(act, panels, steps):
    halves, width, rows = act.shape
    count = sum(p.shape[0] for p in panels)
    pairs = panels[0].shape[1] // (2 * width)
    total = pairs * count
    if steps == 1:
        grid = {"in_specs": [VMEM] * (1 + len(panels)), "out_specs": VMEM}
    else:
        grid = {
            "grid": (steps,),
            "in_specs": [VMEM]
            + [pl.BlockSpec((p.shape[0], p.shape[1] // steps), lambda s: (0, s)) for p in panels],
            "out_specs": pl.BlockSpec((total // steps, 2 * halves * rows), lambda s: (s, 0)),
        }
    return pl.pallas_call(
        functools.partial(inner_kernel, len(panels)),
        out_shape=jax.ShapeDtypeStruct((total, 2 * halves * rows), jnp.float32),
        compiler_params=pltpu.CompilerParams(vmem_limit_bytes=32 * MIB),
        cost_estimate=pl.CostEstimate(
            flops=16 * total * width * halves * rows,
            bytes_accessed=8 * total * halves * rows,
            transcendentals=0,
        ),
        **grid,
    )(act, *panels)


def score_kernel(
    steps, split, me_ref, length_ref, valid_ref, own_ref, other_ref, inner_ref, own_tok, other_tok, doc_ref, grad_ref
):
    rows, wide = own_ref.shape
    halves, width = 2, wide // 2
    count = own_tok.shape[0]
    pairs = inner_ref.shape[0] // count
    step = pl.program_id(0) if steps > 1 else 0
    tokens = (own_tok, other_tok)

    def begin():
        other = other_ref[...].T
        grad_ref[...] = own_ref[...].T + jnp.concatenate([other[width:], other[:width]], axis=0)

    if steps == 1:
        begin()
    else:
        pl.when(step == 0)(begin)

    for r in range(halves):
        total = None
        for k in range(pairs):
            for parity in range(2):
                feature = 2 * k + parity
                if steps == 1:
                    line = grad_ref[r * width + feature : r * width + feature + 1]
                else:
                    line = grad_ref[pl.ds(r * width + 2 * pairs * step + feature, 1)]
                column = (2 * r + parity) * rows
                term = line * inner_ref[k * count : (k + 1) * count, column : column + rows]
                total = term if total is None else total + term
        if steps == 1:
            tokens[r][...] = total
        else:
            tokens[r][...] = jnp.where(step == 0, total, tokens[r][...] + total)

    def finish():
        me = me_ref[0]
        docs = length_ref.shape[0]
        doc_of = lax.broadcasted_iota(jnp.int32, (docs, rows), 0)
        lower = jnp.zeros((docs, rows), jnp.int32)
        upper = jnp.zeros((docs, rows), jnp.int32)
        start = jnp.int32(0)
        for d in range(docs):
            lower = jnp.where(doc_of == d, start, lower)
            used = jnp.minimum(valid_ref[d], length_ref[d])
            upper = jnp.where(doc_of == d, start + used, upper)
            start = start + length_ref[d]
        members, parts = [], []
        for r in range(halves):
            token = (me ^ (split * r)) * rows + lax.broadcasted_iota(jnp.int32, (docs, rows), 1)
            inside = (token >= lower) & (token < upper)
            members.append(jnp.where(inside, 1.0, 0.0).astype(jnp.bfloat16))
            left = tokens[r][...]
            for _ in range(3):
                part = left.astype(jnp.bfloat16)
                left = left - part.astype(jnp.float32)
                parts.append(part)
        partial = lax.dot_general(
            jnp.concatenate(parts, axis=1),
            jnp.concatenate([m for m in members for _ in range(3)], axis=1),
            (((1,), (1,)), ((), ())),
            preferred_element_type=jnp.float32,
        )
        own_q = doc_ref.shape[1]
        for k in range(doc_ref.shape[0]):
            doc_ref[k] = partial[k * own_q : (k + 1) * own_q]

    if steps == 1:
        finish()
    else:
        pl.when(step == steps - 1)(finish)


def score(me, lengths, valid, own, other, products, split, own_q, steps):
    rows, wide = own.shape
    docs = lengths.shape[0]
    count = 4 * products.shape[0] // wide
    if steps == 1:
        grid = {"in_specs": [SMEM] * 3 + [VMEM] * 3, "out_specs": (VMEM,) * 3}
    else:
        block = (products.shape[0] // steps, products.shape[1])
        grid = {
            "grid": (steps,),
            "in_specs": [SMEM] * 3 + [VMEM] * 2 + [pl.BlockSpec(block, lambda s: (s, 0))],
            "out_specs": (VMEM,) * 3,
        }
    return pl.pallas_call(
        functools.partial(score_kernel, steps, split),
        out_shape=(
            jax.ShapeDtypeStruct((count, rows), jnp.float32),
            jax.ShapeDtypeStruct((count, rows), jnp.float32),
            jax.ShapeDtypeStruct((count // own_q, own_q, docs), jnp.float32),
        ),
        scratch_shapes=[pltpu.VMEM((wide, rows), jnp.float32)],
        compiler_params=pltpu.CompilerParams(vmem_limit_bytes=32 * MIB),
        cost_estimate=pl.CostEstimate(
            flops=2 * products.shape[0] * products.shape[1],
            bytes_accessed=4 * products.shape[0] * products.shape[1],
            transcendentals=0,
        ),
        **grid,
    )(me, lengths, valid, own, other, products)


def place_kernel(place, split, me_ref, own_ref, other_ref, out_ref, turned_ref):
    own_q = own_ref.shape[0] // len(place)
    for r, ref in enumerate((own_ref, other_ref)):
        for k, offset in enumerate(place):
            spot = pl.multiple_of((me_ref[0] ^ offset ^ (split * r)) * own_q, own_q)
            turned_ref[pl.ds(spot, own_q)] = ref[k * own_q : (k + 1) * own_q]
    out_ref[...] = turned_ref[...].T


def place_tokens(me, own, other, place, split):
    count, rows = own.shape
    return pl.pallas_call(
        functools.partial(place_kernel, place, split),
        in_specs=[SMEM, VMEM, VMEM],
        out_specs=VMEM,
        out_shape=jax.ShapeDtypeStruct((rows, 2 * count), jnp.float32),
        scratch_shapes=[pltpu.VMEM((2 * count, rows), jnp.float32)],
        compiler_params=pltpu.CompilerParams(vmem_limit_bytes=16 * MIB),
    )(me, own, other)


def offset_of(number, bits):
    last_bit = len(bits) - 1
    return functools.reduce(
        operator.xor, [bit for k, bit in enumerate(bits) if (number >> (last_bit - k)) & 1], 0
    )


def body(size, activations, out_grads, proj_in, proj_out, queries, doc_length, valid_count):
    rows = activations.shape[0]
    width = proj_in.shape[1]
    own_q = queries.shape[0]
    me = lax.axis_index("seq").astype(jnp.int32)[None]
    split = size // 4 + 1
    middle = [(1 << k) + 1 for k in range(1, size.bit_length() - 1) if 1 << k != size // 4]

    proj = proj_out.T
    spots = [offset_of(m, middle) ^ (split * r) for m in range(size // 4) for r in range(2)]
    theirs, table = grad_blocks(me, proj, out_grads, rows, [s ^ 1 for s in spots])
    from_core = swap(theirs, 1, size)
    panel = queries
    got = swap(panel, middle[-1], size)
    sums = grad_blocks(me, proj, out_grads, rows, spots, table) + from_core
    late, _ = lax.optimization_barrier((proj_in, sums))
    for k, bit in enumerate(middle):
        half = sums.shape[0] // 2
        sent = swap(sums[half:].astype(jnp.bfloat16), bit, size)
        sums = sums[:half] + sent.astype(jnp.float32)
        if k == 0:
            got, _ = lax.optimization_barrier((got, sums))
    own = sums[0]
    across = swap(own, split, size)

    panel = jnp.concatenate([panel, got], axis=0)
    place = [0, middle[-1]]
    for bit in middle[-2::-1]:
        panel = jnp.concatenate([panel, swap(panel, bit, size)], axis=0)
        place = place + [p ^ bit for p in place]
    panels = [panel, swap(panel, 1, size)]
    place = tuple(place + [p ^ 1 for p in place])

    act = lax.dot_general(
        late, activations, (((0,), (1,)), ((), ())), preferred_element_type=jnp.float32
    )
    act = jnp.stack([act, swap(act, split, size)])
    steps = max(1, 4 * width * size * own_q * rows // (4 * MIB))
    products = inner(act, panels, steps)
    mine, theirs, doc = score(
        me, doc_length, valid_count, own, across, products, split, own_q, steps
    )
    others = swap(theirs, split, size)
    bits = [1] + middle
    for bit in bits[:-1]:
        half = doc.shape[0] // 2
        doc = doc[:half] + swap(doc[half:], bit, size)
    more = swap(doc[1:], bits[-1], size)
    token_scores = place_tokens(me, mine, others, place, split)
    more, token_scores = lax.optimization_barrier((more, token_scores))
    scale = 1.0 / jnp.sqrt(jnp.minimum(valid_count, doc_length).astype(jnp.float32))
    return (token_scores, ((doc[0] + more[0]) * scale[None, :]).T)


def solution(mesh):
    size = mesh.shape["seq"]
    placed = (
        P(("groups", "seq"), None),
        P("groups", "seq"),
        P(),
        P("seq", None),
        P("seq", None),
        P("groups"),
        P("groups"),
    )
    return jax.shard_map(
        functools.partial(body, size),
        mesh=mesh,
        in_specs=placed,
        out_specs=(P(("groups", "seq"), None), P("groups", "seq")),
        check_vma=False,
    )
```

```python
import functools
import operator

import jax
import jax.numpy as jnp
from jax import lax
from jax.experimental import pallas as pl
from jax.experimental.pallas import tpu as pltpu
from jax.sharding import PartitionSpec as P

MIB = 1 << 20
SMEM = pl.BlockSpec(memory_space=pltpu.SMEM)
VMEM = pl.BlockSpec(memory_space=pltpu.VMEM)
HBM = pl.BlockSpec(memory_space=pltpu.HBM)


def swap(value, offset, size):
    return lax.ppermute(value, "seq", [(i, i ^ offset) for i in range(size)])


def grad_kernel(offsets, me_ref, proj_ref, grads_ref, out_ref, table, proj_buf, grads_buf, proj_sem, sems):
    load = pltpu.make_async_copy(proj_ref, proj_buf, proj_sem)
    load.start()
    halves, total, depth = grads_buf.shape
    count = len(offsets) // halves
    rows = total // count
    copies = []
    for k, offset in enumerate(offsets):
        first = pl.multiple_of((me_ref[0] ^ offset) * rows, rows)
        copy = pltpu.make_async_copy(
            grads_ref.at[pl.ds(first, rows)],
            grads_buf.at[k % halves, pl.ds((k // halves) * rows, rows)],
            sems.at[k],
        )
        copy.start(priority=k % 2)
        copies.append(copy)
    load.wait()
    turned = proj_buf[...].T
    none = jnp.zeros_like(turned)
    for r in range(halves):
        table[r] = jnp.concatenate([turned if c == r else none for c in range(halves)], axis=1)
    for k in range(count):
        made = None
        for r in range(halves):
            copies[k * halves + r].wait()
            part = jnp.dot(
                grads_buf[r, k * rows : (k + 1) * rows],
                table[r],
                preferred_element_type=jnp.float32,
            )
            made = part if made is None else made + part
        out_ref[k] = made


def held_kernel(offsets, me_ref, table, grads_ref, out_ref):
    halves = table.shape[0]
    count, rows, _ = out_ref.shape
    for k in range(0, count, 2):
        made = None
        for r in range(halves):
            left = []
            for offset in (offsets[k * halves + r], offsets[(k + 1) * halves + r]):
                first = pl.multiple_of((me_ref[0] ^ offset) * rows, rows)
                left.append(grads_ref[pl.ds(first, rows)])
            part = jnp.dot(
                jnp.concatenate(left, axis=0), table[r], preferred_element_type=jnp.float32
            )
            made = part if made is None else made + part
        out_ref[k] = made[:rows]
        out_ref[k + 1] = made[rows:]


def grad_blocks(me, proj, out_grads, rows, offsets, table=None):
    width, depth = proj.shape
    count = len(offsets) // 2
    made = jax.ShapeDtypeStruct((count, rows, 2 * width), jnp.float32)
    shared = dict(
        compiler_params=pltpu.CompilerParams(vmem_limit_bytes=24 * MIB),
        cost_estimate=pl.CostEstimate(
            flops=4 * count * rows * depth * width,
            bytes_accessed=4 * count * rows * depth,
            transcendentals=0,
        ),
    )
    if table is not None:
        return pl.pallas_call(
            functools.partial(held_kernel, offsets),
            in_specs=[SMEM, VMEM, VMEM],
            out_specs=VMEM,
            out_shape=made,
            **shared,
        )(me, table, out_grads)
    return pl.pallas_call(
        functools.partial(grad_kernel, offsets),
        in_specs=[SMEM, HBM, HBM],
        out_specs=(VMEM, VMEM),
        out_shape=(made, jax.ShapeDtypeStruct((2, depth, 2 * width), jnp.bfloat16)),
        scratch_shapes=[
            pltpu.VMEM((width, depth), jnp.bfloat16),
            pltpu.VMEM((2, count * rows, depth), jnp.bfloat16),
            pltpu.SemaphoreType.DMA,
            pltpu.SemaphoreType.DMA((2 * count,)),
        ],
        **shared,
    )(
        me,
        pltpu.with_memory_space_constraint(proj, pltpu.HBM),
        pltpu.with_memory_space_constraint(out_grads, pltpu.HBM),
    )


def inner_kernel(pieces, act_ref, *refs):
    out_ref = refs[pieces]
    columns = []
    for r in range(act_ref.shape[0]):
        act = act_ref[r]
        high = act.astype(jnp.bfloat16)
        low = (act - high.astype(jnp.float32)).astype(jnp.bfloat16)
        none = jnp.zeros_like(high)
        columns.append(jnp.concatenate([high, none, low, none], axis=0))
        columns.append(jnp.concatenate([none, high, none, low], axis=0))
    table = jnp.concatenate(columns, axis=1)
    pair = 2 * act_ref.shape[1]
    rows = []
    for k in range(refs[0].shape[1] // pair):
        for ref in refs[:pieces]:
            rows.append(ref[:, k * pair : (k + 1) * pair])
    left = jnp.concatenate(rows, axis=0)
    left = jnp.concatenate([left, left], axis=1)
    out_ref[...] = jnp.dot(left, table, preferred_element_type=jnp.float32)


def inner(act, panels, steps):
    halves, width, rows = act.shape
    count = sum(p.shape[0] for p in panels)
    pairs = panels[0].shape[1] // (2 * width)
    total = pairs * count
    if steps == 1:
        grid = {"in_specs": [VMEM] * (1 + len(panels)), "out_specs": VMEM}
    else:
        grid = {
            "grid": (steps,),
            "in_specs": [VMEM]
            + [pl.BlockSpec((p.shape[0], p.shape[1] // steps), lambda s: (0, s)) for p in panels],
            "out_specs": pl.BlockSpec((total // steps, 2 * halves * rows), lambda s: (s, 0)),
        }
    return pl.pallas_call(
        functools.partial(inner_kernel, len(panels)),
        out_shape=jax.ShapeDtypeStruct((total, 2 * halves * rows), jnp.float32),
        compiler_params=pltpu.CompilerParams(vmem_limit_bytes=32 * MIB),
        cost_estimate=pl.CostEstimate(
            flops=16 * total * width * halves * rows,
            bytes_accessed=8 * total * halves * rows,
            transcendentals=0,
        ),
        **grid,
    )(act, *panels)


def score_kernel(
    steps, split, me_ref, length_ref, valid_ref, own_ref, other_ref, inner_ref, own_tok, other_tok, doc_ref, grad_ref
):
    rows, wide = own_ref.shape
    halves, width = 2, wide // 2
    count = own_tok.shape[0]
    pairs = inner_ref.shape[0] // count
    step = pl.program_id(0) if steps > 1 else 0
    tokens = (own_tok, other_tok)

    def begin():
        other = other_ref[...].T
        grad_ref[...] = own_ref[...].T + jnp.concatenate([other[width:], other[:width]], axis=0)

    if steps == 1:
        begin()
    else:
        pl.when(step == 0)(begin)

    for r in range(halves):
        total = None
        for k in range(pairs):
            for parity in range(2):
                feature = 2 * k + parity
                if steps == 1:
                    line = grad_ref[r * width + feature : r * width + feature + 1]
                else:
                    line = grad_ref[pl.ds(r * width + 2 * pairs * step + feature, 1)]
                column = (2 * r + parity) * rows
                term = line * inner_ref[k * count : (k + 1) * count, column : column + rows]
                total = term if total is None else total + term
        if steps == 1:
            tokens[r][...] = total
        else:
            tokens[r][...] = jnp.where(step == 0, total, tokens[r][...] + total)

    def finish():
        me = me_ref[0]
        docs = length_ref.shape[0]
        doc_of = lax.broadcasted_iota(jnp.int32, (docs, rows), 0)
        lower = jnp.zeros((docs, rows), jnp.int32)
        upper = jnp.zeros((docs, rows), jnp.int32)
        start = jnp.int32(0)
        for d in range(docs):
            lower = jnp.where(doc_of == d, start, lower)
            used = jnp.minimum(valid_ref[d], length_ref[d])
            upper = jnp.where(doc_of == d, start + used, upper)
            start = start + length_ref[d]
        members, parts = [], []
        for r in range(halves):
            token = (me ^ (split * r)) * rows + lax.broadcasted_iota(jnp.int32, (docs, rows), 1)
            inside = (token >= lower) & (token < upper)
            members.append(jnp.where(inside, 1.0, 0.0).astype(jnp.bfloat16))
            left = tokens[r][...]
            for _ in range(3):
                part = left.astype(jnp.bfloat16)
                left = left - part.astype(jnp.float32)
                parts.append(part)
        partial = lax.dot_general(
            jnp.concatenate(parts, axis=1),
            jnp.concatenate([m for m in members for _ in range(3)], axis=1),
            (((1,), (1,)), ((), ())),
            preferred_element_type=jnp.float32,
        )
        own_q = doc_ref.shape[1]
        for k in range(doc_ref.shape[0]):
            doc_ref[k] = partial[k * own_q : (k + 1) * own_q]

    if steps == 1:
        finish()
    else:
        pl.when(step == steps - 1)(finish)


def score(me, lengths, valid, own, other, products, split, own_q, steps):
    rows, wide = own.shape
    docs = lengths.shape[0]
    count = 4 * products.shape[0] // wide
    if steps == 1:
        grid = {"in_specs": [SMEM] * 3 + [VMEM] * 3, "out_specs": (VMEM,) * 3}
    else:
        block = (products.shape[0] // steps, products.shape[1])
        grid = {
            "grid": (steps,),
            "in_specs": [SMEM] * 3 + [VMEM] * 2 + [pl.BlockSpec(block, lambda s: (s, 0))],
            "out_specs": (VMEM,) * 3,
        }
    return pl.pallas_call(
        functools.partial(score_kernel, steps, split),
        out_shape=(
            jax.ShapeDtypeStruct((count, rows), jnp.float32),
            jax.ShapeDtypeStruct((count, rows), jnp.float32),
            jax.ShapeDtypeStruct((count // own_q, own_q, docs), jnp.float32),
        ),
        scratch_shapes=[pltpu.VMEM((wide, rows), jnp.float32)],
        compiler_params=pltpu.CompilerParams(vmem_limit_bytes=32 * MIB),
        cost_estimate=pl.CostEstimate(
            flops=2 * products.shape[0] * products.shape[1],
            bytes_accessed=4 * products.shape[0] * products.shape[1],
            transcendentals=0,
        ),
        **grid,
    )(me, lengths, valid, own, other, products)


def place_kernel(place, split, me_ref, own_ref, other_ref, out_ref, turned_ref):
    own_q = own_ref.shape[0] // len(place)
    for r, ref in enumerate((own_ref, other_ref)):
        for k, offset in enumerate(place):
            spot = pl.multiple_of((me_ref[0] ^ offset ^ (split * r)) * own_q, own_q)
            turned_ref[pl.ds(spot, own_q)] = ref[k * own_q : (k + 1) * own_q]
    out_ref[...] = turned_ref[...].T


def place_tokens(me, own, other, place, split):
    count, rows = own.shape
    return pl.pallas_call(
        functools.partial(place_kernel, place, split),
        in_specs=[SMEM, VMEM, VMEM],
        out_specs=VMEM,
        out_shape=jax.ShapeDtypeStruct((rows, 2 * count), jnp.float32),
        scratch_shapes=[pltpu.VMEM((2 * count, rows), jnp.float32)],
        compiler_params=pltpu.CompilerParams(vmem_limit_bytes=16 * MIB),
    )(me, own, other)


def offset_of(number, bits):
    last_bit = len(bits) - 1
    return functools.reduce(
        operator.xor, [bit for k, bit in enumerate(bits) if (number >> (last_bit - k)) & 1], 0
    )


def body(size, activations, out_grads, proj_in, proj_out, queries, doc_length, valid_count):
    rows = activations.shape[0]
    width = proj_in.shape[1]
    own_q = queries.shape[0]
    me = lax.axis_index("seq").astype(jnp.int32)[None]
    split = size // 4 + 1
    middle = [(1 << k) + 1 for k in range(1, size.bit_length() - 1) if 1 << k != size // 4]

    proj = proj_out.T
    spots = [offset_of(m, middle) ^ (split * r) for m in range(size // 4) for r in range(2)]
    theirs, table = grad_blocks(me, proj, out_grads, rows, [s ^ 1 for s in spots])
    from_core = swap(theirs, 1, size)
    panel = queries
    got = swap(panel, middle[-1], size)
    sums = grad_blocks(me, proj, out_grads, rows, spots, table) + from_core
    late, _ = lax.optimization_barrier((proj_in, sums))
    got, sums = lax.optimization_barrier((got, sums))
    for k, bit in enumerate(middle):
        half = sums.shape[0] // 2
        sent = swap(sums[half:].astype(jnp.bfloat16), bit, size)
        sums = sums[:half] + sent.astype(jnp.float32)
        if k == 0:
            after = sums
    own = sums[0]
    across = swap(own, split, size)
    act = lax.dot_general(
        late, activations, (((0,), (1,)), ((), ())), preferred_element_type=jnp.float32
    )
    sent_act = act
    act = jnp.stack([act, swap(sent_act, split, size)])

    panel = jnp.concatenate([panel, got], axis=0)
    place = [0, middle[-1]]
    for bit in middle[-2::-1]:
        panel = jnp.concatenate([panel, swap(panel, bit, size)], axis=0)
        place = place + [p ^ bit for p in place]
    panels = [panel, swap(panel, 1, size)]
    place = tuple(place + [p ^ 1 for p in place])

    steps = max(1, 4 * width * size * own_q * rows // (4 * MIB))
    products = inner(act, panels, steps)
    mine, theirs, doc = score(
        me, doc_length, valid_count, own, across, products, split, own_q, steps
    )
    others = swap(theirs, split, size)
    bits = [1] + middle
    for bit in bits[:-1]:
        half = doc.shape[0] // 2
        doc = doc[:half] + swap(doc[half:], bit, size)
    more = swap(doc[1:], bits[-1], size)
    token_scores = place_tokens(me, mine, others, place, split)
    more, token_scores = lax.optimization_barrier((more, token_scores))
    scale = 1.0 / jnp.sqrt(jnp.minimum(valid_count, doc_length).astype(jnp.float32))
    return (token_scores, ((doc[0] + more[0]) * scale[None, :]).T)


def solution(mesh):
    size = mesh.shape["seq"]
    placed = (
        P(("groups", "seq"), None),
        P("groups", "seq"),
        P(),
        P("seq", None),
        P("seq", None),
        P("groups"),
        P("groups"),
    )
    return jax.shard_map(
        functools.partial(body, size),
        mesh=mesh,
        in_specs=placed,
        out_specs=(P(("groups", "seq"), None), P("groups", "seq")),
        check_vma=False,
    )
```

```python
import functools
import operator

import jax
import jax.numpy as jnp
from jax import lax
from jax.experimental import pallas as pl
from jax.experimental.pallas import tpu as pltpu
from jax.sharding import PartitionSpec as P

MIB = 1 << 20
SMEM = pl.BlockSpec(memory_space=pltpu.SMEM)
VMEM = pl.BlockSpec(memory_space=pltpu.VMEM)
HBM = pl.BlockSpec(memory_space=pltpu.HBM)


def swap(value, offset, size):
    return lax.ppermute(value, "seq", [(i, i ^ offset) for i in range(size)])


def grad_kernel(offsets, me_ref, proj_ref, grads_ref, out_ref, table, proj_buf, grads_buf, proj_sem, sems):
    load = pltpu.make_async_copy(proj_ref, proj_buf, proj_sem)
    load.start()
    halves, total, depth = grads_buf.shape
    count = len(offsets) // halves
    rows = total // count
    copies = []
    for k, offset in enumerate(offsets):
        first = pl.multiple_of((me_ref[0] ^ offset) * rows, rows)
        copy = pltpu.make_async_copy(
            grads_ref.at[pl.ds(first, rows)],
            grads_buf.at[k % halves, pl.ds((k // halves) * rows, rows)],
            sems.at[k],
        )
        copy.start(priority=k % 2)
        copies.append(copy)
    load.wait()
    turned = proj_buf[...].T
    none = jnp.zeros_like(turned)
    for r in range(halves):
        table[r] = jnp.concatenate([turned if c == r else none for c in range(halves)], axis=1)
    for k in range(count):
        made = None
        for r in range(halves):
            copies[k * halves + r].wait()
            part = jnp.dot(
                grads_buf[r, k * rows : (k + 1) * rows],
                table[r],
                preferred_element_type=jnp.float32,
            )
            made = part if made is None else made + part
        out_ref[k] = made


def held_kernel(offsets, me_ref, table, grads_ref, out_ref):
    halves = table.shape[0]
    count, rows, _ = out_ref.shape
    for k in range(0, count, 2):
        made = None
        for r in range(halves):
            left = []
            for offset in (offsets[k * halves + r], offsets[(k + 1) * halves + r]):
                first = pl.multiple_of((me_ref[0] ^ offset) * rows, rows)
                left.append(grads_ref[pl.ds(first, rows)])
            part = jnp.dot(
                jnp.concatenate(left, axis=0), table[r], preferred_element_type=jnp.float32
            )
            made = part if made is None else made + part
        out_ref[k] = made[:rows]
        out_ref[k + 1] = made[rows:]


def grad_blocks(me, proj, out_grads, rows, offsets, table=None):
    width, depth = proj.shape
    count = len(offsets) // 2
    made = jax.ShapeDtypeStruct((count, rows, 2 * width), jnp.float32)
    shared = dict(
        compiler_params=pltpu.CompilerParams(vmem_limit_bytes=24 * MIB),
        cost_estimate=pl.CostEstimate(
            flops=4 * count * rows * depth * width,
            bytes_accessed=4 * count * rows * depth,
            transcendentals=0,
        ),
    )
    if table is not None:
        return pl.pallas_call(
            functools.partial(held_kernel, offsets),
            in_specs=[SMEM, VMEM, VMEM],
            out_specs=VMEM,
            out_shape=made,
            **shared,
        )(me, table, out_grads)
    return pl.pallas_call(
        functools.partial(grad_kernel, offsets),
        in_specs=[SMEM, HBM, HBM],
        out_specs=(VMEM, VMEM),
        out_shape=(made, jax.ShapeDtypeStruct((2, depth, 2 * width), jnp.bfloat16)),
        scratch_shapes=[
            pltpu.VMEM((width, depth), jnp.bfloat16),
            pltpu.VMEM((2, count * rows, depth), jnp.bfloat16),
            pltpu.SemaphoreType.DMA,
            pltpu.SemaphoreType.DMA((2 * count,)),
        ],
        **shared,
    )(
        me,
        pltpu.with_memory_space_constraint(proj, pltpu.HBM),
        pltpu.with_memory_space_constraint(out_grads, pltpu.HBM),
    )


def inner_kernel(pieces, act_ref, *refs):
    out_ref = refs[pieces]
    columns = []
    for r in range(act_ref.shape[0]):
        act = act_ref[r]
        high = act.astype(jnp.bfloat16)
        low = (act - high.astype(jnp.float32)).astype(jnp.bfloat16)
        none = jnp.zeros_like(high)
        columns.append(jnp.concatenate([high, none, low, none], axis=0))
        columns.append(jnp.concatenate([none, high, none, low], axis=0))
    table = jnp.concatenate(columns, axis=1)
    pair = 2 * act_ref.shape[1]
    rows = []
    for k in range(refs[0].shape[1] // pair):
        for ref in refs[:pieces]:
            rows.append(ref[:, k * pair : (k + 1) * pair])
    left = jnp.concatenate(rows, axis=0)
    left = jnp.concatenate([left, left], axis=1)
    out_ref[...] = jnp.dot(left, table, preferred_element_type=jnp.float32)


def inner(act, panels, steps):
    halves, width, rows = act.shape
    count = sum(p.shape[0] for p in panels)
    pairs = panels[0].shape[1] // (2 * width)
    total = pairs * count
    if steps == 1:
        grid = {"in_specs": [VMEM] * (1 + len(panels)), "out_specs": VMEM}
    else:
        grid = {
            "grid": (steps,),
            "in_specs": [VMEM]
            + [pl.BlockSpec((p.shape[0], p.shape[1] // steps), lambda s: (0, s)) for p in panels],
            "out_specs": pl.BlockSpec((total // steps, 2 * halves * rows), lambda s: (s, 0)),
        }
    return pl.pallas_call(
        functools.partial(inner_kernel, len(panels)),
        out_shape=jax.ShapeDtypeStruct((total, 2 * halves * rows), jnp.float32),
        compiler_params=pltpu.CompilerParams(vmem_limit_bytes=32 * MIB),
        cost_estimate=pl.CostEstimate(
            flops=16 * total * width * halves * rows,
            bytes_accessed=8 * total * halves * rows,
            transcendentals=0,
        ),
        **grid,
    )(act, *panels)


def score_kernel(
    steps, split, me_ref, length_ref, valid_ref, own_ref, other_ref, inner_ref, own_tok, other_tok, doc_ref, grad_ref
):
    rows, wide = own_ref.shape
    halves, width = 2, wide // 2
    count = own_tok.shape[0]
    pairs = inner_ref.shape[0] // count
    step = pl.program_id(0) if steps > 1 else 0
    tokens = (own_tok, other_tok)

    def begin():
        other = other_ref[...].astype(jnp.float32).T
        grad_ref[...] = own_ref[...].T + jnp.concatenate([other[width:], other[:width]], axis=0)

    if steps == 1:
        begin()
    else:
        pl.when(step == 0)(begin)

    for r in range(halves):
        total = None
        for k in range(pairs):
            for parity in range(2):
                feature = 2 * k + parity
                if steps == 1:
                    line = grad_ref[r * width + feature : r * width + feature + 1]
                else:
                    line = grad_ref[pl.ds(r * width + 2 * pairs * step + feature, 1)]
                column = (2 * r + parity) * rows
                term = line * inner_ref[k * count : (k + 1) * count, column : column + rows]
                total = term if total is None else total + term
        if steps == 1:
            tokens[r][...] = total
        else:
            tokens[r][...] = jnp.where(step == 0, total, tokens[r][...] + total)

    def finish():
        me = me_ref[0]
        docs = length_ref.shape[0]
        doc_of = lax.broadcasted_iota(jnp.int32, (docs, rows), 0)
        lower = jnp.zeros((docs, rows), jnp.int32)
        upper = jnp.zeros((docs, rows), jnp.int32)
        start = jnp.int32(0)
        for d in range(docs):
            lower = jnp.where(doc_of == d, start, lower)
            used = jnp.minimum(valid_ref[d], length_ref[d])
            upper = jnp.where(doc_of == d, start + used, upper)
            start = start + length_ref[d]
        members, parts = [], []
        for r in range(halves):
            token = (me ^ (split * r)) * rows + lax.broadcasted_iota(jnp.int32, (docs, rows), 1)
            inside = (token >= lower) & (token < upper)
            members.append(jnp.where(inside, 1.0, 0.0).astype(jnp.bfloat16))
            left = tokens[r][...]
            for _ in range(3):
                part = left.astype(jnp.bfloat16)
                left = left - part.astype(jnp.float32)
                parts.append(part)
        partial = lax.dot_general(
            jnp.concatenate(parts, axis=1),
            jnp.concatenate([m for m in members for _ in range(3)], axis=1),
            (((1,), (1,)), ((), ())),
            preferred_element_type=jnp.float32,
        )
        own_q = doc_ref.shape[1]
        for k in range(doc_ref.shape[0]):
            doc_ref[k] = partial[k * own_q : (k + 1) * own_q]

    if steps == 1:
        finish()
    else:
        pl.when(step == steps - 1)(finish)


def score(me, lengths, valid, own, other, products, split, own_q, steps):
    rows, wide = own.shape
    docs = lengths.shape[0]
    count = 4 * products.shape[0] // wide
    if steps == 1:
        grid = {"in_specs": [SMEM] * 3 + [VMEM] * 3, "out_specs": (VMEM,) * 3}
    else:
        block = (products.shape[0] // steps, products.shape[1])
        grid = {
            "grid": (steps,),
            "in_specs": [SMEM] * 3 + [VMEM] * 2 + [pl.BlockSpec(block, lambda s: (s, 0))],
            "out_specs": (VMEM,) * 3,
        }
    return pl.pallas_call(
        functools.partial(score_kernel, steps, split),
        out_shape=(
            jax.ShapeDtypeStruct((count, rows), jnp.float32),
            jax.ShapeDtypeStruct((count, rows), jnp.float32),
            jax.ShapeDtypeStruct((count // own_q, own_q, docs), jnp.float32),
        ),
        scratch_shapes=[pltpu.VMEM((wide, rows), jnp.float32)],
        compiler_params=pltpu.CompilerParams(vmem_limit_bytes=32 * MIB),
        cost_estimate=pl.CostEstimate(
            flops=2 * products.shape[0] * products.shape[1],
            bytes_accessed=4 * products.shape[0] * products.shape[1],
            transcendentals=0,
        ),
        **grid,
    )(me, lengths, valid, own, other, products)


def place_kernel(place, split, me_ref, own_ref, other_ref, out_ref, turned_ref):
    own_q = own_ref.shape[0] // len(place)
    for r, ref in enumerate((own_ref, other_ref)):
        for k, offset in enumerate(place):
            spot = pl.multiple_of((me_ref[0] ^ offset ^ (split * r)) * own_q, own_q)
            turned_ref[pl.ds(spot, own_q)] = ref[k * own_q : (k + 1) * own_q]
    out_ref[...] = turned_ref[...].T


def place_tokens(me, own, other, place, split):
    count, rows = own.shape
    return pl.pallas_call(
        functools.partial(place_kernel, place, split),
        in_specs=[SMEM, VMEM, VMEM],
        out_specs=VMEM,
        out_shape=jax.ShapeDtypeStruct((rows, 2 * count), jnp.float32),
        scratch_shapes=[pltpu.VMEM((2 * count, rows), jnp.float32)],
        compiler_params=pltpu.CompilerParams(vmem_limit_bytes=16 * MIB),
    )(me, own, other)


def offset_of(number, bits):
    last_bit = len(bits) - 1
    return functools.reduce(
        operator.xor, [bit for k, bit in enumerate(bits) if (number >> (last_bit - k)) & 1], 0
    )


def body(size, activations, out_grads, proj_in, proj_out, queries, doc_length, valid_count):
    rows = activations.shape[0]
    width = proj_in.shape[1]
    own_q = queries.shape[0]
    me = lax.axis_index("seq").astype(jnp.int32)[None]
    split = size // 2 + 1
    middle = [(1 << k) + 1 for k in range(1, size.bit_length() - 2)]

    proj = proj_out.T
    spots = [offset_of(m, middle) ^ (split * r) for m in range(size // 4) for r in range(2)]
    theirs, table = grad_blocks(me, proj, out_grads, rows, [s ^ 1 for s in spots])
    from_core = swap(theirs, 1, size)
    panel = queries
    got = swap(panel, middle[-1], size)
    sums = grad_blocks(me, proj, out_grads, rows, spots, table) + from_core
    late, _ = lax.optimization_barrier((proj_in, sums))
    got, sums = lax.optimization_barrier((got, sums))
    for k, bit in enumerate(middle):
        half = sums.shape[0] // 2
        kind = jnp.bfloat16 if k == 0 else jnp.float32
        sent = swap(sums[half:].astype(kind), bit, size)
        sums = sums[:half] + sent.astype(jnp.float32)
    own = sums[0]
    across = swap(own.astype(jnp.bfloat16), split, size)
    act = lax.dot_general(
        late, activations, (((0,), (1,)), ((), ())), preferred_element_type=jnp.float32
    )
    act = jnp.stack([act, swap(act, split, size)])

    panel = jnp.concatenate([panel, got], axis=0)
    place = [0, middle[-1]]
    for bit in middle[-2::-1]:
        panel = jnp.concatenate([panel, swap(panel, bit, size)], axis=0)
        place = place + [p ^ bit for p in place]
    panels = [panel, swap(panel, 1, size)]
    place = tuple(place + [p ^ 1 for p in place])

    steps = max(1, 4 * width * size * own_q * rows // (4 * MIB))
    products = inner(act, panels, steps)
    mine, theirs, doc = score(
        me, doc_length, valid_count, own, across, products, split, own_q, steps
    )
    others = swap(theirs, split, size)
    bits = [1] + middle
    for bit in bits[:-1]:
        half = doc.shape[0] // 2
        doc = doc[:half] + swap(doc[half:], bit, size)
    more = swap(doc[1:], bits[-1], size)
    token_scores = place_tokens(me, mine, others, place, split)
    more, token_scores = lax.optimization_barrier((more, token_scores))
    scale = 1.0 / jnp.sqrt(jnp.minimum(valid_count, doc_length).astype(jnp.float32))
    return (token_scores, ((doc[0] + more[0]) * scale[None, :]).T)


def solution(mesh):
    size = mesh.shape["seq"]
    placed = (
        P(("groups", "seq"), None),
        P("groups", "seq"),
        P(),
        P("seq", None),
        P("seq", None),
        P("groups"),
        P("groups"),
    )
    return jax.shard_map(
        functools.partial(body, size),
        mesh=mesh,
        in_specs=placed,
        out_specs=(P(("groups", "seq"), None), P("groups", "seq")),
        check_vma=False,
    )
```

```python
import functools
import operator

import jax
import jax.numpy as jnp
from jax import lax
from jax.experimental import pallas as pl
from jax.experimental.pallas import tpu as pltpu
from jax.sharding import PartitionSpec as P

MIB = 1 << 20
SMEM = pl.BlockSpec(memory_space=pltpu.SMEM)
VMEM = pl.BlockSpec(memory_space=pltpu.VMEM)
HBM = pl.BlockSpec(memory_space=pltpu.HBM)


def swap(value, offset, size):
    return lax.ppermute(value, "seq", [(i, i ^ offset) for i in range(size)])


def grad_kernel(offsets, me_ref, proj_ref, grads_ref, out_ref, table, proj_buf, grads_buf, proj_sem, sems):
    load = pltpu.make_async_copy(proj_ref, proj_buf, proj_sem)
    load.start()
    halves, total, depth = grads_buf.shape
    count = len(offsets) // halves
    rows = total // count
    copies = []
    for k, offset in enumerate(offsets):
        first = pl.multiple_of((me_ref[0] ^ offset) * rows, rows)
        copy = pltpu.make_async_copy(
            grads_ref.at[pl.ds(first, rows)],
            grads_buf.at[k % halves, pl.ds((k // halves) * rows, rows)],
            sems.at[k],
        )
        copy.start(priority=k % 2)
        copies.append(copy)
    load.wait()
    turned = proj_buf[...].T
    none = jnp.zeros_like(turned)
    for r in range(halves):
        table[r] = jnp.concatenate([turned if c == r else none for c in range(halves)], axis=1)
    for k in range(count):
        made = None
        for r in range(halves):
            copies[k * halves + r].wait()
            part = jnp.dot(
                grads_buf[r, k * rows : (k + 1) * rows],
                table[r],
                preferred_element_type=jnp.float32,
            )
            made = part if made is None else made + part
        out_ref[k] = made


def held_kernel(offsets, me_ref, table, grads_ref, out_ref):
    halves = table.shape[0]
    count, rows, _ = out_ref.shape
    for k in range(0, count, 2):
        made = None
        for r in range(halves):
            left = []
            for offset in (offsets[k * halves + r], offsets[(k + 1) * halves + r]):
                first = pl.multiple_of((me_ref[0] ^ offset) * rows, rows)
                left.append(grads_ref[pl.ds(first, rows)])
            part = jnp.dot(
                jnp.concatenate(left, axis=0), table[r], preferred_element_type=jnp.float32
            )
            made = part if made is None else made + part
        out_ref[k] = made[:rows]
        out_ref[k + 1] = made[rows:]


def grad_blocks(me, proj, out_grads, rows, offsets, table=None):
    width, depth = proj.shape
    count = len(offsets) // 2
    made = jax.ShapeDtypeStruct((count, rows, 2 * width), jnp.float32)
    shared = dict(
        compiler_params=pltpu.CompilerParams(vmem_limit_bytes=24 * MIB),
        cost_estimate=pl.CostEstimate(
            flops=4 * count * rows * depth * width,
            bytes_accessed=4 * count * rows * depth,
            transcendentals=0,
        ),
    )
    if table is not None:
        return pl.pallas_call(
            functools.partial(held_kernel, offsets),
            in_specs=[SMEM, VMEM, VMEM],
            out_specs=VMEM,
            out_shape=made,
            **shared,
        )(me, table, out_grads)
    return pl.pallas_call(
        functools.partial(grad_kernel, offsets),
        in_specs=[SMEM, HBM, HBM],
        out_specs=(VMEM, VMEM),
        out_shape=(made, jax.ShapeDtypeStruct((2, depth, 2 * width), jnp.bfloat16)),
        scratch_shapes=[
            pltpu.VMEM((width, depth), jnp.bfloat16),
            pltpu.VMEM((2, count * rows, depth), jnp.bfloat16),
            pltpu.SemaphoreType.DMA,
            pltpu.SemaphoreType.DMA((2 * count,)),
        ],
        **shared,
    )(
        me,
        pltpu.with_memory_space_constraint(proj, pltpu.HBM),
        pltpu.with_memory_space_constraint(out_grads, pltpu.HBM),
    )


def inner_kernel(pieces, act_ref, *refs):
    out_ref = refs[pieces]
    columns = []
    for r in range(act_ref.shape[0]):
        act = act_ref[r]
        high = act.astype(jnp.bfloat16)
        low = (act - high.astype(jnp.float32)).astype(jnp.bfloat16)
        none = jnp.zeros_like(high)
        columns.append(jnp.concatenate([high, none, low, none], axis=0))
        columns.append(jnp.concatenate([none, high, none, low], axis=0))
    table = jnp.concatenate(columns, axis=1)
    pair = 2 * act_ref.shape[1]
    rows = []
    for k in range(refs[0].shape[1] // pair):
        for ref in refs[:pieces]:
            rows.append(ref[:, k * pair : (k + 1) * pair])
    left = jnp.concatenate(rows, axis=0)
    left = jnp.concatenate([left, left], axis=1)
    out_ref[...] = jnp.dot(left, table, preferred_element_type=jnp.float32)


def inner(act, panels, steps):
    halves, width, rows = act.shape
    count = sum(p.shape[0] for p in panels)
    pairs = panels[0].shape[1] // (2 * width)
    total = pairs * count
    if steps == 1:
        grid = {"in_specs": [VMEM] * (1 + len(panels)), "out_specs": VMEM}
    else:
        grid = {
            "grid": (steps,),
            "in_specs": [VMEM]
            + [pl.BlockSpec((p.shape[0], p.shape[1] // steps), lambda s: (0, s)) for p in panels],
            "out_specs": pl.BlockSpec((total // steps, 2 * halves * rows), lambda s: (s, 0)),
        }
    return pl.pallas_call(
        functools.partial(inner_kernel, len(panels)),
        out_shape=jax.ShapeDtypeStruct((total, 2 * halves * rows), jnp.float32),
        compiler_params=pltpu.CompilerParams(vmem_limit_bytes=32 * MIB),
        cost_estimate=pl.CostEstimate(
            flops=16 * total * width * halves * rows,
            bytes_accessed=8 * total * halves * rows,
            transcendentals=0,
        ),
        **grid,
    )(act, *panels)


def score_kernel(
    steps, split, me_ref, length_ref, valid_ref, own_ref, other_ref, inner_ref, own_tok, other_tok, doc_ref, grad_ref
):
    rows, wide = own_ref.shape
    halves, width = 2, wide // 2
    count = own_tok.shape[0]
    pairs = inner_ref.shape[0] // count
    step = pl.program_id(0) if steps > 1 else 0
    tokens = (own_tok, other_tok)

    def begin():
        other = other_ref[...].astype(jnp.float32).T
        grad_ref[...] = own_ref[...].T + jnp.concatenate([other[width:], other[:width]], axis=0)

    if steps == 1:
        begin()
    else:
        pl.when(step == 0)(begin)

    for r in range(halves):
        total = None
        for k in range(pairs):
            for parity in range(2):
                feature = 2 * k + parity
                if steps == 1:
                    line = grad_ref[r * width + feature : r * width + feature + 1]
                else:
                    line = grad_ref[pl.ds(r * width + 2 * pairs * step + feature, 1)]
                column = (2 * r + parity) * rows
                term = line * inner_ref[k * count : (k + 1) * count, column : column + rows]
                total = term if total is None else total + term
        if steps == 1:
            tokens[r][...] = total
        else:
            tokens[r][...] = jnp.where(step == 0, total, tokens[r][...] + total)

    def finish():
        me = me_ref[0]
        docs = length_ref.shape[0]
        doc_of = lax.broadcasted_iota(jnp.int32, (docs, rows), 0)
        lower = jnp.zeros((docs, rows), jnp.int32)
        upper = jnp.zeros((docs, rows), jnp.int32)
        start = jnp.int32(0)
        for d in range(docs):
            lower = jnp.where(doc_of == d, start, lower)
            used = jnp.minimum(valid_ref[d], length_ref[d])
            upper = jnp.where(doc_of == d, start + used, upper)
            start = start + length_ref[d]
        members, parts = [], []
        for r in range(halves):
            token = (me ^ (split * r)) * rows + lax.broadcasted_iota(jnp.int32, (docs, rows), 1)
            inside = (token >= lower) & (token < upper)
            members.append(jnp.where(inside, 1.0, 0.0).astype(jnp.bfloat16))
            left = tokens[r][...]
            for _ in range(3):
                part = left.astype(jnp.bfloat16)
                left = left - part.astype(jnp.float32)
                parts.append(part)
        partial = lax.dot_general(
            jnp.concatenate(parts, axis=1),
            jnp.concatenate([m for m in members for _ in range(3)], axis=1),
            (((1,), (1,)), ((), ())),
            preferred_element_type=jnp.float32,
        )
        own_q = doc_ref.shape[1]
        for k in range(doc_ref.shape[0]):
            doc_ref[k] = partial[k * own_q : (k + 1) * own_q]

    if steps == 1:
        finish()
    else:
        pl.when(step == steps - 1)(finish)


def score(me, lengths, valid, own, other, products, split, own_q, steps):
    rows, wide = own.shape
    docs = lengths.shape[0]
    count = 4 * products.shape[0] // wide
    if steps == 1:
        grid = {"in_specs": [SMEM] * 3 + [VMEM] * 3, "out_specs": (VMEM,) * 3}
    else:
        block = (products.shape[0] // steps, products.shape[1])
        grid = {
            "grid": (steps,),
            "in_specs": [SMEM] * 3 + [VMEM] * 2 + [pl.BlockSpec(block, lambda s: (s, 0))],
            "out_specs": (VMEM,) * 3,
        }
    return pl.pallas_call(
        functools.partial(score_kernel, steps, split),
        out_shape=(
            jax.ShapeDtypeStruct((count, rows), jnp.float32),
            jax.ShapeDtypeStruct((count, rows), jnp.float32),
            jax.ShapeDtypeStruct((count // own_q, own_q, docs), jnp.float32),
        ),
        scratch_shapes=[pltpu.VMEM((wide, rows), jnp.float32)],
        compiler_params=pltpu.CompilerParams(vmem_limit_bytes=32 * MIB),
        cost_estimate=pl.CostEstimate(
            flops=2 * products.shape[0] * products.shape[1],
            bytes_accessed=4 * products.shape[0] * products.shape[1],
            transcendentals=0,
        ),
        **grid,
    )(me, lengths, valid, own, other, products)


def place_kernel(place, split, me_ref, own_ref, other_ref, out_ref, turned_ref):
    own_q = own_ref.shape[0] // len(place)
    for r, ref in enumerate((own_ref, other_ref)):
        for k, offset in enumerate(place):
            spot = pl.multiple_of((me_ref[0] ^ offset ^ (split * r)) * own_q, own_q)
            turned_ref[pl.ds(spot, own_q)] = ref[k * own_q : (k + 1) * own_q]
    out_ref[...] = turned_ref[...].T


def place_tokens(me, own, other, place, split):
    count, rows = own.shape
    return pl.pallas_call(
        functools.partial(place_kernel, place, split),
        in_specs=[SMEM, VMEM, VMEM],
        out_specs=VMEM,
        out_shape=jax.ShapeDtypeStruct((rows, 2 * count), jnp.float32),
        scratch_shapes=[pltpu.VMEM((2 * count, rows), jnp.float32)],
        compiler_params=pltpu.CompilerParams(vmem_limit_bytes=16 * MIB),
    )(me, own, other)


def offset_of(number, bits):
    last_bit = len(bits) - 1
    return functools.reduce(
        operator.xor, [bit for k, bit in enumerate(bits) if (number >> (last_bit - k)) & 1], 0
    )


def body(size, activations, out_grads, proj_in, proj_out, queries, doc_length, valid_count):
    rows = activations.shape[0]
    width = proj_in.shape[1]
    own_q = queries.shape[0]
    me = lax.axis_index("seq").astype(jnp.int32)[None]
    split = size // 2 + 1
    middle = [(1 << k) + 1 for k in range(1, size.bit_length() - 2)]

    proj = proj_out.T
    spots = [offset_of(m, middle) ^ (split * r) for m in range(size // 4) for r in range(2)]
    theirs, table = grad_blocks(me, proj, out_grads, rows, [s ^ 1 for s in spots])
    from_core = swap(theirs, 1, size)
    panel = queries
    got = swap(panel, middle[-1], size)
    sums = grad_blocks(me, proj, out_grads, rows, spots, table) + from_core
    late, _ = lax.optimization_barrier((proj_in, sums))
    got, sums = lax.optimization_barrier((got, sums))
    for k, bit in enumerate(middle):
        half = sums.shape[0] // 2
        kind = jnp.bfloat16 if k == 0 else jnp.float32
        sent = swap(sums[half:].astype(kind), bit, size)
        sums = sums[:half] + sent.astype(jnp.float32)
        if k == 0:
            after = sums
    own = sums[0]
    across = swap(own.astype(jnp.bfloat16), split, size)
    act = lax.dot_general(
        late, activations, (((0,), (1,)), ((), ())), preferred_element_type=jnp.float32
    )
    early, _ = lax.optimization_barrier((act, after))
    more_act, _ = lax.optimization_barrier((swap(early, split, size), own))
    act = jnp.stack([act, more_act])

    panel = jnp.concatenate([panel, got], axis=0)
    place = [0, middle[-1]]
    for bit in middle[-2::-1]:
        panel = jnp.concatenate([panel, swap(panel, bit, size)], axis=0)
        place = place + [p ^ bit for p in place]
    panels = [panel, swap(panel, 1, size)]
    place = tuple(place + [p ^ 1 for p in place])

    steps = max(1, 4 * width * size * own_q * rows // (4 * MIB))
    products = inner(act, panels, steps)
    mine, theirs, doc = score(
        me, doc_length, valid_count, own, across, products, split, own_q, steps
    )
    others = swap(theirs, split, size)
    bits = [1] + middle
    for bit in bits[:-1]:
        half = doc.shape[0] // 2
        doc = doc[:half] + swap(doc[half:], bit, size)
    more = swap(doc[1:], bits[-1], size)
    token_scores = place_tokens(me, mine, others, place, split)
    more, token_scores = lax.optimization_barrier((more, token_scores))
    scale = 1.0 / jnp.sqrt(jnp.minimum(valid_count, doc_length).astype(jnp.float32))
    return (token_scores, ((doc[0] + more[0]) * scale[None, :]).T)


def solution(mesh):
    size = mesh.shape["seq"]
    placed = (
        P(("groups", "seq"), None),
        P("groups", "seq"),
        P(),
        P("seq", None),
        P("seq", None),
        P("groups"),
        P("groups"),
    )
    return jax.shard_map(
        functools.partial(body, size),
        mesh=mesh,
        in_specs=placed,
        out_specs=(P(("groups", "seq"), None), P("groups", "seq")),
        check_vma=False,
    )
```

```python
import functools
import operator

import jax
import jax.numpy as jnp
from jax import lax
from jax.experimental import pallas as pl
from jax.experimental.pallas import tpu as pltpu
from jax.sharding import PartitionSpec as P

MIB = 1 << 20
SMEM = pl.BlockSpec(memory_space=pltpu.SMEM)
VMEM = pl.BlockSpec(memory_space=pltpu.VMEM)
HBM = pl.BlockSpec(memory_space=pltpu.HBM)


def swap(value, offset, size):
    return lax.ppermute(value, "seq", [(i, i ^ offset) for i in range(size)])


def grad_kernel(offsets, me_ref, proj_ref, grads_ref, out_ref, table, proj_buf, grads_buf, proj_sem, sems):
    load = pltpu.make_async_copy(proj_ref, proj_buf, proj_sem)
    load.start()
    halves, total, depth = grads_buf.shape
    count = len(offsets) // halves
    rows = total // count
    copies = []
    for k, offset in enumerate(offsets):
        first = pl.multiple_of((me_ref[0] ^ offset) * rows, rows)
        copy = pltpu.make_async_copy(
            grads_ref.at[pl.ds(first, rows)],
            grads_buf.at[k % halves, pl.ds((k // halves) * rows, rows)],
            sems.at[k],
        )
        copy.start(priority=k % 2)
        copies.append(copy)
    load.wait()
    turned = proj_buf[...].T
    none = jnp.zeros_like(turned)
    for r in range(halves):
        table[r] = jnp.concatenate([turned if c == r else none for c in range(halves)], axis=1)
    for k in range(count):
        made = None
        for r in range(halves):
            copies[k * halves + r].wait()
            part = jnp.dot(
                grads_buf[r, k * rows : (k + 1) * rows],
                table[r],
                preferred_element_type=jnp.float32,
            )
            made = part if made is None else made + part
        out_ref[k] = made


def held_kernel(offsets, me_ref, table, grads_ref, out_ref):
    halves = table.shape[0]
    count, rows, _ = out_ref.shape
    for k in range(0, count, 2):
        made = None
        for r in range(halves):
            left = []
            for offset in (offsets[k * halves + r], offsets[(k + 1) * halves + r]):
                first = pl.multiple_of((me_ref[0] ^ offset) * rows, rows)
                left.append(grads_ref[pl.ds(first, rows)])
            part = jnp.dot(
                jnp.concatenate(left, axis=0), table[r], preferred_element_type=jnp.float32
            )
            made = part if made is None else made + part
        out_ref[k] = made[:rows]
        out_ref[k + 1] = made[rows:]


def grad_blocks(me, proj, out_grads, rows, offsets, table=None):
    width, depth = proj.shape
    count = len(offsets) // 2
    made = jax.ShapeDtypeStruct((count, rows, 2 * width), jnp.float32)
    shared = dict(
        compiler_params=pltpu.CompilerParams(vmem_limit_bytes=24 * MIB),
        cost_estimate=pl.CostEstimate(
            flops=4 * count * rows * depth * width,
            bytes_accessed=4 * count * rows * depth,
            transcendentals=0,
        ),
    )
    if table is not None:
        return pl.pallas_call(
            functools.partial(held_kernel, offsets),
            in_specs=[SMEM, VMEM, VMEM],
            out_specs=VMEM,
            out_shape=made,
            **shared,
        )(me, table, out_grads)
    return pl.pallas_call(
        functools.partial(grad_kernel, offsets),
        in_specs=[SMEM, HBM, HBM],
        out_specs=(VMEM, VMEM),
        out_shape=(made, jax.ShapeDtypeStruct((2, depth, 2 * width), jnp.bfloat16)),
        scratch_shapes=[
            pltpu.VMEM((width, depth), jnp.bfloat16),
            pltpu.VMEM((2, count * rows, depth), jnp.bfloat16),
            pltpu.SemaphoreType.DMA,
            pltpu.SemaphoreType.DMA((2 * count,)),
        ],
        **shared,
    )(
        me,
        pltpu.with_memory_space_constraint(proj, pltpu.HBM),
        pltpu.with_memory_space_constraint(out_grads, pltpu.HBM),
    )


def act_kernel(pieces, proj_ref, rows_ref, out_ref, rows_buf, sems):
    depth = rows_ref.shape[1] // pieces
    copies = []
    for k in range(pieces):
        copy = pltpu.make_async_copy(
            rows_ref.at[:, pl.ds(k * depth, depth)], rows_buf.at[k], sems.at[k]
        )
        copy.start(priority=k % 2)
        copies.append(copy)
    total = None
    for k in range(pieces):
        copies[k].wait()
        part = lax.dot_general(
            proj_ref[:, k * depth : (k + 1) * depth],
            rows_buf[k],
            (((1,), (1,)), ((), ())),
            preferred_element_type=jnp.float32,
        )
        total = part if total is None else total + part
    out_ref[...] = total


def act_blocks(proj, activations):
    width, depth = proj.shape
    rows = activations.shape[0]
    pieces = 8
    return pl.pallas_call(
        functools.partial(act_kernel, pieces),
        in_specs=[VMEM, HBM],
        out_specs=VMEM,
        out_shape=jax.ShapeDtypeStruct((width, rows), jnp.float32),
        scratch_shapes=[
            pltpu.VMEM((pieces, rows, depth // pieces), jnp.bfloat16),
            pltpu.SemaphoreType.DMA((pieces,)),
        ],
        compiler_params=pltpu.CompilerParams(vmem_limit_bytes=24 * MIB),
        cost_estimate=pl.CostEstimate(
            flops=2 * width * rows * depth, bytes_accessed=2 * rows * depth, transcendentals=0
        ),
    )(proj, pltpu.with_memory_space_constraint(activations, pltpu.HBM))


def inner_kernel(pieces, act_ref, *refs):
    out_ref = refs[pieces]
    columns = []
    for r in range(act_ref.shape[0]):
        act = act_ref[r]
        high = act.astype(jnp.bfloat16)
        low = (act - high.astype(jnp.float32)).astype(jnp.bfloat16)
        none = jnp.zeros_like(high)
        columns.append(jnp.concatenate([high, none, low, none], axis=0))
        columns.append(jnp.concatenate([none, high, none, low], axis=0))
    table = jnp.concatenate(columns, axis=1)
    pair = 2 * act_ref.shape[1]
    rows = []
    for k in range(refs[0].shape[1] // pair):
        for ref in refs[:pieces]:
            rows.append(ref[:, k * pair : (k + 1) * pair])
    left = jnp.concatenate(rows, axis=0)
    left = jnp.concatenate([left, left], axis=1)
    out_ref[...] = jnp.dot(left, table, preferred_element_type=jnp.float32)


def inner(act, panels, steps):
    halves, width, rows = act.shape
    count = sum(p.shape[0] for p in panels)
    pairs = panels[0].shape[1] // (2 * width)
    total = pairs * count
    if steps == 1:
        grid = {"in_specs": [VMEM] * (1 + len(panels)), "out_specs": VMEM}
    else:
        grid = {
            "grid": (steps,),
            "in_specs": [VMEM]
            + [pl.BlockSpec((p.shape[0], p.shape[1] // steps), lambda s: (0, s)) for p in panels],
            "out_specs": pl.BlockSpec((total // steps, 2 * halves * rows), lambda s: (s, 0)),
        }
    return pl.pallas_call(
        functools.partial(inner_kernel, len(panels)),
        out_shape=jax.ShapeDtypeStruct((total, 2 * halves * rows), jnp.float32),
        compiler_params=pltpu.CompilerParams(vmem_limit_bytes=32 * MIB),
        cost_estimate=pl.CostEstimate(
            flops=16 * total * width * halves * rows,
            bytes_accessed=8 * total * halves * rows,
            transcendentals=0,
        ),
        **grid,
    )(act, *panels)


def score_kernel(
    steps, split, me_ref, length_ref, valid_ref, own_ref, other_ref, inner_ref, own_tok, other_tok, doc_ref, grad_ref
):
    rows, wide = own_ref.shape
    halves, width = 2, wide // 2
    count = own_tok.shape[0]
    pairs = inner_ref.shape[0] // count
    step = pl.program_id(0) if steps > 1 else 0
    tokens = (own_tok, other_tok)

    def begin():
        other = other_ref[...].astype(jnp.float32).T
        grad_ref[...] = own_ref[...].T + jnp.concatenate([other[width:], other[:width]], axis=0)

    if steps == 1:
        begin()
    else:
        pl.when(step == 0)(begin)

    for r in range(halves):
        total = None
        for k in range(pairs):
            for parity in range(2):
                feature = 2 * k + parity
                if steps == 1:
                    line = grad_ref[r * width + feature : r * width + feature + 1]
                else:
                    line = grad_ref[pl.ds(r * width + 2 * pairs * step + feature, 1)]
                column = (2 * r + parity) * rows
                term = line * inner_ref[k * count : (k + 1) * count, column : column + rows]
                total = term if total is None else total + term
        if steps == 1:
            tokens[r][...] = total
        else:
            tokens[r][...] = jnp.where(step == 0, total, tokens[r][...] + total)

    def finish():
        me = me_ref[0]
        docs = length_ref.shape[0]
        doc_of = lax.broadcasted_iota(jnp.int32, (docs, rows), 0)
        lower = jnp.zeros((docs, rows), jnp.int32)
        upper = jnp.zeros((docs, rows), jnp.int32)
        start = jnp.int32(0)
        for d in range(docs):
            lower = jnp.where(doc_of == d, start, lower)
            used = jnp.minimum(valid_ref[d], length_ref[d])
            upper = jnp.where(doc_of == d, start + used, upper)
            start = start + length_ref[d]
        members, parts = [], []
        for r in range(halves):
            token = (me ^ (split * r)) * rows + lax.broadcasted_iota(jnp.int32, (docs, rows), 1)
            inside = (token >= lower) & (token < upper)
            members.append(jnp.where(inside, 1.0, 0.0).astype(jnp.bfloat16))
            left = tokens[r][...]
            for _ in range(3):
                part = left.astype(jnp.bfloat16)
                left = left - part.astype(jnp.float32)
                parts.append(part)
        partial = lax.dot_general(
            jnp.concatenate(parts, axis=1),
            jnp.concatenate([m for m in members for _ in range(3)], axis=1),
            (((1,), (1,)), ((), ())),
            preferred_element_type=jnp.float32,
        )
        own_q = doc_ref.shape[1]
        for k in range(doc_ref.shape[0]):
            doc_ref[k] = partial[k * own_q : (k + 1) * own_q]

    if steps == 1:
        finish()
    else:
        pl.when(step == steps - 1)(finish)


def score(me, lengths, valid, own, other, products, split, own_q, steps):
    rows, wide = own.shape
    docs = lengths.shape[0]
    count = 4 * products.shape[0] // wide
    if steps == 1:
        grid = {"in_specs": [SMEM] * 3 + [VMEM] * 3, "out_specs": (VMEM,) * 3}
    else:
        block = (products.shape[0] // steps, products.shape[1])
        grid = {
            "grid": (steps,),
            "in_specs": [SMEM] * 3 + [VMEM] * 2 + [pl.BlockSpec(block, lambda s: (s, 0))],
            "out_specs": (VMEM,) * 3,
        }
    return pl.pallas_call(
        functools.partial(score_kernel, steps, split),
        out_shape=(
            jax.ShapeDtypeStruct((count, rows), jnp.float32),
            jax.ShapeDtypeStruct((count, rows), jnp.float32),
            jax.ShapeDtypeStruct((count // own_q, own_q, docs), jnp.float32),
        ),
        scratch_shapes=[pltpu.VMEM((wide, rows), jnp.float32)],
        compiler_params=pltpu.CompilerParams(vmem_limit_bytes=32 * MIB),
        cost_estimate=pl.CostEstimate(
            flops=2 * products.shape[0] * products.shape[1],
            bytes_accessed=4 * products.shape[0] * products.shape[1],
            transcendentals=0,
        ),
        **grid,
    )(me, lengths, valid, own, other, products)


def place_kernel(place, split, me_ref, own_ref, other_ref, out_ref, turned_ref):
    own_q = own_ref.shape[0] // len(place)
    for r, ref in enumerate((own_ref, other_ref)):
        for k, offset in enumerate(place):
            spot = pl.multiple_of((me_ref[0] ^ offset ^ (split * r)) * own_q, own_q)
            turned_ref[pl.ds(spot, own_q)] = ref[k * own_q : (k + 1) * own_q]
    out_ref[...] = turned_ref[...].T


def place_tokens(me, own, other, place, split):
    count, rows = own.shape
    return pl.pallas_call(
        functools.partial(place_kernel, place, split),
        in_specs=[SMEM, VMEM, VMEM],
        out_specs=VMEM,
        out_shape=jax.ShapeDtypeStruct((rows, 2 * count), jnp.float32),
        scratch_shapes=[pltpu.VMEM((2 * count, rows), jnp.float32)],
        compiler_params=pltpu.CompilerParams(vmem_limit_bytes=16 * MIB),
    )(me, own, other)


def offset_of(number, bits):
    last_bit = len(bits) - 1
    return functools.reduce(
        operator.xor, [bit for k, bit in enumerate(bits) if (number >> (last_bit - k)) & 1], 0
    )


def body(size, activations, out_grads, proj_in, proj_out, queries, doc_length, valid_count):
    rows = activations.shape[0]
    width = proj_in.shape[1]
    own_q = queries.shape[0]
    me = lax.axis_index("seq").astype(jnp.int32)[None]
    split = size // 2 + 1
    middle = [(1 << k) + 1 for k in range(1, size.bit_length() - 2)]

    proj = proj_out.T
    spots = [offset_of(m, middle) ^ (split * r) for m in range(size // 4) for r in range(2)]
    theirs, table = grad_blocks(me, proj, out_grads, rows, [s ^ 1 for s in spots])
    from_core = swap(theirs, 1, size)
    panel = queries
    got = swap(panel, middle[-1], size)
    sums = grad_blocks(me, proj, out_grads, rows, spots, table) + from_core
    late, _ = lax.optimization_barrier((proj_in, sums))
    got, sums = lax.optimization_barrier((got, sums))
    for k, bit in enumerate(middle):
        half = sums.shape[0] // 2
        sent = swap(sums[half:].astype(jnp.bfloat16), bit, size)
        sums = sums[:half] + sent.astype(jnp.float32)
        if k == 0:
            after = sums
    own = sums[0]
    across = swap(own.astype(jnp.bfloat16), split, size)
    act = act_blocks(late.T, activations)
    early, _ = lax.optimization_barrier((act, after))
    more_act, _ = lax.optimization_barrier((swap(early, split, size), own))
    act = jnp.stack([act, more_act])

    panel = jnp.concatenate([panel, got], axis=0)
    place = [0, middle[-1]]
    for bit in middle[-2::-1]:
        panel = jnp.concatenate([panel, swap(panel, bit, size)], axis=0)
        place = place + [p ^ bit for p in place]
    panels = [panel, swap(panel, 1, size)]
    place = tuple(place + [p ^ 1 for p in place])

    steps = max(1, 4 * width * size * own_q * rows // (4 * MIB))
    products = inner(act, panels, steps)
    mine, theirs, doc = score(
        me, doc_length, valid_count, own, across, products, split, own_q, steps
    )
    others = swap(theirs, split, size)
    bits = [1] + middle
    for bit in bits[:-1]:
        half = doc.shape[0] // 2
        doc = doc[:half] + swap(doc[half:], bit, size)
    more = swap(doc[1:], bits[-1], size)
    token_scores = place_tokens(me, mine, others, place, split)
    more, token_scores = lax.optimization_barrier((more, token_scores))
    scale = 1.0 / jnp.sqrt(jnp.minimum(valid_count, doc_length).astype(jnp.float32))
    return (token_scores, ((doc[0] + more[0]) * scale[None, :]).T)


def solution(mesh):
    size = mesh.shape["seq"]
    placed = (
        P(("groups", "seq"), None),
        P("groups", "seq"),
        P(),
        P("seq", None),
        P("seq", None),
        P("groups"),
        P("groups"),
    )
    return jax.shard_map(
        functools.partial(body, size),
        mesh=mesh,
        in_specs=placed,
        out_specs=(P(("groups", "seq"), None), P("groups", "seq")),
        check_vma=False,
    )
```

```python
import functools
import operator

import jax
import jax.numpy as jnp
from jax import lax
from jax.experimental import pallas as pl
from jax.experimental.pallas import tpu as pltpu
from jax.sharding import PartitionSpec as P

MIB = 1 << 20
SMEM = pl.BlockSpec(memory_space=pltpu.SMEM)
VMEM = pl.BlockSpec(memory_space=pltpu.VMEM)
HBM = pl.BlockSpec(memory_space=pltpu.HBM)


def swap(value, offset, size):
    return lax.ppermute(value, "seq", [(i, i ^ offset) for i in range(size)])


def grad_kernel(offsets, me_ref, proj_ref, grads_ref, out_ref, table, proj_buf, grads_buf, proj_sem, sems):
    load = pltpu.make_async_copy(proj_ref, proj_buf, proj_sem)
    load.start()
    halves, total, depth = grads_buf.shape
    count = len(offsets) // halves
    rows = total // count
    copies = []
    for k, offset in enumerate(offsets):
        first = pl.multiple_of((me_ref[0] ^ offset) * rows, rows)
        copy = pltpu.make_async_copy(
            grads_ref.at[pl.ds(first, rows)],
            grads_buf.at[k % halves, pl.ds((k // halves) * rows, rows)],
            sems.at[k],
        )
        copy.start(priority=k % 2)
        copies.append(copy)
    load.wait()
    turned = proj_buf[...].T
    none = jnp.zeros_like(turned)
    for r in range(halves):
        table[r] = jnp.concatenate([turned if c == r else none for c in range(halves)], axis=1)
    for k in range(count):
        made = None
        for r in range(halves):
            copies[k * halves + r].wait()
            part = jnp.dot(
                grads_buf[r, k * rows : (k + 1) * rows],
                table[r],
                preferred_element_type=jnp.float32,
            )
            made = part if made is None else made + part
        out_ref[k] = made


def held_kernel(offsets, me_ref, table, grads_ref, out_ref):
    halves = table.shape[0]
    count, rows, _ = out_ref.shape
    for k in range(0, count, 2):
        made = None
        for r in range(halves):
            left = []
            for offset in (offsets[k * halves + r], offsets[(k + 1) * halves + r]):
                first = pl.multiple_of((me_ref[0] ^ offset) * rows, rows)
                left.append(grads_ref[pl.ds(first, rows)])
            part = jnp.dot(
                jnp.concatenate(left, axis=0), table[r], preferred_element_type=jnp.float32
            )
            made = part if made is None else made + part
        out_ref[k] = made[:rows]
        out_ref[k + 1] = made[rows:]


def grad_blocks(me, proj, out_grads, rows, offsets, table=None):
    width, depth = proj.shape
    count = len(offsets) // 2
    made = jax.ShapeDtypeStruct((count, rows, 2 * width), jnp.float32)
    shared = dict(
        compiler_params=pltpu.CompilerParams(vmem_limit_bytes=24 * MIB),
        cost_estimate=pl.CostEstimate(
            flops=4 * count * rows * depth * width,
            bytes_accessed=4 * count * rows * depth,
            transcendentals=0,
        ),
    )
    if table is not None:
        return pl.pallas_call(
            functools.partial(held_kernel, offsets),
            in_specs=[SMEM, VMEM, VMEM],
            out_specs=VMEM,
            out_shape=made,
            **shared,
        )(me, table, out_grads)
    return pl.pallas_call(
        functools.partial(grad_kernel, offsets),
        in_specs=[SMEM, HBM, HBM],
        out_specs=(VMEM, VMEM),
        out_shape=(made, jax.ShapeDtypeStruct((2, depth, 2 * width), jnp.bfloat16)),
        scratch_shapes=[
            pltpu.VMEM((width, depth), jnp.bfloat16),
            pltpu.VMEM((2, count * rows, depth), jnp.bfloat16),
            pltpu.SemaphoreType.DMA,
            pltpu.SemaphoreType.DMA((2 * count,)),
        ],
        **shared,
    )(
        me,
        pltpu.with_memory_space_constraint(proj, pltpu.HBM),
        pltpu.with_memory_space_constraint(out_grads, pltpu.HBM),
    )


def inner_kernel(pieces, act_ref, *refs):
    out_ref = refs[pieces]
    columns = []
    for r in range(act_ref.shape[0]):
        act = act_ref[r]
        high = act.astype(jnp.bfloat16)
        low = (act - high.astype(jnp.float32)).astype(jnp.bfloat16)
        none = jnp.zeros_like(high)
        columns.append(jnp.concatenate([high, none, low, none], axis=0))
        columns.append(jnp.concatenate([none, high, none, low], axis=0))
    table = jnp.concatenate(columns, axis=1)
    pair = 2 * act_ref.shape[1]
    rows = []
    for k in range(refs[0].shape[1] // pair):
        for ref in refs[:pieces]:
            rows.append(ref[:, k * pair : (k + 1) * pair])
    left = jnp.concatenate(rows, axis=0)
    left = jnp.concatenate([left, left], axis=1)
    out_ref[...] = jnp.dot(left, table, preferred_element_type=jnp.float32)


def inner(act, panels, steps):
    halves, width, rows = act.shape
    count = sum(p.shape[0] for p in panels)
    pairs = panels[0].shape[1] // (2 * width)
    total = pairs * count
    if steps == 1:
        grid = {"in_specs": [VMEM] * (1 + len(panels)), "out_specs": VMEM}
    else:
        grid = {
            "grid": (steps,),
            "in_specs": [VMEM]
            + [pl.BlockSpec((p.shape[0], p.shape[1] // steps), lambda s: (0, s)) for p in panels],
            "out_specs": pl.BlockSpec((total // steps, 2 * halves * rows), lambda s: (s, 0)),
        }
    return pl.pallas_call(
        functools.partial(inner_kernel, len(panels)),
        out_shape=jax.ShapeDtypeStruct((total, 2 * halves * rows), jnp.float32),
        compiler_params=pltpu.CompilerParams(vmem_limit_bytes=32 * MIB),
        cost_estimate=pl.CostEstimate(
            flops=16 * total * width * halves * rows,
            bytes_accessed=8 * total * halves * rows,
            transcendentals=0,
        ),
        **grid,
    )(act, *panels)


def score_kernel(
    steps, split, me_ref, length_ref, valid_ref, own_ref, other_ref, inner_ref, own_tok, other_tok, doc_ref, grad_ref
):
    rows, wide = own_ref.shape
    halves, width = 2, wide // 2
    count = own_tok.shape[0]
    pairs = inner_ref.shape[0] // count
    step = pl.program_id(0) if steps > 1 else 0
    tokens = (own_tok, other_tok)

    def begin():
        other = other_ref[...].astype(jnp.float32).T
        grad_ref[...] = own_ref[...].T + jnp.concatenate([other[width:], other[:width]], axis=0)

    if steps == 1:
        begin()
    else:
        pl.when(step == 0)(begin)

    for r in range(halves):
        total = None
        for k in range(pairs):
            for parity in range(2):
                feature = 2 * k + parity
                if steps == 1:
                    line = grad_ref[r * width + feature : r * width + feature + 1]
                else:
                    line = grad_ref[pl.ds(r * width + 2 * pairs * step + feature, 1)]
                column = (2 * r + parity) * rows
                term = line * inner_ref[k * count : (k + 1) * count, column : column + rows]
                total = term if total is None else total + term
        if steps == 1:
            tokens[r][...] = total
        else:
            tokens[r][...] = jnp.where(step == 0, total, tokens[r][...] + total)

    def finish():
        me = me_ref[0]
        docs = length_ref.shape[0]
        doc_of = lax.broadcasted_iota(jnp.int32, (docs, rows), 0)
        lower = jnp.zeros((docs, rows), jnp.int32)
        upper = jnp.zeros((docs, rows), jnp.int32)
        start = jnp.int32(0)
        for d in range(docs):
            lower = jnp.where(doc_of == d, start, lower)
            used = jnp.minimum(valid_ref[d], length_ref[d])
            upper = jnp.where(doc_of == d, start + used, upper)
            start = start + length_ref[d]
        members, parts = [], []
        for r in range(halves):
            token = (me ^ (split * r)) * rows + lax.broadcasted_iota(jnp.int32, (docs, rows), 1)
            inside = (token >= lower) & (token < upper)
            members.append(jnp.where(inside, 1.0, 0.0).astype(jnp.bfloat16))
            left = tokens[r][...]
            for _ in range(3):
                part = left.astype(jnp.bfloat16)
                left = left - part.astype(jnp.float32)
                parts.append(part)
        partial = lax.dot_general(
            jnp.concatenate(parts, axis=1),
            jnp.concatenate([m for m in members for _ in range(3)], axis=1),
            (((1,), (1,)), ((), ())),
            preferred_element_type=jnp.float32,
        )
        own_q = doc_ref.shape[1]
        for k in range(doc_ref.shape[0]):
            doc_ref[k] = partial[k * own_q : (k + 1) * own_q]

    if steps == 1:
        finish()
    else:
        pl.when(step == steps - 1)(finish)


def score(me, lengths, valid, own, other, products, split, own_q, steps):
    rows, wide = own.shape
    docs = lengths.shape[0]
    count = 4 * products.shape[0] // wide
    if steps == 1:
        grid = {"in_specs": [SMEM] * 3 + [VMEM] * 3, "out_specs": (VMEM,) * 3}
    else:
        block = (products.shape[0] // steps, products.shape[1])
        grid = {
            "grid": (steps,),
            "in_specs": [SMEM] * 3 + [VMEM] * 2 + [pl.BlockSpec(block, lambda s: (s, 0))],
            "out_specs": (VMEM,) * 3,
        }
    return pl.pallas_call(
        functools.partial(score_kernel, steps, split),
        out_shape=(
            jax.ShapeDtypeStruct((count, rows), jnp.float32),
            jax.ShapeDtypeStruct((count, rows), jnp.float32),
            jax.ShapeDtypeStruct((count // own_q, own_q, docs), jnp.float32),
        ),
        scratch_shapes=[pltpu.VMEM((wide, rows), jnp.float32)],
        compiler_params=pltpu.CompilerParams(vmem_limit_bytes=32 * MIB),
        cost_estimate=pl.CostEstimate(
            flops=2 * products.shape[0] * products.shape[1],
            bytes_accessed=4 * products.shape[0] * products.shape[1],
            transcendentals=0,
        ),
        **grid,
    )(me, lengths, valid, own, other, products)


def place_kernel(place, split, me_ref, own_ref, other_ref, out_ref, turned_ref):
    own_q = own_ref.shape[0] // len(place)
    for r, ref in enumerate((own_ref, other_ref)):
        for k, offset in enumerate(place):
            spot = pl.multiple_of((me_ref[0] ^ offset ^ (split * r)) * own_q, own_q)
            turned_ref[pl.ds(spot, own_q)] = ref[k * own_q : (k + 1) * own_q]
    out_ref[...] = turned_ref[...].T


def place_tokens(me, own, other, place, split):
    count, rows = own.shape
    return pl.pallas_call(
        functools.partial(place_kernel, place, split),
        in_specs=[SMEM, VMEM, VMEM],
        out_specs=VMEM,
        out_shape=jax.ShapeDtypeStruct((rows, 2 * count), jnp.float32),
        scratch_shapes=[pltpu.VMEM((2 * count, rows), jnp.float32)],
        compiler_params=pltpu.CompilerParams(vmem_limit_bytes=16 * MIB),
    )(me, own, other)


def offset_of(number, bits):
    last_bit = len(bits) - 1
    return functools.reduce(
        operator.xor, [bit for k, bit in enumerate(bits) if (number >> (last_bit - k)) & 1], 0
    )


def body(size, activations, out_grads, proj_in, proj_out, queries, doc_length, valid_count):
    rows = activations.shape[0]
    width = proj_in.shape[1]
    own_q = queries.shape[0]
    me = lax.axis_index("seq").astype(jnp.int32)[None]
    split = size // 2 + 1
    middle = [(1 << k) + 1 for k in range(1, size.bit_length() - 2)]

    proj = proj_out.T
    spots = [offset_of(m, middle) ^ (split * r) for m in range(size // 4) for r in range(2)]
    theirs, table = grad_blocks(me, proj, out_grads, rows, [s ^ 1 for s in spots])
    from_core = swap(theirs, 1, size)
    panel = queries
    got = swap(panel, middle[-1], size)
    sums = grad_blocks(me, proj, out_grads, rows, spots, table) + from_core
    late, _ = lax.optimization_barrier((proj_in, sums))
    got, sums = lax.optimization_barrier((got, sums))
    for k, bit in enumerate(middle):
        half = sums.shape[0] // 2
        sent = swap(sums[half:].astype(jnp.bfloat16), bit, size)
        sums = sums[:half] + sent.astype(jnp.float32)
        if k == 0:
            after = sums
    own = sums[0]
    across = swap(own.astype(jnp.bfloat16), split, size)
    act = lax.dot_general(
        late, activations, (((0,), (1,)), ((), ())), preferred_element_type=jnp.float32
    )
    early, _ = lax.optimization_barrier((act, after))
    more_act, _ = lax.optimization_barrier((swap(early, split, size), own))
    act = jnp.stack([act, more_act])

    panel = jnp.concatenate([panel, got], axis=0)
    place = [0, middle[-1]]
    for bit in middle[-2::-1]:
        panel = jnp.concatenate([panel, swap(panel, bit, size)], axis=0)
        place = place + [p ^ bit for p in place]
    panels = [panel, swap(panel, 1, size)]
    place = tuple(place + [p ^ 1 for p in place])

    steps = max(1, 4 * width * size * own_q * rows // (4 * MIB))
    products = inner(act, panels, steps)
    mine, theirs, doc = score(
        me, doc_length, valid_count, own, across, products, split, own_q, steps
    )
    others = swap(theirs, split, size)
    bits = [1] + middle
    for bit in bits[:-1]:
        half = doc.shape[0] // 2
        doc = doc[:half] + swap(doc[half:], bit, size)
    more = swap(doc[1:], bits[-1], size)
    token_scores = place_tokens(me, mine, others, place, split)
    more, token_scores = lax.optimization_barrier((more, token_scores))
    scale = 1.0 / jnp.sqrt(jnp.minimum(valid_count, doc_length).astype(jnp.float32))
    return (token_scores, ((doc[0] + more[0]) * scale[None, :]).T)


def solution(mesh):
    size = mesh.shape["seq"]
    placed = (
        P(("groups", "seq"), None),
        P("groups", "seq"),
        P(),
        P("seq", None),
        P("seq", None),
        P("groups"),
        P("groups"),
    )
    return jax.shard_map(
        functools.partial(body, size),
        mesh=mesh,
        in_specs=placed,
        out_specs=(P(("groups", "seq"), None), P("groups", "seq")),
        check_vma=False,
    )
```

```python
import functools
import operator

import jax
import jax.numpy as jnp
from jax import lax
from jax.experimental import pallas as pl
from jax.experimental.pallas import tpu as pltpu
from jax.sharding import PartitionSpec as P

MIB = 1 << 20
SMEM = pl.BlockSpec(memory_space=pltpu.SMEM)
VMEM = pl.BlockSpec(memory_space=pltpu.VMEM)
HBM = pl.BlockSpec(memory_space=pltpu.HBM)


def swap(value, offset, size):
    return lax.ppermute(value, "seq", [(i, i ^ offset) for i in range(size)])


def grad_kernel(offsets, me_ref, proj_ref, grads_ref, out_ref, table, proj_buf, grads_buf, proj_sem, sems):
    load = pltpu.make_async_copy(proj_ref, proj_buf, proj_sem)
    load.start()
    halves, total, depth = grads_buf.shape
    count = len(offsets) // halves
    rows = total // count
    copies = []
    for k, offset in enumerate(offsets):
        first = pl.multiple_of((me_ref[0] ^ offset) * rows, rows)
        copy = pltpu.make_async_copy(
            grads_ref.at[pl.ds(first, rows)],
            grads_buf.at[k % halves, pl.ds((k // halves) * rows, rows)],
            sems.at[k],
        )
        copy.start(priority=k % 2)
        copies.append(copy)
    load.wait()
    turned = proj_buf[...].T
    none = jnp.zeros_like(turned)
    for r in range(halves):
        table[r] = jnp.concatenate([turned if c == r else none for c in range(halves)], axis=1)
    for k in range(count):
        made = None
        for r in range(halves):
            copies[k * halves + r].wait()
            part = jnp.dot(
                grads_buf[r, k * rows : (k + 1) * rows],
                table[r],
                preferred_element_type=jnp.float32,
            )
            made = part if made is None else made + part
        out_ref[k] = made


def held_kernel(offsets, me_ref, table, grads_ref, out_ref):
    halves = table.shape[0]
    count, rows, _ = out_ref.shape
    for k in range(0, count, 2):
        made = None
        for r in range(halves):
            left = []
            for offset in (offsets[k * halves + r], offsets[(k + 1) * halves + r]):
                first = pl.multiple_of((me_ref[0] ^ offset) * rows, rows)
                left.append(grads_ref[pl.ds(first, rows)])
            part = jnp.dot(
                jnp.concatenate(left, axis=0), table[r], preferred_element_type=jnp.float32
            )
            made = part if made is None else made + part
        out_ref[k] = made[:rows]
        out_ref[k + 1] = made[rows:]


def grad_blocks(me, proj, out_grads, rows, offsets, table=None):
    width, depth = proj.shape
    count = len(offsets) // 2
    made = jax.ShapeDtypeStruct((count, rows, 2 * width), jnp.float32)
    shared = dict(
        compiler_params=pltpu.CompilerParams(vmem_limit_bytes=24 * MIB),
        cost_estimate=pl.CostEstimate(
            flops=4 * count * rows * depth * width,
            bytes_accessed=4 * count * rows * depth,
            transcendentals=0,
        ),
    )
    if table is not None:
        return pl.pallas_call(
            functools.partial(held_kernel, offsets),
            in_specs=[SMEM, VMEM, VMEM],
            out_specs=VMEM,
            out_shape=made,
            **shared,
        )(me, table, out_grads)
    return pl.pallas_call(
        functools.partial(grad_kernel, offsets),
        in_specs=[SMEM, HBM, HBM],
        out_specs=(VMEM, VMEM),
        out_shape=(made, jax.ShapeDtypeStruct((2, depth, 2 * width), jnp.bfloat16)),
        scratch_shapes=[
            pltpu.VMEM((width, depth), jnp.bfloat16),
            pltpu.VMEM((2, count * rows, depth), jnp.bfloat16),
            pltpu.SemaphoreType.DMA,
            pltpu.SemaphoreType.DMA((2 * count,)),
        ],
        **shared,
    )(
        me,
        pltpu.with_memory_space_constraint(proj, pltpu.HBM),
        pltpu.with_memory_space_constraint(out_grads, pltpu.HBM),
    )


def inner_kernel(pieces, act_ref, *refs):
    out_ref = refs[pieces]
    columns = []
    for r in range(act_ref.shape[0]):
        act = act_ref[r]
        high = act.astype(jnp.bfloat16)
        low = (act - high.astype(jnp.float32)).astype(jnp.bfloat16)
        none = jnp.zeros_like(high)
        columns.append(jnp.concatenate([high, none, low, none], axis=0))
        columns.append(jnp.concatenate([none, high, none, low], axis=0))
    table = jnp.concatenate(columns, axis=1)
    pair = 2 * act_ref.shape[1]
    rows = []
    for k in range(refs[0].shape[1] // pair):
        for ref in refs[:pieces]:
            rows.append(ref[:, k * pair : (k + 1) * pair])
    left = jnp.concatenate(rows, axis=0)
    left = jnp.concatenate([left, left], axis=1)
    out_ref[...] = jnp.dot(left, table, preferred_element_type=jnp.float32)


def inner(act, panels, steps):
    halves, width, rows = act.shape
    count = sum(p.shape[0] for p in panels)
    pairs = panels[0].shape[1] // (2 * width)
    total = pairs * count
    if steps == 1:
        grid = {"in_specs": [VMEM] * (1 + len(panels)), "out_specs": VMEM}
    else:
        grid = {
            "grid": (steps,),
            "in_specs": [VMEM]
            + [pl.BlockSpec((p.shape[0], p.shape[1] // steps), lambda s: (0, s)) for p in panels],
            "out_specs": pl.BlockSpec((total // steps, 2 * halves * rows), lambda s: (s, 0)),
        }
    return pl.pallas_call(
        functools.partial(inner_kernel, len(panels)),
        out_shape=jax.ShapeDtypeStruct((total, 2 * halves * rows), jnp.float32),
        compiler_params=pltpu.CompilerParams(vmem_limit_bytes=32 * MIB),
        cost_estimate=pl.CostEstimate(
            flops=16 * total * width * halves * rows,
            bytes_accessed=8 * total * halves * rows,
            transcendentals=0,
        ),
        **grid,
    )(act, *panels)


def score_kernel(
    steps, split, me_ref, length_ref, valid_ref, own_ref, other_ref, inner_ref, own_tok, other_tok, doc_ref, grad_ref
):
    rows, wide = own_ref.shape
    halves, width = 2, wide // 2
    count = own_tok.shape[0]
    pairs = inner_ref.shape[0] // count
    step = pl.program_id(0) if steps > 1 else 0
    tokens = (own_tok, other_tok)

    def begin():
        other = other_ref[...].astype(jnp.float32).T
        grad_ref[...] = own_ref[...].T + jnp.concatenate([other[width:], other[:width]], axis=0)

    if steps == 1:
        begin()
    else:
        pl.when(step == 0)(begin)

    for r in range(halves):
        total = None
        for k in range(pairs):
            for parity in range(2):
                feature = 2 * k + parity
                if steps == 1:
                    line = grad_ref[r * width + feature : r * width + feature + 1]
                else:
                    line = grad_ref[pl.ds(r * width + 2 * pairs * step + feature, 1)]
                column = (2 * r + parity) * rows
                term = line * inner_ref[k * count : (k + 1) * count, column : column + rows]
                total = term if total is None else total + term
        if steps == 1:
            tokens[r][...] = total
        else:
            tokens[r][...] = jnp.where(step == 0, total, tokens[r][...] + total)

    def finish():
        me = me_ref[0]
        docs = length_ref.shape[0]
        doc_of = lax.broadcasted_iota(jnp.int32, (docs, rows), 0)
        lower = jnp.zeros((docs, rows), jnp.int32)
        upper = jnp.zeros((docs, rows), jnp.int32)
        start = jnp.int32(0)
        for d in range(docs):
            lower = jnp.where(doc_of == d, start, lower)
            used = jnp.minimum(valid_ref[d], length_ref[d])
            upper = jnp.where(doc_of == d, start + used, upper)
            start = start + length_ref[d]
        members, parts = [], []
        for r in range(halves):
            token = (me ^ (split * r)) * rows + lax.broadcasted_iota(jnp.int32, (docs, rows), 1)
            inside = (token >= lower) & (token < upper)
            members.append(jnp.where(inside, 1.0, 0.0).astype(jnp.bfloat16))
            left = tokens[r][...]
            for _ in range(3):
                part = left.astype(jnp.bfloat16)
                left = left - part.astype(jnp.float32)
                parts.append(part)
        partial = lax.dot_general(
            jnp.concatenate(parts, axis=1),
            jnp.concatenate([m for m in members for _ in range(3)], axis=1),
            (((1,), (1,)), ((), ())),
            preferred_element_type=jnp.float32,
        )
        own_q = doc_ref.shape[1]
        for k in range(doc_ref.shape[0]):
            doc_ref[k] = partial[k * own_q : (k + 1) * own_q]

    if steps == 1:
        finish()
    else:
        pl.when(step == steps - 1)(finish)


def score(me, lengths, valid, own, other, products, split, own_q, steps):
    rows, wide = own.shape
    docs = lengths.shape[0]
    count = 4 * products.shape[0] // wide
    if steps == 1:
        grid = {"in_specs": [SMEM] * 3 + [VMEM] * 3, "out_specs": (VMEM,) * 3}
    else:
        block = (products.shape[0] // steps, products.shape[1])
        grid = {
            "grid": (steps,),
            "in_specs": [SMEM] * 3 + [VMEM] * 2 + [pl.BlockSpec(block, lambda s: (s, 0))],
            "out_specs": (VMEM,) * 3,
        }
    return pl.pallas_call(
        functools.partial(score_kernel, steps, split),
        out_shape=(
            jax.ShapeDtypeStruct((count, rows), jnp.float32),
            jax.ShapeDtypeStruct((count, rows), jnp.float32),
            jax.ShapeDtypeStruct((count // own_q, own_q, docs), jnp.float32),
        ),
        scratch_shapes=[pltpu.VMEM((wide, rows), jnp.float32)],
        compiler_params=pltpu.CompilerParams(vmem_limit_bytes=32 * MIB),
        cost_estimate=pl.CostEstimate(
            flops=2 * products.shape[0] * products.shape[1],
            bytes_accessed=4 * products.shape[0] * products.shape[1],
            transcendentals=0,
        ),
        **grid,
    )(me, lengths, valid, own, other, products)


def last_kernel(
    place, split, me_ref, length_ref, valid_ref, own_ref, other_ref, doc_ref, more_ref,
    token_out, doc_out, turned_ref, token_buf, doc_buf, sems,
):
    own_q, docs = doc_buf.shape
    for r, ref in enumerate((own_ref, other_ref)):
        for k, offset in enumerate(place):
            spot = pl.multiple_of((me_ref[0] ^ offset ^ (split * r)) * own_q, own_q)
            turned_ref[pl.ds(spot, own_q)] = ref[k * own_q : (k + 1) * own_q]
    token_buf[...] = turned_ref[...].T
    tokens = pltpu.make_async_copy(token_buf, token_out, sems.at[0])
    tokens.start()
    doc_of = lax.broadcasted_iota(jnp.int32, (own_q, docs), 1)
    used = jnp.zeros((own_q, docs), jnp.int32)
    for d in range(docs):
        used = jnp.where(doc_of == d, jnp.minimum(valid_ref[d], length_ref[d]), used)
    doc_buf[...] = (doc_ref[0] + more_ref[0]) * (1.0 / jnp.sqrt(used.astype(jnp.float32)))
    scores = pltpu.make_async_copy(doc_buf, doc_out, sems.at[1])
    scores.start()
    tokens.wait()
    scores.wait()


def last(me, lengths, valid, own, other, doc, more, place, split):
    count, rows = own.shape
    _, own_q, docs = doc.shape
    tokens = jax.ShapeDtypeStruct((rows, 2 * count), jnp.float32)
    scores = jax.ShapeDtypeStruct((own_q, docs), jnp.float32)
    return pl.pallas_call(
        functools.partial(last_kernel, place, split),
        in_specs=[SMEM] * 3 + [VMEM] * 4,
        out_specs=(HBM, HBM),
        out_shape=(tokens, scores),
        scratch_shapes=[
            pltpu.VMEM((2 * count, rows), jnp.float32),
            pltpu.VMEM(tokens.shape, jnp.float32),
            pltpu.VMEM(scores.shape, jnp.float32),
            pltpu.SemaphoreType.DMA((2,)),
        ],
        compiler_params=pltpu.CompilerParams(vmem_limit_bytes=16 * MIB),
    )(me, lengths, valid, own, other, doc, more)


def offset_of(number, bits):
    last_bit = len(bits) - 1
    return functools.reduce(
        operator.xor, [bit for k, bit in enumerate(bits) if (number >> (last_bit - k)) & 1], 0
    )


def body(size, activations, out_grads, proj_in, proj_out, queries, doc_length, valid_count):
    rows = activations.shape[0]
    width = proj_in.shape[1]
    own_q = queries.shape[0]
    me = lax.axis_index("seq").astype(jnp.int32)[None]
    split = size // 2 + 1
    middle = [(1 << k) + 1 for k in range(1, size.bit_length() - 2)]

    proj = proj_out.T
    spots = [offset_of(m, middle) ^ (split * r) for m in range(size // 4) for r in range(2)]
    theirs, table = grad_blocks(me, proj, out_grads, rows, [s ^ 1 for s in spots])
    from_core = swap(theirs, 1, size)
    panel = queries
    got = swap(panel, middle[-1], size)
    sums = grad_blocks(me, proj, out_grads, rows, spots, table) + from_core
    late, _ = lax.optimization_barrier((proj_in, sums))
    got, sums = lax.optimization_barrier((got, sums))
    for k, bit in enumerate(middle):
        half = sums.shape[0] // 2
        sent = swap(sums[half:].astype(jnp.bfloat16), bit, size)
        sums = sums[:half] + sent.astype(jnp.float32)
        if k == 0:
            after = sums
    own = sums[0]
    across = swap(own.astype(jnp.bfloat16), split, size)
    act = lax.dot_general(
        late, activations, (((0,), (1,)), ((), ())), preferred_element_type=jnp.float32
    )
    early, _ = lax.optimization_barrier((act, after))
    more_act, _ = lax.optimization_barrier((swap(early, split, size), own))
    act = jnp.stack([act, more_act])

    panel = jnp.concatenate([panel, got], axis=0)
    place = [0, middle[-1]]
    for bit in middle[-2::-1]:
        panel = jnp.concatenate([panel, swap(panel, bit, size)], axis=0)
        place = place + [p ^ bit for p in place]
    panels = [panel, swap(panel, 1, size)]
    place = tuple(place + [p ^ 1 for p in place])

    steps = max(1, 4 * width * size * own_q * rows // (4 * MIB))
    products = inner(act, panels, steps)
    mine, theirs, doc = score(
        me, doc_length, valid_count, own, across, products, split, own_q, steps
    )
    others = swap(theirs, split, size)
    bits = [1] + middle
    for bit in bits[:-1]:
        half = doc.shape[0] // 2
        doc = doc[:half] + swap(doc[half:], bit, size)
    more = swap(doc[1:], bits[-1], size)
    token_scores, doc = last(
        me, doc_length, valid_count, mine, others, doc[:1], more, place, split
    )
    return (token_scores, doc.T)


def solution(mesh):
    size = mesh.shape["seq"]
    placed = (
        P(("groups", "seq"), None),
        P("groups", "seq"),
        P(),
        P("seq", None),
        P("seq", None),
        P("groups"),
        P("groups"),
    )
    return jax.shard_map(
        functools.partial(body, size),
        mesh=mesh,
        in_specs=placed,
        out_specs=(P(("groups", "seq"), None), P("groups", "seq")),
        check_vma=False,
    )
```

```python
import functools
import operator

import jax
import jax.numpy as jnp
from jax import lax
from jax.experimental import pallas as pl
from jax.experimental.pallas import tpu as pltpu
from jax.sharding import PartitionSpec as P

MIB = 1 << 20
SMEM = pl.BlockSpec(memory_space=pltpu.SMEM)
VMEM = pl.BlockSpec(memory_space=pltpu.VMEM)
HBM = pl.BlockSpec(memory_space=pltpu.HBM)


def swap(value, offset, size):
    return lax.ppermute(value, "seq", [(i, i ^ offset) for i in range(size)])


def grad_kernel(offsets, me_ref, proj_ref, grads_ref, out_ref, table, proj_buf, grads_buf, proj_sem, sems):
    load = pltpu.make_async_copy(proj_ref, proj_buf, proj_sem)
    load.start()
    halves, total, depth = grads_buf.shape
    count = len(offsets) // halves
    rows = total // count
    copies = []
    for k, offset in enumerate(offsets):
        first = pl.multiple_of((me_ref[0] ^ offset) * rows, rows)
        copy = pltpu.make_async_copy(
            grads_ref.at[pl.ds(first, rows)],
            grads_buf.at[k % halves, pl.ds((k // halves) * rows, rows)],
            sems.at[k],
        )
        copy.start(priority=k % 2)
        copies.append(copy)
    load.wait()
    turned = proj_buf[...].T
    none = jnp.zeros_like(turned)
    for r in range(halves):
        table[r] = jnp.concatenate([turned if c == r else none for c in range(halves)], axis=1)
    for k in range(count):
        made = None
        for r in range(halves):
            copies[k * halves + r].wait()
            part = jnp.dot(
                grads_buf[r, k * rows : (k + 1) * rows],
                table[r],
                preferred_element_type=jnp.float32,
            )
            made = part if made is None else made + part
        out_ref[k] = made


def held_kernel(offsets, me_ref, table, grads_ref, out_ref):
    halves = table.shape[0]
    count, rows, _ = out_ref.shape
    for k in range(0, count, 2):
        made = None
        for r in range(halves):
            left = []
            for offset in (offsets[k * halves + r], offsets[(k + 1) * halves + r]):
                first = pl.multiple_of((me_ref[0] ^ offset) * rows, rows)
                left.append(grads_ref[pl.ds(first, rows)])
            part = jnp.dot(
                jnp.concatenate(left, axis=0), table[r], preferred_element_type=jnp.float32
            )
            made = part if made is None else made + part
        out_ref[k] = made[:rows]
        out_ref[k + 1] = made[rows:]


def grad_blocks(me, proj, out_grads, rows, offsets, table=None):
    width, depth = proj.shape
    count = len(offsets) // 2
    made = jax.ShapeDtypeStruct((count, rows, 2 * width), jnp.float32)
    shared = dict(
        compiler_params=pltpu.CompilerParams(vmem_limit_bytes=24 * MIB),
        cost_estimate=pl.CostEstimate(
            flops=4 * count * rows * depth * width,
            bytes_accessed=4 * count * rows * depth,
            transcendentals=0,
        ),
    )
    if table is not None:
        return pl.pallas_call(
            functools.partial(held_kernel, offsets),
            in_specs=[SMEM, VMEM, VMEM],
            out_specs=VMEM,
            out_shape=made,
            **shared,
        )(me, table, out_grads)
    return pl.pallas_call(
        functools.partial(grad_kernel, offsets),
        in_specs=[SMEM, HBM, HBM],
        out_specs=(VMEM, VMEM),
        out_shape=(made, jax.ShapeDtypeStruct((2, depth, 2 * width), jnp.bfloat16)),
        scratch_shapes=[
            pltpu.VMEM((width, depth), jnp.bfloat16),
            pltpu.VMEM((2, count * rows, depth), jnp.bfloat16),
            pltpu.SemaphoreType.DMA,
            pltpu.SemaphoreType.DMA((2 * count,)),
        ],
        **shared,
    )(
        me,
        pltpu.with_memory_space_constraint(proj, pltpu.HBM),
        pltpu.with_memory_space_constraint(out_grads, pltpu.HBM),
    )


def inner_kernel(pieces, act_ref, *refs):
    out_ref = refs[pieces]
    columns = []
    for r in range(act_ref.shape[0]):
        act = act_ref[r]
        high = act.astype(jnp.bfloat16)
        low = (act - high.astype(jnp.float32)).astype(jnp.bfloat16)
        none = jnp.zeros_like(high)
        columns.append(jnp.concatenate([high, none, low, none], axis=0))
        columns.append(jnp.concatenate([none, high, none, low], axis=0))
    table = jnp.concatenate(columns, axis=1)
    pair = 2 * act_ref.shape[1]
    rows = []
    for k in range(refs[0].shape[1] // pair):
        for ref in refs[:pieces]:
            rows.append(ref[:, k * pair : (k + 1) * pair])
    left = jnp.concatenate(rows, axis=0)
    left = jnp.concatenate([left, left], axis=1)
    out_ref[...] = jnp.dot(left, table, preferred_element_type=jnp.float32)


def inner(act, panels, steps):
    halves, width, rows = act.shape
    count = sum(p.shape[0] for p in panels)
    pairs = panels[0].shape[1] // (2 * width)
    total = pairs * count
    if steps == 1:
        grid = {"in_specs": [VMEM] * (1 + len(panels)), "out_specs": VMEM}
    else:
        grid = {
            "grid": (steps,),
            "in_specs": [VMEM]
            + [pl.BlockSpec((p.shape[0], p.shape[1] // steps), lambda s: (0, s)) for p in panels],
            "out_specs": pl.BlockSpec((total // steps, 2 * halves * rows), lambda s: (s, 0)),
        }
    return pl.pallas_call(
        functools.partial(inner_kernel, len(panels)),
        out_shape=jax.ShapeDtypeStruct((total, 2 * halves * rows), jnp.float32),
        compiler_params=pltpu.CompilerParams(vmem_limit_bytes=32 * MIB),
        cost_estimate=pl.CostEstimate(
            flops=16 * total * width * halves * rows,
            bytes_accessed=8 * total * halves * rows,
            transcendentals=0,
        ),
        **grid,
    )(act, *panels)


def score_kernel(
    steps, member_ref, own_ref, other_ref, inner_ref, own_tok, other_tok, doc_ref, grad_ref
):
    rows, wide = own_ref.shape
    halves, width = 2, wide // 2
    count = own_tok.shape[0]
    pairs = inner_ref.shape[0] // count
    step = pl.program_id(0) if steps > 1 else 0
    tokens = (own_tok, other_tok)

    def begin():
        other = other_ref[...].astype(jnp.float32).T
        grad_ref[...] = own_ref[...].T + jnp.concatenate([other[width:], other[:width]], axis=0)

    if steps == 1:
        begin()
    else:
        pl.when(step == 0)(begin)

    for r in range(halves):
        total = None
        for k in range(pairs):
            for parity in range(2):
                feature = 2 * k + parity
                if steps == 1:
                    line = grad_ref[r * width + feature : r * width + feature + 1]
                else:
                    line = grad_ref[pl.ds(r * width + 2 * pairs * step + feature, 1)]
                column = (2 * r + parity) * rows
                term = line * inner_ref[k * count : (k + 1) * count, column : column + rows]
                total = term if total is None else total + term
        if steps == 1:
            tokens[r][...] = total
        else:
            tokens[r][...] = jnp.where(step == 0, total, tokens[r][...] + total)

    def finish():
        parts = []
        for r in range(halves):
            left = tokens[r][...]
            for _ in range(3):
                part = left.astype(jnp.bfloat16)
                left = left - part.astype(jnp.float32)
                parts.append(part)
        partial = lax.dot_general(
            jnp.concatenate(parts, axis=1),
            member_ref[...],
            (((1,), (1,)), ((), ())),
            preferred_element_type=jnp.float32,
        )
        own_q = doc_ref.shape[1]
        for k in range(doc_ref.shape[0]):
            doc_ref[k] = partial[k * own_q : (k + 1) * own_q]

    if steps == 1:
        finish()
    else:
        pl.when(step == steps - 1)(finish)


def score(members, own, other, products, own_q, steps):
    rows, wide = own.shape
    docs = members.shape[0]
    count = 4 * products.shape[0] // wide
    if steps == 1:
        grid = {"in_specs": [VMEM] * 4, "out_specs": (VMEM,) * 3}
    else:
        block = (products.shape[0] // steps, products.shape[1])
        grid = {
            "grid": (steps,),
            "in_specs": [VMEM] * 3 + [pl.BlockSpec(block, lambda s: (s, 0))],
            "out_specs": (VMEM,) * 3,
        }
    return pl.pallas_call(
        functools.partial(score_kernel, steps),
        out_shape=(
            jax.ShapeDtypeStruct((count, rows), jnp.float32),
            jax.ShapeDtypeStruct((count, rows), jnp.float32),
            jax.ShapeDtypeStruct((count // own_q, own_q, docs), jnp.float32),
        ),
        scratch_shapes=[pltpu.VMEM((wide, rows), jnp.float32)],
        compiler_params=pltpu.CompilerParams(vmem_limit_bytes=32 * MIB),
        cost_estimate=pl.CostEstimate(
            flops=2 * products.shape[0] * products.shape[1],
            bytes_accessed=4 * products.shape[0] * products.shape[1],
            transcendentals=0,
        ),
        **grid,
    )(members, own, other, products)


def place_kernel(place, split, me_ref, own_ref, other_ref, out_ref, turned_ref):
    own_q = own_ref.shape[0] // len(place)
    for r, ref in enumerate((own_ref, other_ref)):
        for k, offset in enumerate(place):
            spot = pl.multiple_of((me_ref[0] ^ offset ^ (split * r)) * own_q, own_q)
            turned_ref[pl.ds(spot, own_q)] = ref[k * own_q : (k + 1) * own_q]
    out_ref[...] = turned_ref[...].T


def place_tokens(me, own, other, place, split):
    count, rows = own.shape
    return pl.pallas_call(
        functools.partial(place_kernel, place, split),
        in_specs=[SMEM, VMEM, VMEM],
        out_specs=VMEM,
        out_shape=jax.ShapeDtypeStruct((rows, 2 * count), jnp.float32),
        scratch_shapes=[pltpu.VMEM((2 * count, rows), jnp.float32)],
        compiler_params=pltpu.CompilerParams(vmem_limit_bytes=16 * MIB),
    )(me, own, other)


def masks(me, split, rows, doc_length, valid_count):
    lower = jnp.cumsum(doc_length) - doc_length
    upper = lower + jnp.minimum(valid_count, doc_length)
    place = jnp.arange(6 * rows, dtype=jnp.int32)
    token = (me ^ (split * (place // (3 * rows)))) * rows + place % rows
    inside = (token[None, :] >= lower[:, None]) & (token[None, :] < upper[:, None])
    return inside.astype(jnp.bfloat16)


def offset_of(number, bits):
    last_bit = len(bits) - 1
    return functools.reduce(
        operator.xor, [bit for k, bit in enumerate(bits) if (number >> (last_bit - k)) & 1], 0
    )


def body(size, activations, out_grads, proj_in, proj_out, queries, doc_length, valid_count):
    rows = activations.shape[0]
    width = proj_in.shape[1]
    own_q = queries.shape[0]
    me = lax.axis_index("seq").astype(jnp.int32)[None]
    split = size // 2 + 1
    middle = [(1 << k) + 1 for k in range(1, size.bit_length() - 2)]

    proj = proj_out.T
    spots = [offset_of(m, middle) ^ (split * r) for m in range(size // 4) for r in range(2)]
    theirs, table = grad_blocks(me, proj, out_grads, rows, [s ^ 1 for s in spots])
    from_core = swap(theirs, 1, size)
    panel = queries
    got = swap(panel, middle[-1], size)
    sums = grad_blocks(me, proj, out_grads, rows, spots, table) + from_core
    late, _ = lax.optimization_barrier((proj_in, sums))
    got, sums = lax.optimization_barrier((got, sums))
    for k, bit in enumerate(middle):
        half = sums.shape[0] // 2
        sent = swap(sums[half:].astype(jnp.bfloat16), bit, size)
        sums = sums[:half] + sent.astype(jnp.float32)
        if k == 0:
            after = sums
    own = sums[0]
    across = swap(own.astype(jnp.bfloat16), split, size)
    act = lax.dot_general(
        late, activations, (((0,), (1,)), ((), ())), preferred_element_type=jnp.float32
    )
    early, _ = lax.optimization_barrier((act, after))
    more_act = swap(early, split, size)
    act = jnp.stack([act, more_act])

    panel = jnp.concatenate([panel, got], axis=0)
    place = [0, middle[-1]]
    for bit in middle[-2::-1]:
        panel = jnp.concatenate([panel, swap(panel, bit, size)], axis=0)
        place = place + [p ^ bit for p in place]
    panels = [panel, swap(panel, 1, size)]
    place = tuple(place + [p ^ 1 for p in place])

    steps = max(1, 4 * width * size * own_q * rows // (4 * MIB))
    products = inner(act, panels, steps)
    members = masks(me[0], split, rows, doc_length, valid_count)
    members, _ = lax.optimization_barrier((members, own))
    mine, theirs, doc = score(members, own, across, products, own_q, steps)
    others = swap(theirs, split, size)
    bits = [1] + middle
    for bit in bits[:-1]:
        half = doc.shape[0] // 2
        doc = doc[:half] + swap(doc[half:], bit, size)
    more = swap(doc[1:], bits[-1], size)
    token_scores = place_tokens(me, mine, others, place, split)
    more, token_scores = lax.optimization_barrier((more, token_scores))
    scale = 1.0 / jnp.sqrt(jnp.minimum(valid_count, doc_length).astype(jnp.float32))
    return (token_scores, ((doc[0] + more[0]) * scale[None, :]).T)


def solution(mesh):
    size = mesh.shape["seq"]
    placed = (
        P(("groups", "seq"), None),
        P("groups", "seq"),
        P(),
        P("seq", None),
        P("seq", None),
        P("groups"),
        P("groups"),
    )
    return jax.shard_map(
        functools.partial(body, size),
        mesh=mesh,
        in_specs=placed,
        out_specs=(P(("groups", "seq"), None), P("groups", "seq")),
        check_vma=False,
    )
```

```python
import functools
import operator

import jax
import jax.numpy as jnp
from jax import lax
from jax.experimental import pallas as pl
from jax.experimental.pallas import tpu as pltpu
from jax.sharding import PartitionSpec as P

MIB = 1 << 20
SMEM = pl.BlockSpec(memory_space=pltpu.SMEM)
VMEM = pl.BlockSpec(memory_space=pltpu.VMEM)
HBM = pl.BlockSpec(memory_space=pltpu.HBM)


def swap(value, offset, size):
    return lax.ppermute(value, "seq", [(i, i ^ offset) for i in range(size)])


def grad_kernel(offsets, me_ref, proj_ref, grads_ref, out_ref, table, proj_buf, grads_buf, proj_sem, sems):
    load = pltpu.make_async_copy(proj_ref, proj_buf, proj_sem)
    load.start()
    halves, total, depth = grads_buf.shape
    count = len(offsets) // halves
    rows = total // count
    copies = []
    for k, offset in enumerate(offsets):
        first = pl.multiple_of((me_ref[0] ^ offset) * rows, rows)
        copy = pltpu.make_async_copy(
            grads_ref.at[pl.ds(first, rows)],
            grads_buf.at[k % halves, pl.ds((k // halves) * rows, rows)],
            sems.at[k],
        )
        copy.start(priority=k % 2)
        copies.append(copy)
    load.wait()
    turned = proj_buf[...].T
    none = jnp.zeros_like(turned)
    for r in range(halves):
        table[r] = jnp.concatenate([turned if c == r else none for c in range(halves)], axis=1)
    for k in range(count):
        made = None
        for r in range(halves):
            copies[k * halves + r].wait()
            part = jnp.dot(
                grads_buf[r, k * rows : (k + 1) * rows],
                table[r],
                preferred_element_type=jnp.float32,
            )
            made = part if made is None else made + part
        out_ref[k] = made


def held_kernel(offsets, me_ref, table, grads_ref, out_ref):
    halves = table.shape[0]
    count, rows, _ = out_ref.shape
    for k in range(0, count, 2):
        made = None
        for r in range(halves):
            left = []
            for offset in (offsets[k * halves + r], offsets[(k + 1) * halves + r]):
                first = pl.multiple_of((me_ref[0] ^ offset) * rows, rows)
                left.append(grads_ref[pl.ds(first, rows)])
            part = jnp.dot(
                jnp.concatenate(left, axis=0), table[r], preferred_element_type=jnp.float32
            )
            made = part if made is None else made + part
        out_ref[k] = made[:rows]
        out_ref[k + 1] = made[rows:]


def grad_blocks(me, proj, out_grads, rows, offsets, table=None):
    width, depth = proj.shape
    count = len(offsets) // 2
    made = jax.ShapeDtypeStruct((count, rows, 2 * width), jnp.float32)
    shared = dict(
        compiler_params=pltpu.CompilerParams(vmem_limit_bytes=24 * MIB),
        cost_estimate=pl.CostEstimate(
            flops=4 * count * rows * depth * width,
            bytes_accessed=4 * count * rows * depth,
            transcendentals=0,
        ),
    )
    if table is not None:
        return pl.pallas_call(
            functools.partial(held_kernel, offsets),
            in_specs=[SMEM, VMEM, VMEM],
            out_specs=VMEM,
            out_shape=made,
            **shared,
        )(me, table, out_grads)
    return pl.pallas_call(
        functools.partial(grad_kernel, offsets),
        in_specs=[SMEM, HBM, HBM],
        out_specs=(VMEM, VMEM),
        out_shape=(made, jax.ShapeDtypeStruct((2, depth, 2 * width), jnp.bfloat16)),
        scratch_shapes=[
            pltpu.VMEM((width, depth), jnp.bfloat16),
            pltpu.VMEM((2, count * rows, depth), jnp.bfloat16),
            pltpu.SemaphoreType.DMA,
            pltpu.SemaphoreType.DMA((2 * count,)),
        ],
        **shared,
    )(
        me,
        pltpu.with_memory_space_constraint(proj, pltpu.HBM),
        pltpu.with_memory_space_constraint(out_grads, pltpu.HBM),
    )


def inner_kernel(pieces, act_ref, *refs):
    out_ref = refs[pieces]
    columns = []
    for r in range(act_ref.shape[0]):
        act = act_ref[r]
        high = act.astype(jnp.bfloat16)
        low = (act - high.astype(jnp.float32)).astype(jnp.bfloat16)
        none = jnp.zeros_like(high)
        columns.append(jnp.concatenate([high, none, low, none], axis=0))
        columns.append(jnp.concatenate([none, high, none, low], axis=0))
    table = jnp.concatenate(columns, axis=1)
    pair = 2 * act_ref.shape[1]
    rows = []
    for k in range(refs[0].shape[1] // pair):
        for ref in refs[:pieces]:
            rows.append(ref[:, k * pair : (k + 1) * pair])
    left = jnp.concatenate(rows, axis=0)
    left = jnp.concatenate([left, left], axis=1)
    out_ref[...] = jnp.dot(left, table, preferred_element_type=jnp.float32)


def inner(act, panels, steps):
    halves, width, rows = act.shape
    count = sum(p.shape[0] for p in panels)
    pairs = panels[0].shape[1] // (2 * width)
    total = pairs * count
    if steps == 1:
        grid = {"in_specs": [VMEM] * (1 + len(panels)), "out_specs": VMEM}
    else:
        grid = {
            "grid": (steps,),
            "in_specs": [VMEM]
            + [pl.BlockSpec((p.shape[0], p.shape[1] // steps), lambda s: (0, s)) for p in panels],
            "out_specs": pl.BlockSpec((total // steps, 2 * halves * rows), lambda s: (s, 0)),
        }
    return pl.pallas_call(
        functools.partial(inner_kernel, len(panels)),
        out_shape=jax.ShapeDtypeStruct((total, 2 * halves * rows), jnp.float32),
        compiler_params=pltpu.CompilerParams(vmem_limit_bytes=32 * MIB),
        cost_estimate=pl.CostEstimate(
            flops=16 * total * width * halves * rows,
            bytes_accessed=8 * total * halves * rows,
            transcendentals=0,
        ),
        **grid,
    )(act, *panels)


def score_kernel(
    steps, member_ref, own_ref, other_ref, inner_ref, own_tok, other_tok, doc_ref, grad_ref
):
    rows, wide = own_ref.shape
    halves, width = 2, wide // 2
    count = own_tok.shape[0]
    pairs = inner_ref.shape[0] // count
    step = pl.program_id(0) if steps > 1 else 0
    tokens = (own_tok, other_tok)

    def begin():
        other = other_ref[...].astype(jnp.float32).T
        grad_ref[...] = own_ref[...].T + jnp.concatenate([other[width:], other[:width]], axis=0)

    if steps == 1:
        begin()
    else:
        pl.when(step == 0)(begin)

    for r in range(halves):
        total = None
        for k in range(pairs):
            for parity in range(2):
                feature = 2 * k + parity
                if steps == 1:
                    line = grad_ref[r * width + feature : r * width + feature + 1]
                else:
                    line = grad_ref[pl.ds(r * width + 2 * pairs * step + feature, 1)]
                column = (2 * r + parity) * rows
                term = line * inner_ref[k * count : (k + 1) * count, column : column + rows]
                total = term if total is None else total + term
        if steps == 1:
            tokens[r][...] = total
        else:
            tokens[r][...] = jnp.where(step == 0, total, tokens[r][...] + total)

    def finish():
        parts = []
        for r in range(halves):
            left = tokens[r][...]
            for _ in range(3):
                part = left.astype(jnp.bfloat16)
                left = left - part.astype(jnp.float32)
                parts.append(part)
        partial = lax.dot_general(
            jnp.concatenate(parts, axis=1),
            member_ref[...],
            (((1,), (1,)), ((), ())),
            preferred_element_type=jnp.float32,
        )
        own_q = doc_ref.shape[1]
        for k in range(doc_ref.shape[0]):
            doc_ref[k] = partial[k * own_q : (k + 1) * own_q]

    if steps == 1:
        finish()
    else:
        pl.when(step == steps - 1)(finish)


def score(members, own, other, products, own_q, steps):
    rows, wide = own.shape
    docs = members.shape[0]
    count = 4 * products.shape[0] // wide
    if steps == 1:
        grid = {"in_specs": [VMEM] * 4, "out_specs": (VMEM,) * 3}
    else:
        block = (products.shape[0] // steps, products.shape[1])
        grid = {
            "grid": (steps,),
            "in_specs": [VMEM] * 3 + [pl.BlockSpec(block, lambda s: (s, 0))],
            "out_specs": (VMEM,) * 3,
        }
    return pl.pallas_call(
        functools.partial(score_kernel, steps),
        out_shape=(
            jax.ShapeDtypeStruct((count, rows), jnp.float32),
            jax.ShapeDtypeStruct((count, rows), jnp.float32),
            jax.ShapeDtypeStruct((count // own_q, own_q, docs), jnp.float32),
        ),
        scratch_shapes=[pltpu.VMEM((wide, rows), jnp.float32)],
        compiler_params=pltpu.CompilerParams(vmem_limit_bytes=32 * MIB),
        cost_estimate=pl.CostEstimate(
            flops=2 * products.shape[0] * products.shape[1],
            bytes_accessed=4 * products.shape[0] * products.shape[1],
            transcendentals=0,
        ),
        **grid,
    )(members, own, other, products)


def place_kernel(place, split, me_ref, own_ref, other_ref, out_ref, turned_ref):
    own_q = own_ref.shape[0] // len(place)
    for r, ref in enumerate((own_ref, other_ref)):
        for k, offset in enumerate(place):
            spot = pl.multiple_of((me_ref[0] ^ offset ^ (split * r)) * own_q, own_q)
            turned_ref[pl.ds(spot, own_q)] = ref[k * own_q : (k + 1) * own_q]
    out_ref[...] = turned_ref[...].T


def place_tokens(me, own, other, place, split):
    count, rows = own.shape
    return pl.pallas_call(
        functools.partial(place_kernel, place, split),
        in_specs=[SMEM, VMEM, VMEM],
        out_specs=VMEM,
        out_shape=jax.ShapeDtypeStruct((rows, 2 * count), jnp.float32),
        scratch_shapes=[pltpu.VMEM((2 * count, rows), jnp.float32)],
        compiler_params=pltpu.CompilerParams(vmem_limit_bytes=16 * MIB),
    )(me, own, other)


def masks(me, split, rows, doc_length, valid_count):
    lower = jnp.cumsum(doc_length) - doc_length
    upper = lower + jnp.minimum(valid_count, doc_length)
    place = jnp.arange(6 * rows, dtype=jnp.int32)
    token = (me ^ (split * (place // (3 * rows)))) * rows + place % rows
    inside = (token[None, :] >= lower[:, None]) & (token[None, :] < upper[:, None])
    return inside.astype(jnp.bfloat16)


def offset_of(number, bits):
    last_bit = len(bits) - 1
    return functools.reduce(
        operator.xor, [bit for k, bit in enumerate(bits) if (number >> (last_bit - k)) & 1], 0
    )


def body(size, activations, out_grads, proj_in, proj_out, queries, doc_length, valid_count):
    rows = activations.shape[0]
    width = proj_in.shape[1]
    own_q = queries.shape[0]
    me = lax.axis_index("seq").astype(jnp.int32)[None]
    split = size // 2 + 1
    middle = [(1 << k) + 1 for k in range(1, size.bit_length() - 2)]

    proj = proj_out.T
    spots = [offset_of(m, middle) ^ (split * r) for m in range(size // 4) for r in range(2)]
    theirs, table = grad_blocks(me, proj, out_grads, rows, [s ^ 1 for s in spots])
    from_core = swap(theirs, 1, size)
    panel = queries
    got = swap(panel, middle[-1], size)
    sums = grad_blocks(me, proj, out_grads, rows, spots, table) + from_core
    late, _ = lax.optimization_barrier((proj_in, sums))
    got, sums = lax.optimization_barrier((got, sums))
    for k, bit in enumerate(middle):
        half = sums.shape[0] // 2
        sent = swap(sums[half:].astype(jnp.bfloat16), bit, size)
        sums = sums[:half] + sent.astype(jnp.float32)
        if k == 0:
            after = sums
    own = sums[0]
    across = swap(own.astype(jnp.bfloat16), split, size)
    act = lax.dot_general(
        late, activations, (((0,), (1,)), ((), ())), preferred_element_type=jnp.float32
    )
    early, _ = lax.optimization_barrier((act, after))
    more_act, _ = lax.optimization_barrier((swap(early, split, size), own))
    act = jnp.stack([act, more_act])

    panel = jnp.concatenate([panel, got], axis=0)
    place = [0, middle[-1]]
    for bit in middle[-2::-1]:
        panel = jnp.concatenate([panel, swap(panel, bit, size)], axis=0)
        place = place + [p ^ bit for p in place]
    panels = [panel, swap(panel, 1, size)]
    place = tuple(place + [p ^ 1 for p in place])

    steps = max(1, 4 * width * size * own_q * rows // (4 * MIB))
    products = inner(act, panels, steps)
    lengths, counts, late_me, _ = lax.optimization_barrier((doc_length, valid_count, me, after))
    members = masks(late_me[0], split, rows, lengths, counts)
    mine, theirs, doc = score(members, own, across, products, own_q, steps)
    others = swap(theirs, split, size)
    bits = [1] + middle
    for bit in bits[:-1]:
        half = doc.shape[0] // 2
        doc = doc[:half] + swap(doc[half:], bit, size)
    more = swap(doc[1:], bits[-1], size)
    token_scores = place_tokens(me, mine, others, place, split)
    more, token_scores = lax.optimization_barrier((more, token_scores))
    scale = 1.0 / jnp.sqrt(jnp.minimum(valid_count, doc_length).astype(jnp.float32))
    return (token_scores, ((doc[0] + more[0]) * scale[None, :]).T)


def solution(mesh):
    size = mesh.shape["seq"]
    placed = (
        P(("groups", "seq"), None),
        P("groups", "seq"),
        P(),
        P("seq", None),
        P("seq", None),
        P("groups"),
        P("groups"),
    )
    return jax.shard_map(
        functools.partial(body, size),
        mesh=mesh,
        in_specs=placed,
        out_specs=(P(("groups", "seq"), None), P("groups", "seq")),
        check_vma=False,
    )
```

```python
import functools
import operator

import jax
import jax.numpy as jnp
from jax import lax
from jax.experimental import pallas as pl
from jax.experimental.pallas import tpu as pltpu
from jax.sharding import PartitionSpec as P

MIB = 1 << 20
SMEM = pl.BlockSpec(memory_space=pltpu.SMEM)
VMEM = pl.BlockSpec(memory_space=pltpu.VMEM)
HBM = pl.BlockSpec(memory_space=pltpu.HBM)


def swap(value, offset, size):
    return lax.ppermute(value, "seq", [(i, i ^ offset) for i in range(size)])


def grad_kernel(offsets, me_ref, proj_ref, grads_ref, out_ref, table, proj_buf, grads_buf, proj_sem, sems):
    load = pltpu.make_async_copy(proj_ref, proj_buf, proj_sem)
    load.start()
    halves, total, depth = grads_buf.shape
    count = len(offsets) // halves
    rows = total // count
    copies = []
    for k, offset in enumerate(offsets):
        first = pl.multiple_of((me_ref[0] ^ offset) * rows, rows)
        copy = pltpu.make_async_copy(
            grads_ref.at[pl.ds(first, rows)],
            grads_buf.at[k % halves, pl.ds((k // halves) * rows, rows)],
            sems.at[k],
        )
        copy.start(priority=k % 2)
        copies.append(copy)
    load.wait()
    turned = proj_buf[...].T
    none = jnp.zeros_like(turned)
    for r in range(halves):
        table[r] = jnp.concatenate([turned if c == r else none for c in range(halves)], axis=1)
    for k in range(count):
        made = None
        for r in range(halves):
            copies[k * halves + r].wait()
            part = jnp.dot(
                grads_buf[r, k * rows : (k + 1) * rows],
                table[r],
                preferred_element_type=jnp.float32,
            )
            made = part if made is None else made + part
        out_ref[k] = made


def held_kernel(offsets, me_ref, table, grads_ref, out_ref):
    halves = table.shape[0]
    count, rows, _ = out_ref.shape
    for k in range(0, count, 2):
        made = None
        for r in range(halves):
            left = []
            for offset in (offsets[k * halves + r], offsets[(k + 1) * halves + r]):
                first = pl.multiple_of((me_ref[0] ^ offset) * rows, rows)
                left.append(grads_ref[pl.ds(first, rows)])
            part = jnp.dot(
                jnp.concatenate(left, axis=0), table[r], preferred_element_type=jnp.float32
            )
            made = part if made is None else made + part
        out_ref[k] = made[:rows]
        out_ref[k + 1] = made[rows:]


def grad_blocks(me, proj, out_grads, rows, offsets, table=None):
    width, depth = proj.shape
    count = len(offsets) // 2
    made = jax.ShapeDtypeStruct((count, rows, 2 * width), jnp.float32)
    shared = dict(
        compiler_params=pltpu.CompilerParams(vmem_limit_bytes=24 * MIB),
        cost_estimate=pl.CostEstimate(
            flops=4 * count * rows * depth * width,
            bytes_accessed=4 * count * rows * depth,
            transcendentals=0,
        ),
    )
    if table is not None:
        return pl.pallas_call(
            functools.partial(held_kernel, offsets),
            in_specs=[SMEM, VMEM, VMEM],
            out_specs=VMEM,
            out_shape=made,
            **shared,
        )(me, table, out_grads)
    return pl.pallas_call(
        functools.partial(grad_kernel, offsets),
        in_specs=[SMEM, HBM, HBM],
        out_specs=(VMEM, VMEM),
        out_shape=(made, jax.ShapeDtypeStruct((2, depth, 2 * width), jnp.bfloat16)),
        scratch_shapes=[
            pltpu.VMEM((width, depth), jnp.bfloat16),
            pltpu.VMEM((2, count * rows, depth), jnp.bfloat16),
            pltpu.SemaphoreType.DMA,
            pltpu.SemaphoreType.DMA((2 * count,)),
        ],
        **shared,
    )(
        me,
        pltpu.with_memory_space_constraint(proj, pltpu.HBM),
        pltpu.with_memory_space_constraint(out_grads, pltpu.HBM),
    )


def inner_kernel(pieces, own_ref, act_ref, *refs):
    out_ref, turned_ref = refs[pieces:]
    turned_ref[...] = own_ref[...].T
    columns = []
    for r in range(act_ref.shape[0]):
        act = act_ref[r]
        high = act.astype(jnp.bfloat16)
        low = (act - high.astype(jnp.float32)).astype(jnp.bfloat16)
        none = jnp.zeros_like(high)
        columns.append(jnp.concatenate([high, none, low, none], axis=0))
        columns.append(jnp.concatenate([none, high, none, low], axis=0))
    table = jnp.concatenate(columns, axis=1)
    pair = 2 * act_ref.shape[1]
    rows = []
    for k in range(refs[0].shape[1] // pair):
        for ref in refs[:pieces]:
            rows.append(ref[:, k * pair : (k + 1) * pair])
    left = jnp.concatenate(rows, axis=0)
    left = jnp.concatenate([left, left], axis=1)
    out_ref[...] = jnp.dot(left, table, preferred_element_type=jnp.float32)


def inner(own, act, panels, steps):
    halves, width, rows = act.shape
    count = sum(p.shape[0] for p in panels)
    pairs = panels[0].shape[1] // (2 * width)
    total = pairs * count
    if steps == 1:
        grid = {"in_specs": [VMEM] * (2 + len(panels)), "out_specs": (VMEM, VMEM)}
    else:
        grid = {
            "grid": (steps,),
            "in_specs": [VMEM] * 2
            + [pl.BlockSpec((p.shape[0], p.shape[1] // steps), lambda s: (0, s)) for p in panels],
            "out_specs": (
                pl.BlockSpec((total // steps, 2 * halves * rows), lambda s: (s, 0)),
                VMEM,
            ),
        }
    return pl.pallas_call(
        functools.partial(inner_kernel, len(panels)),
        out_shape=(
            jax.ShapeDtypeStruct((total, 2 * halves * rows), jnp.float32),
            jax.ShapeDtypeStruct((halves * width, rows), jnp.float32),
        ),
        compiler_params=pltpu.CompilerParams(vmem_limit_bytes=32 * MIB),
        cost_estimate=pl.CostEstimate(
            flops=16 * total * width * halves * rows,
            bytes_accessed=8 * total * halves * rows,
            transcendentals=0,
        ),
        **grid,
    )(own, act, *panels)


def score_kernel(
    steps, member_ref, own_ref, other_ref, inner_ref, own_tok, other_tok, doc_ref, grad_ref
):
    wide, rows = own_ref.shape
    halves, width = 2, wide // 2
    count = own_tok.shape[0]
    pairs = inner_ref.shape[0] // count
    step = pl.program_id(0) if steps > 1 else 0
    tokens = (own_tok, other_tok)

    def begin():
        other = other_ref[...].astype(jnp.float32).T
        grad_ref[...] = own_ref[...] + jnp.concatenate([other[width:], other[:width]], axis=0)

    if steps == 1:
        begin()
    else:
        pl.when(step == 0)(begin)

    for r in range(halves):
        total = None
        for k in range(pairs):
            for parity in range(2):
                feature = 2 * k + parity
                if steps == 1:
                    line = grad_ref[r * width + feature : r * width + feature + 1]
                else:
                    line = grad_ref[pl.ds(r * width + 2 * pairs * step + feature, 1)]
                column = (2 * r + parity) * rows
                term = line * inner_ref[k * count : (k + 1) * count, column : column + rows]
                total = term if total is None else total + term
        if steps == 1:
            tokens[r][...] = total
        else:
            tokens[r][...] = jnp.where(step == 0, total, tokens[r][...] + total)

    def finish():
        parts = []
        for r in range(halves):
            left = tokens[r][...]
            for _ in range(3):
                part = left.astype(jnp.bfloat16)
                left = left - part.astype(jnp.float32)
                parts.append(part)
        partial = lax.dot_general(
            jnp.concatenate(parts, axis=1),
            member_ref[...],
            (((1,), (1,)), ((), ())),
            preferred_element_type=jnp.float32,
        )
        own_q = doc_ref.shape[1]
        for k in range(doc_ref.shape[0]):
            doc_ref[k] = partial[k * own_q : (k + 1) * own_q]

    if steps == 1:
        finish()
    else:
        pl.when(step == steps - 1)(finish)


def score(members, own, other, products, own_q, steps):
    wide, rows = own.shape
    docs = members.shape[0]
    count = 4 * products.shape[0] // wide
    if steps == 1:
        grid = {"in_specs": [VMEM] * 4, "out_specs": (VMEM,) * 3}
    else:
        block = (products.shape[0] // steps, products.shape[1])
        grid = {
            "grid": (steps,),
            "in_specs": [VMEM] * 3 + [pl.BlockSpec(block, lambda s: (s, 0))],
            "out_specs": (VMEM,) * 3,
        }
    return pl.pallas_call(
        functools.partial(score_kernel, steps),
        out_shape=(
            jax.ShapeDtypeStruct((count, rows), jnp.float32),
            jax.ShapeDtypeStruct((count, rows), jnp.float32),
            jax.ShapeDtypeStruct((count // own_q, own_q, docs), jnp.float32),
        ),
        scratch_shapes=[pltpu.VMEM((wide, rows), jnp.float32)],
        compiler_params=pltpu.CompilerParams(vmem_limit_bytes=32 * MIB),
        cost_estimate=pl.CostEstimate(
            flops=2 * products.shape[0] * products.shape[1],
            bytes_accessed=4 * products.shape[0] * products.shape[1],
            transcendentals=0,
        ),
        **grid,
    )(members, own, other, products)


def place_kernel(place, split, me_ref, own_ref, other_ref, out_ref, turned_ref):
    own_q = own_ref.shape[0] // len(place)
    for r, ref in enumerate((own_ref, other_ref)):
        for k, offset in enumerate(place):
            spot = pl.multiple_of((me_ref[0] ^ offset ^ (split * r)) * own_q, own_q)
            turned_ref[pl.ds(spot, own_q)] = ref[k * own_q : (k + 1) * own_q]
    out_ref[...] = turned_ref[...].T


def place_tokens(me, own, other, place, split):
    count, rows = own.shape
    return pl.pallas_call(
        functools.partial(place_kernel, place, split),
        in_specs=[SMEM, VMEM, VMEM],
        out_specs=VMEM,
        out_shape=jax.ShapeDtypeStruct((rows, 2 * count), jnp.float32),
        scratch_shapes=[pltpu.VMEM((2 * count, rows), jnp.float32)],
        compiler_params=pltpu.CompilerParams(vmem_limit_bytes=16 * MIB),
    )(me, own, other)


def masks(me, split, rows, doc_length, valid_count):
    lower = jnp.cumsum(doc_length) - doc_length
    upper = lower + jnp.minimum(valid_count, doc_length)
    place = jnp.arange(6 * rows, dtype=jnp.int32)
    token = (me ^ (split * (place // (3 * rows)))) * rows + place % rows
    inside = (token[None, :] >= lower[:, None]) & (token[None, :] < upper[:, None])
    return inside.astype(jnp.bfloat16)


def offset_of(number, bits):
    last_bit = len(bits) - 1
    return functools.reduce(
        operator.xor, [bit for k, bit in enumerate(bits) if (number >> (last_bit - k)) & 1], 0
    )


def body(size, activations, out_grads, proj_in, proj_out, queries, doc_length, valid_count):
    rows = activations.shape[0]
    width = proj_in.shape[1]
    own_q = queries.shape[0]
    me = lax.axis_index("seq").astype(jnp.int32)[None]
    split = size // 2 + 1
    middle = [(1 << k) + 1 for k in range(1, size.bit_length() - 2)]

    proj = proj_out.T
    spots = [offset_of(m, middle) ^ (split * r) for m in range(size // 4) for r in range(2)]
    theirs, table = grad_blocks(me, proj, out_grads, rows, [s ^ 1 for s in spots])
    from_core = swap(theirs, 1, size)
    panel = queries
    got = swap(panel, middle[-1], size)
    sums = grad_blocks(me, proj, out_grads, rows, spots, table) + from_core
    late, _ = lax.optimization_barrier((proj_in, sums))
    got, sums = lax.optimization_barrier((got, sums))
    for k, bit in enumerate(middle):
        half = sums.shape[0] // 2
        sent = swap(sums[half:].astype(jnp.bfloat16), bit, size)
        sums = sums[:half] + sent.astype(jnp.float32)
        if k == 0:
            after = sums
    own = sums[0]
    across = swap(own.astype(jnp.bfloat16), split, size)
    act = lax.dot_general(
        late, activations, (((0,), (1,)), ((), ())), preferred_element_type=jnp.float32
    )
    early, _ = lax.optimization_barrier((act, after))
    more_act = swap(early, split, size)
    act = jnp.stack([act, more_act])

    panel = jnp.concatenate([panel, got], axis=0)
    place = [0, middle[-1]]
    for bit in middle[-2::-1]:
        panel = jnp.concatenate([panel, swap(panel, bit, size)], axis=0)
        place = place + [p ^ bit for p in place]
    panels = [panel, swap(panel, 1, size)]
    place = tuple(place + [p ^ 1 for p in place])

    steps = max(1, 4 * width * size * own_q * rows // (4 * MIB))
    products, turned = inner(own, act, panels, steps)
    lengths, counts, late_me, _ = lax.optimization_barrier((doc_length, valid_count, me, after))
    members = masks(late_me[0], split, rows, lengths, counts)
    mine, theirs, doc = score(members, turned, across, products, own_q, steps)
    others = swap(theirs, split, size)
    bits = [1] + middle
    for bit in bits[:-1]:
        half = doc.shape[0] // 2
        doc = doc[:half] + swap(doc[half:], bit, size)
    more = swap(doc[1:], bits[-1], size)
    token_scores = place_tokens(me, mine, others, place, split)
    more, token_scores = lax.optimization_barrier((more, token_scores))
    scale = 1.0 / jnp.sqrt(jnp.minimum(valid_count, doc_length).astype(jnp.float32))
    return (token_scores, ((doc[0] + more[0]) * scale[None, :]).T)


def solution(mesh):
    size = mesh.shape["seq"]
    placed = (
        P(("groups", "seq"), None),
        P("groups", "seq"),
        P(),
        P("seq", None),
        P("seq", None),
        P("groups"),
        P("groups"),
    )
    return jax.shard_map(
        functools.partial(body, size),
        mesh=mesh,
        in_specs=placed,
        out_specs=(P(("groups", "seq"), None), P("groups", "seq")),
        check_vma=False,
    )
```
